128 devices in a mesh: slab: 32 (over y, x, core), col: 4 (over z).
Axes of the slice: x: 4, y: 4, z: 4, core: 2. Of those that a mesh axis runs over, the one named last changes fastest.
Arguments:
- residual: float32 [256, 256, 512], P('slab', None, 'col'), may hold values from -40 to 40
- direction: float32 [256, 256, 512], P('slab', None, 'col'), may hold values from -60 to 60
- diagonal: float32 [256, 256, 512], P('slab', None, 'col'), may hold values from 0.05 to 2
- first_weight: float32 [7, 4], replicated, may hold values from -2 to 2
- conv_weights: float32 [6, 7, 4, 4], replicated, may hold values from -1.2 to 1.2
- last_weight: float32 [7, 4], replicated, may hold values from -1.2 to 1.2
- biases: float32 [7, 4], replicated, may hold values from -1.5 to 1.5
Outputs:
- new_residual: float32 [256, 256, 512], P('slab', None, 'col')
- new_direction: float32 [256, 256, 512], P('slab', None, 'col')
The draws below stay inside these ranges and needn't reach their ends.
All inputs are finite; a program needn't handle non-finite values.
Results may differ from the reference program's by a relative error of at most 0.00095.
Values sent between devices are 32-bit elements; how exact they have to be, the bound alone decides.
A program may use at most 256 MiB of HBM per device.

```python
import math
import jax
import jax.numpy as jnp
from jax import lax

NY = 256
CH = 4
NX = 256
NZ = 512


def common_field(key):
    normal_key = jax.random.fold_in(key, 0)
    row_key = jax.random.fold_in(key, 2)
    column_key = jax.random.fold_in(key, 3)
    shape = (NX, NY, NZ)
    normal_part = jnp.clip(jax.random.normal(normal_key, shape, jnp.float32), -4.0, 4.0)
    ramp = jnp.arange(NX, dtype=jnp.float32) / max(NX - 1, 1)
    noise = normal_part
    jitter = jax.random.uniform(row_key, (NX,), jnp.float32, 0.0, 0.3)
    rising = ramp
    row_scale = jnp.exp(math.log(10.0) * (0.7 * rising + jitter))
    column_scale = jnp.exp(math.log(10.0) * jax.random.uniform(column_key, (NZ,), jnp.float32))
    scales = 0.1 * row_scale[:, None, None] * column_scale[None, None, :]
    return (noise, scales)


def draw_residual(key, part):
    base_key = key
    noise, scales = common_field(base_key)
    return (noise * scales).astype(jnp.float32)


def draw_direction(key, part):
    base_key = key
    key = jax.random.fold_in(key, 23)
    noise, scales = common_field(base_key)
    own = jnp.clip(jax.random.normal(key, (NX, NY, NZ), jnp.float32), -4.0, 4.0)
    return (scales * (0.8 * noise + 0.6 * own)).astype(jnp.float32)


def block_scale(rng, dims, shards, least, top_value):
    def one(dim, parts):
        draws = jax.random.uniform(jax.random.fold_in(jax.random.fold_in(rng, 6), dim), (parts,), jnp.float32, least / len(shards), top_value / len(shards))
        return jnp.repeat(jnp.exp(draws), dims[dim] // parts).reshape((-1,) + (1,) * (len(dims) - dim - 1))

    gain = one(*shards[0])
    for cut in shards[1:]:
        gain = gain * one(*cut)
    return gain


def bell_draw(own_key, extent, width, limit, kind=jnp.bfloat16):
    values = jax.random.normal(own_key, extent, jnp.float32) * width
    return jnp.minimum(jnp.maximum(values, -limit), limit).astype(kind)


def setup_inputs(seed: int = 0) -> dict:
    seeds = jax.random.split(jax.random.key(seed), 8)
    residual = draw_residual(jax.random.fold_in(seeds[7], 71), 0)
    direction = draw_direction(jax.random.fold_in(seeds[7], 71), 0)
    diagonal = jnp.clip(jnp.exp(math.log(2.0) - 3.6888794 * jax.random.uniform(seeds[2], (NX, NY, NZ), jnp.float32) ** block_scale(seeds[2], (NX, NY, NZ), ((0, 32), (2, 4)), -0.2, 0.2)), 0.05, 2.0)
    first_weight = bell_draw(seeds[3], (7, CH), 0.53, 2.0, jnp.float32)
    conv_weights = bell_draw(seeds[4], (6, 7, CH, CH), 0.27, 1.2, jnp.float32)
    last_weight = bell_draw(seeds[5], (7, CH), 0.27, 1.2, jnp.float32)
    biases = bell_draw(seeds[6], (7, CH), 0.3, 1.5, jnp.float32)
    return {"residual": residual, "direction": direction, "diagonal": diagonal, "first_weight": first_weight, "conv_weights": conv_weights, "last_weight": last_weight, "biases": biases}


STENCIL_STEPS = ((0, 0, 0), (-1, 0, 0), (1, 0, 0), (0, -1, 0), (0, 1, 0), (0, 0, -1), (0, 0, 1))

def operate(field, diagonal):
    padded = jnp.pad(field, 1)
    beside = padded[2:, 1:-1, 1:-1] + padded[:-2, 1:-1, 1:-1]
    beside = beside + padded[1:-1, 2:, 1:-1] + padded[1:-1, :-2, 1:-1]
    beside = beside + padded[1:-1, 1:-1, 2:] + padded[1:-1, 1:-1, :-2]
    return (6.0 + diagonal) * field - beside

def convolve(values, weights, bias_terms):
    padded = jnp.pad(values, ((0, 0), (1, 1), (1, 1), (1, 1)))
    extent_x, extent_y, extent_z = (values.shape[1], values.shape[2], values.shape[3])
    shifts = []
    for step_x, step_y, step_z in STENCIL_STEPS:
        shifts.append(padded[:, 1 + step_x:1 + step_x + extent_x, 1 + step_y:1 + step_y + extent_y, 1 + step_z:1 + step_z + extent_z])
    outputs = []
    for out_chan in range(weights.shape[1]):
        total = jnp.zeros((extent_x, extent_y, extent_z), jnp.float32) + bias_terms[out_chan]
        for position in range(len(STENCIL_STEPS)):
            for in_chan in range(weights.shape[2]):
                total = total + weights[position, out_chan, in_chan] * shifts[position][in_chan]
        outputs.append(total)
    return jnp.stack(outputs)

def coarsen(values):
    chans, extent_x, extent_y, extent_z = values.shape
    blocks = values.reshape(chans, extent_x // 2, 2, extent_y // 2, 2, extent_z // 2, 2)
    return lax.optimization_barrier(jnp.mean(blocks, axis=(2, 4, 6)))

def refine(values):
    return jnp.repeat(jnp.repeat(jnp.repeat(values, 2, axis=1), 2, axis=2), 2, axis=3)

def network_of(feed, first_weight, conv_weights, last_weight, biases):
    down_zero = jax.nn.relu(convolve(feed, first_weight[:, :, None], biases[0]))
    down_one = jax.nn.relu(convolve(coarsen(down_zero), conv_weights[0], biases[1]))
    down_two = jax.nn.relu(convolve(coarsen(down_one), conv_weights[1], biases[2]))
    down_three = jax.nn.relu(convolve(coarsen(down_two), conv_weights[2], biases[3]))
    rise_two = jax.nn.relu(convolve(refine(down_three) + down_two, conv_weights[3], biases[4]))
    rise_one = jax.nn.relu(convolve(refine(rise_two) + down_one, conv_weights[4], biases[5]))
    rise_zero = jax.nn.relu(convolve(refine(rise_one) + down_zero, conv_weights[5], biases[6]))
    return convolve(rise_zero, last_weight[:, None, :], jnp.zeros((1,), jnp.float32))[0]

def reference(residual, direction, diagonal, first_weight, conv_weights, last_weight, biases):
    image = operate(direction, diagonal)
    curvature = jnp.sum(direction * image)
    along = jnp.sum(residual * direction)
    alpha = along / curvature
    new_residual = residual - alpha * image
    scale = jnp.sqrt(jnp.mean(new_residual * new_residual) + 1e-06)
    network = network_of((new_residual / scale)[None], first_weight, conv_weights, last_weight, biases)
    preconditioned = new_residual / (6.0 + diagonal) + scale * network
    beta = jnp.sum(preconditioned * image) / curvature
    new_direction = preconditioned - beta * direction
    return (new_residual, new_direction)
```

```python
import functools

import jax
import jax.numpy as jnp
from jax import lax
from jax.experimental import pallas as pl
from jax.experimental.pallas import tpu as pltpu
from jax.sharding import PartitionSpec as P

MESH = pl.DeviceIdType.MESH
L = 128
PAD = 8
CH = 4
F32 = jnp.float32
BF16 = jnp.bfloat16

FIRST, CONV, LAST, BIAS = 0, 28, 700, 728

E_DIR, E_RES, E_IMG, E_P1, E_D0, E_P2, E_P3, E_S2, E_S1, E_R1, E_NET = range(11)
N_EX = 11


def split2(value):
    high = value.astype(BF16)
    low = (value - high.astype(F32)).astype(BF16)
    return high, low


def kernel(n_slab, n_col, X, Z, *refs):
    (w, res_in, dir_in, diag_in, res_out, dir_out,
     dT, rT, iT, nT, gT, d0, z0, net, pre,
     p1, d1, r1, p2, d2, r2, p3, d3,
     zs0, zr0, zsd, zrd, zs1, zr1, zs2, zr2, zs3, zr3, xs_m, xr_m, zs_m, zr_m,
     pool_m, up_m, sc, a_send, a_recv, b_send, b_recv,
     send_sem, recv_sem, asend_sem, arecv_sem, bsend_sem, brecv_sem) = refs
    H = 2
    slab = lax.axis_index("slab")
    col = lax.axis_index("col")
    core = lax.rem(slab, 2)
    chip = slab // 2
    n_chip = n_slab // 2
    n_a = 2 * n_col
    Zp = [Z // 2**l + 2 * PAD for l in range(4)]
    Zl = [Z // 2**l for l in range(4)]
    Xl = [X // 2**l for l in range(4)]
    has = (slab > 0, slab < n_slab - 1, col > 0, col < n_col - 1)
    targets = (
        (jnp.maximum(slab - 1, 0), col),
        (jnp.minimum(slab + 1, n_slab - 1), col),
        (slab, jnp.maximum(col - 1, 0)),
        (slab, jnp.minimum(col + 1, n_col - 1)),
    )
    opposite = (1, 0, 3, 2)

    def x_views(ref, level):
        rows, pitch, count = Zl[level], Zp[level], Xl[level]
        if len(ref.shape) == 3:
            def view(plane):
                return ref.at[:, pl.ds(plane * pitch + PAD, rows), :]
        else:
            def view(plane):
                return ref.at[:, :, pl.ds(plane * pitch + PAD, rows), :]
        return (view(1), view(count)), (view(0), view(count + 1))

    def x_views4(ref, level):
        return x_views(ref, level)

    exchanges = {}

    def define(e, x_src, x_dst, z_src, z_dst):
        msgs = []
        for side in range(4):
            if side < 2:
                src, dst = x_src[side], x_dst[opposite[side]]
            else:
                src, dst = z_src.at[side - 2], z_dst.at[opposite[side] - 2]
            msgs.append(pltpu.make_async_remote_copy(
                src_ref=src, dst_ref=dst,
                send_sem=send_sem.at[e, side],
                recv_sem=recv_sem.at[e, opposite[side]],
                device_id=targets[side], device_id_type=MESH))
        exchanges[e] = msgs

    def send(e, sides=(0, 1, 2, 3)):
        for side in sides:
            @pl.when(has[side])
            def _(side=side):
                exchanges[e][side].start()

    def receive(e, sides=(0, 1, 2, 3)):
        for side in sides:
            @pl.when(has[side])
            def _(side=side):
                exchanges[e][opposite[side]].wait_recv()

    def sent(e):
        for side in range(4):
            @pl.when(has[side])
            def _(side=side):
                exchanges[e][side].wait_send()

    for e, ref, level, zs, zr in (
        (E_DIR, dT, 0, zs0.at[0], zr0.at[0]),
        (E_RES, rT, 0, zs0.at[1], zr0.at[1]),
        (E_IMG, iT, 0, zs0.at[2], zr0.at[2]),
        (E_P1, p1, 1, zs1.at[0], zr1.at[0]),
        (E_D0, d0, 0, zsd, zrd),
        (E_P2, p2, 2, zs2.at[0], zr2.at[0]),
        (E_P3, p3, 3, zs3.at[0], zr3.at[0]),
        (E_S2, d2, 2, zs2.at[1], zr2.at[1]),
        (E_S1, d1, 1, zs1.at[1], zr1.at[1]),
        (E_R1, r1, 1, zs1.at[2], zr1.at[2]),
    ):
        src, dst = x_views(ref, level)
        define(e, src, dst, zs, zr)
    define(E_NET, (xs_m.at[0], xs_m.at[1]), (xr_m.at[0], xr_m.at[1]), zs_m, zr_m)

    def groups(ref):
        if len(ref.shape) == 3:
            return [(i,) for i in range(ref.shape[0])]
        return [(c, h) for c in range(ref.shape[0]) for h in range(ref.shape[1])]

    def rows_at(start, count, stride):
        return pl.ds(start, count, stride=stride) if count > 1 else pl.ds(start, 1)

    def pack(ref, level, zs):
        pitch, count = Zp[level], Xl[level]
        for side, row in ((0, 0), (1, Zl[level] - 1)):
            for g, index in enumerate(groups(ref)):
                zs[side, pl.ds(g * count, count), :] = ref[
                    (*index, rows_at(pitch + PAD + row, count, pitch), slice(None))]

    def unpack(ref, level, zr):
        pitch, count = Zp[level], Xl[level]
        for side, row in ((0, -1), (1, Zl[level])):
            for g, index in enumerate(groups(ref)):
                ref[(*index, rows_at(pitch + PAD + row, count, pitch), slice(None))] = zr[
                    side, pl.ds(g * count, count), :]

    for side in (0, 1):
        @pl.when(jnp.logical_not(has[side]))
        def _(side=side):
            for ref, level in ((dT, 0), (rT, 0), (iT, 0), (p1, 1), (p2, 2), (p3, 3),
                               (d2, 2), (d1, 1), (r1, 1)):
                plane = 0 if side == 0 else Xl[level] + 1
                for index in groups(ref):
                    ref[(*index, pl.ds(plane * Zp[level] + PAD, Zl[level]), slice(None))] = (
                        jnp.zeros((Zl[level], L), F32))
            plane = 0 if side == 0 else X + 1
            for c in range(CH):
                for h in range(H):
                    d0[c, h, pl.ds(plane * Zp[0] + PAD, Z), :] = jnp.zeros((Z, L), F32)
            for h in range(H):
                xr_m[side, h] = jnp.zeros((Z, L), F32)
    for side in (2, 3):
        @pl.when(jnp.logical_not(has[side]))
        def _(side=side):
            s = side - 2
            for ref in (zr0, zr1, zr2, zr3):
                for i in range(ref.shape[0]):
                    ref[i, s] = jnp.zeros(ref.shape[2:], F32)
            zrd[s] = jnp.zeros(zrd.shape[1:], F32)
            zr_m[s] = jnp.zeros(zr_m.shape[1:], F32)

    rank_a = col * 2 + core

    def peer_a(j):
        rank = lax.rem(rank_a + j, n_a)
        return (chip * 2 + lax.rem(rank, 2), rank // 2)

    def peer_b(j):
        return (lax.rem(chip + j, n_chip) * 2 + core, col)

    barrier = pltpu.get_barrier_semaphore()
    for j in range(1, n_a):
        pl.semaphore_signal(barrier, inc=1, device_id=peer_a(j), device_id_type=MESH)
    for j in range(1, n_chip):
        pl.semaphore_signal(barrier, inc=1, device_id=peer_b(j), device_id_type=MESH)
    for side in (0, 1):
        @pl.when(has[side])
        def _(side=side):
            pl.semaphore_signal(barrier, inc=1, device_id=targets[side], device_id_type=MESH)

    def turn_in(source, target):
        def body(i, carry):
            x, h = i // H, lax.rem(i, H)
            block = source[x, pl.ds(pl.multiple_of(h * L, L), L), :]
            target[h, pl.ds(pl.multiple_of((x + 1) * Zp[0] + PAD, 8), Z), :] = block.T
            return carry
        lax.fori_loop(0, X * H, body, 0)

    turn_in(dir_in, dT)
    pack(dT, 0, zs0.at[0])
    n_wait = (n_a - 1) + (n_chip - 1) + jnp.where(slab > 0, 1, 0) + jnp.where(slab < n_slab - 1, 1, 0)
    pl.semaphore_wait(barrier, n_wait)
    send(E_DIR)
    turn_in(res_in, rT)
    pack(rT, 0, zs0.at[1])
    send(E_RES)
    turn_in(diag_in, gT)

    def beside_y(center, ny):
        rows = center[0].shape[0]
        lane = lax.broadcasted_iota(jnp.int32, (rows, L), 1)
        count = len(center)
        last = L - 1 if count > 1 else ny - 1
        up = [pltpu.roll(v, 1, 1) for v in center]
        down = [pltpu.roll(v, L - 1, 1) for v in center]
        zero = jnp.zeros((rows, L), F32)
        minus = [jnp.where(lane == 0, up[h - 1] if h > 0 else zero, up[h]) for h in range(count)]
        plus = [jnp.where(lane == last, down[h + 1] if h < count - 1 else zero, down[h])
                for h in range(count)]
        return minus, plus

    def fold(value):
        return jnp.sum(value.reshape(value.shape[0] // 8, 8, L), axis=0)

    receive(E_DIR)
    unpack(dT, 0, zr0.at[0])
    RI = 32

    def image_body(i, carry):
        per = Z // RI
        base = pl.multiple_of((i // per + 1) * Zp[0] + PAD + lax.rem(i, per) * RI, 8)
        center = [dT[h, pl.ds(base, RI), :] for h in range(H)]
        minus, plus = beside_y(center, 2 * L)
        sums = list(carry)
        for h in range(H):
            beside = dT[h, pl.ds(base + Zp[0], RI), :] + dT[h, pl.ds(base - Zp[0], RI), :]
            beside = beside + plus[h] + minus[h]
            beside = beside + dT[h, pl.ds(base + 1, RI), :] + dT[h, pl.ds(base - 1, RI), :]
            image = (6.0 + gT[h, pl.ds(base, RI), :]) * center[h] - beside
            iT[h, pl.ds(base, RI), :] = image
            r = rT[h, pl.ds(base, RI), :]
            for q, term in enumerate((center[h] * image, r * center[h], r * r, r * image,
                                      image * image)):
                sums[q] = sums[q] + fold(term)
        return tuple(sums)

    sums = lax.fori_loop(0, X * (Z // RI), image_body,
                         tuple(jnp.zeros((8, L), F32) for _ in range(5)))

    def reduce_start(n, send_ref, recv_ref, ssem, rsem, peer):
        copies = []
        for j in range(1, n):
            copy = pltpu.make_async_remote_copy(
                src_ref=send_ref, dst_ref=recv_ref.at[j - 1], send_sem=ssem.at[j - 1],
                recv_sem=rsem.at[j - 1], device_id=peer(j), device_id_type=MESH)
            copy.start()
            copies.append(copy)
        return copies

    def reduce_end(copies, send_ref, recv_ref):
        total = send_ref[...]
        for j, copy in enumerate(copies):
            copy.wait_recv()
        for j in range(len(copies)):
            total = total + recv_ref[j]
        return total

    pending = []
    a_send[0] = jnp.zeros((8, L), F32)
    for q in range(5):
        a_send[0, q:q + 1, :] = jnp.sum(sums[q], axis=0, keepdims=True)
    copies = reduce_start(n_a, a_send.at[0], a_recv.at[0], asend_sem.at[0], arecv_sem.at[0], peer_a)
    pending += copies
    pack(iT, 0, zs0.at[2])
    send(E_IMG)
    b_send[0] = reduce_end(copies, a_send.at[0], a_recv.at[0])
    copies = reduce_start(n_chip, b_send.at[0], b_recv.at[0], bsend_sem.at[0], brecv_sem.at[0], peer_b)
    pending += copies

    row = lax.broadcasted_iota(jnp.int32, (2 * L, L), 0)
    lane = lax.broadcasted_iota(jnp.int32, (2 * L, L), 1)
    pool_m[...] = jnp.where(row // 2 == lane, 0.125, 0.0).astype(BF16)
    row = lax.broadcasted_iota(jnp.int32, (L, 2 * L), 0)
    lane = lax.broadcasted_iota(jnp.int32, (L, 2 * L), 1)
    up_m[...] = jnp.where(lane // 2 == row, 1.0, 0.0).astype(BF16)
    for c in range(CH):
        for h in range(H):
            for plane in (0, X + 1):
                z0[c, h, pl.ds(plane * Zp[0] + PAD, Z), :] = jnp.zeros((Z, L), F32)
            for at in (PAD - 1, PAD + Z):
                z0[c, h, pl.ds(Zp[0] + at, X, stride=Zp[0]), :] = jnp.zeros((X, L), F32)

    total = reduce_end(copies, b_send.at[0], b_recv.at[0])
    full = jnp.broadcast_to(jnp.sum(total, axis=1, keepdims=True), (8, L))
    curvature = full[0:1]
    alpha = full[1:2] / curvature
    mixed = total[2:3] - 2.0 * alpha * total[3:4] + alpha * alpha * total[4:5]
    squares = jnp.maximum(jnp.broadcast_to(jnp.sum(mixed, axis=1, keepdims=True), (1, L)), 0.0)
    cells = float(X * n_slab) * float(2 * L) * float(Z * n_col)
    scale = jnp.sqrt(squares / cells + 1e-06)
    sc[0:1] = alpha
    sc[1:2] = 1.0 / scale
    sc[2:3] = scale
    sc[3:4] = curvature

    receive(E_RES)
    unpack(rT, 0, zr0.at[1])
    receive(E_IMG)
    unpack(iT, 0, zr0.at[2])
    RN = 2 * PAD

    def feed_body(i, carry):
        base = pl.multiple_of(i * RN, 8)
        a, s = sc[0:1], sc[1:2]
        for h in range(H):
            at = (h, pl.ds(base, RN), slice(None))
            nT[at] = (rT[at] - a * iT[at]) * s
        return carry
    lax.fori_loop(0, (X + 2) * Zp[0] // RN, feed_body, 0)

    def conv(load, store, weight, bias, n_in, n_out, count_h, level, ny, rows, x_from, x_to):
        per = Zl[level] // rows
        pitch = Zp[level]

        def body(i, carry):
            base = pl.multiple_of((i // per + x_from + 1) * pitch + PAD + lax.rem(i, per) * rows, 8)
            acc = [[None] * count_h for _ in range(n_out)]
            for k in range(n_in):
                center = [load(k, h, base, rows) for h in range(count_h)]
                minus, plus = beside_y(center, ny)
                for o in range(7):
                    for h in range(count_h):
                        tap = (center[h] if o == 0 else
                               load(k, h, base - pitch, rows) if o == 1 else
                               load(k, h, base + pitch, rows) if o == 2 else
                               minus[h] if o == 3 else plus[h] if o == 4 else
                               load(k, h, base - 1, rows) if o == 5 else
                               load(k, h, base + 1, rows))
                        for c in range(n_out):
                            term = weight(o, c, k) * tap
                            acc[c][h] = term if acc[c][h] is None else acc[c][h] + term
            for c in range(n_out):
                for h in range(count_h):
                    value = acc[c][h]
                    if bias is not None:
                        value = jnp.maximum(value + bias(c), 0.0)
                    store(c, h, base, rows, value)
            return carry
        lax.fori_loop(0, (x_to - x_from) * per, body, 0)

    def loader(ref):
        if len(ref.shape) == 3:
            return lambda k, h, base, rows: ref[k, pl.ds(base, rows), :]
        return lambda k, h, base, rows: ref[k, h, pl.ds(base, rows), :]

    def storer(ref):
        def put(c, h, base, rows, value):
            if len(ref.shape) == 3:
                ref[c, pl.ds(base, rows), :] = value
            else:
                ref[c, h, pl.ds(base, rows), :] = value
        return put

    def inner_conv(which, source, target, count_h, level, ny, rows, x_from=0, x_to=None):
        conv(loader(source), storer(target),
             lambda o, c, k: w[CONV + ((which * 7 + o) * CH + c) * CH + k],
             lambda c: w[BIAS + (which + 1) * CH + c],
             CH, CH, count_h, level, ny, rows, x_from, Xl[level] if x_to is None else x_to)

    def pool(source, target, level, count_h):
        Z1, X1 = Zl[level + 1], Xl[level + 1]

        def body(i, carry):
            c, x1 = i // X1, lax.rem(i, X1)
            parts = []
            for h in range(count_h):
                total = None
                for dx in range(2):
                    for dz in range(2):
                        at = pl.ds((2 * x1 + dx + 1) * Zp[level] + PAD + dz, Z1, stride=2)
                        v = source[c, h, at, :] if count_h > 1 else source[c, at, :]
                        total = v if total is None else total + v
                parts.append(total)
            value = jnp.concatenate(parts, axis=1) if count_h > 1 else parts[0]
            high, low = split2(value)
            m = pool_m[0:count_h * L, :]
            out = jnp.dot(high, m, preferred_element_type=F32) + jnp.dot(low, m, preferred_element_type=F32)
            target[c, pl.ds(pl.multiple_of((x1 + 1) * Zp[level + 1] + PAD, 8), Z1), :] = out
            return carry
        lax.fori_loop(0, CH * X1, body, 0)

    def raised(value, count_h):
        high, low = split2(value)
        m = up_m[:, 0:count_h * L]
        return jnp.dot(high, m, preferred_element_type=F32) + jnp.dot(low, m, preferred_element_type=F32)

    def add_up(source, target, level, count_h):
        Z1, X1 = Zl[level + 1], Xl[level + 1]

        def body(i, carry):
            c, x1 = i // X1, lax.rem(i, X1)
            value = raised(source[c, pl.ds(pl.multiple_of((x1 + 1) * Zp[level + 1] + PAD, 8), Z1), :], count_h)
            for dx in range(2):
                for dz in range(2):
                    rows = pl.ds((2 * x1 + dx + 1) * Zp[level] + PAD + dz, Z1, stride=2)
                    for h in range(count_h):
                        at = (c, h, rows, slice(None)) if count_h > 1 else (c, rows, slice(None))
                        target[at] = target[at] + value[:, h * L:(h + 1) * L]
            return carry
        lax.fori_loop(0, CH * X1, body, 0)

    conv(lambda k, h, base, rows: nT[h, pl.ds(base, rows), :], storer(d0),
         lambda o, c, k: w[FIRST + o * CH + c], lambda c: w[BIAS + c],
         1, CH, H, 0, 2 * L, 16, 0, X)
    pool(d0, p1, 0, H)
    pack(p1, 1, zs1.at[0])
    send(E_P1)
    pack(d0, 0, zsd)
    send(E_D0)
    receive(E_P1)
    unpack(p1, 1, zr1.at[0])
    inner_conv(0, p1, d1, 1, 1, L, min(32, Zl[1]))
    pool(d1, p2, 1, 1)
    pack(p2, 2, zs2.at[0])
    send(E_P2)

    def residual_out(i, carry):
        x, h = i // H, lax.rem(i, H)
        at = (h, pl.ds(pl.multiple_of((x + 1) * Zp[0] + PAD, 8), Z), slice(None))
        block = rT[at] - sc[0:1] * iT[at]
        res_out[x, pl.ds(pl.multiple_of(h * L, L), L), :] = block.T
        return carry
    lax.fori_loop(0, X * H // 2, residual_out, 0)

    receive(E_P2)
    unpack(p2, 2, zr2.at[0])
    inner_conv(1, p2, d2, 1, 2, L // 2, min(32, Zl[2]))
    pool(d2, p3, 2, 1)
    pack(p3, 3, zs3.at[0])
    send(E_P3)
    lax.fori_loop(X * H // 2, X * H, residual_out, 0)
    receive(E_P3)
    unpack(p3, 3, zr3.at[0])
    inner_conv(2, p3, d3, 1, 3, L // 4, min(16, Zl[3]))
    add_up(d3, d2, 2, 1)
    pack(d2, 2, zs2.at[1])
    send(E_S2)

    def pre_body(i, carry):
        per = Z // RI
        base = pl.multiple_of((i // per + 1) * Zp[0] + PAD + lax.rem(i, per) * RI, 8)
        for h in range(H):
            at = (h, pl.ds(base, RI), slice(None))
            pre[at] = (rT[at] - sc[0:1] * iT[at]) / (6.0 + gT[at])
        return carry
    lax.fori_loop(0, X * (Z // RI), pre_body, 0)

    receive(E_S2)
    unpack(d2, 2, zr2.at[1])
    inner_conv(3, d2, r2, 1, 2, L // 2, min(32, Zl[2]))
    add_up(r2, d1, 1, 1)
    pack(d1, 1, zs1.at[1])
    send(E_S1)
    receive(E_S1)
    unpack(d1, 1, zr1.at[1])
    inner_conv(4, d1, r1, 1, 1, L, min(32, Zl[1]))
    pack(r1, 1, zs1.at[2])
    send(E_R1)
    sent(E_D0)
    add_up(r1, d0, 0, H)
    receive(E_D0)
    unpack(d0, 0, zrd)
    receive(E_R1)

    for side, plane1, plane0 in ((0, 0, 0), (1, Xl[1] + 1, X + 1)):
        def halo_body(c, carry, plane1=plane1, plane0=plane0):
            value = raised(r1[c, pl.ds(plane1 * Zp[1] + PAD, Zl[1]), :], H)
            for dz in range(2):
                rows = pl.ds(plane0 * Zp[0] + PAD + dz, Zl[1], stride=2)
                for h in range(H):
                    d0[c, h, rows, :] = d0[c, h, rows, :] + value[:, h * L:(h + 1) * L]
            return carry
        lax.fori_loop(0, CH, halo_body, 0)
    for side, at in ((0, PAD - 1), (1, PAD + Z)):
        value = raised(zr1[2, side], H)
        for c in range(CH):
            for x1 in range(Xl[1]):
                for dx in range(2):
                    for h in range(H):
                        row = (2 * x1 + dx + 1) * Zp[0] + at
                        line = value[c * Xl[1] + x1:c * Xl[1] + x1 + 1, h * L:(h + 1) * L]
                        d0[c, h, row:row + 1, :] = d0[c, h, row:row + 1, :] + line

    inner_conv(5, d0, z0, H, 0, 2 * L, 16)

    def last_w(o, k):
        return w[LAST + o * CH + k]

    for side, plane, o in ((0, 1, 2), (1, X, 1)):
        def part_body(i, carry, side=side, plane=plane, o=o):
            base = pl.multiple_of(i * 32, 8)
            for h in range(H):
                total = None
                for k in range(CH):
                    term = last_w(o, k) * z0[k, h, pl.ds(plane * Zp[0] + PAD + base, 32), :]
                    total = term if total is None else total + term
                xs_m[side, h, pl.ds(base, 32), :] = total
            return carry
        lax.fori_loop(0, Z // 32, part_body, 0)
    for side, at, o in ((0, 0, 6), (1, Z - 1, 5)):
        for h in range(H):
            total = None
            for k in range(CH):
                term = last_w(o, k) * z0[k, h, pl.ds(Zp[0] + PAD + at, X, stride=Zp[0]), :]
                total = term if total is None else total + term
            zs_m[side, pl.ds(h * X, X), :] = total
    send(E_NET)

    def put_net(c, h, base, rows, value):
        net[h, pl.ds(base, rows), :] = value

    conv(loader(z0), put_net, lambda o, c, k: last_w(o, k), None,
         CH, 1, H, 0, 2 * L, 32, 0, X)
    receive(E_NET)
    for side, plane in ((0, 1), (1, X)):
        for h in range(H):
            at = (h, pl.ds(plane * Zp[0] + PAD, Z), slice(None))
            net[at] = net[at] + xr_m[side, h]
    for side, row in ((0, 0), (1, Z - 1)):
        for h in range(H):
            at = (h, pl.ds(Zp[0] + PAD + row, X, stride=Zp[0]), slice(None))
            net[at] = net[at] + zr_m[side, pl.ds(h * X, X), :]

    def pre_sum(i, carry):
        per = Z // RI
        base = pl.multiple_of((i // per + 1) * Zp[0] + PAD + lax.rem(i, per) * RI, 8)
        for h in range(H):
            at = (h, pl.ds(base, RI), slice(None))
            value = pre[at] + sc[2:3] * net[at]
            pre[at] = value
            carry = carry + fold(value * iT[at])
        return carry
    over = lax.fori_loop(0, X * (Z // RI), pre_sum, jnp.zeros((8, L), F32))
    a_send[1] = over
    copies = reduce_start(n_a, a_send.at[1], a_recv.at[1], asend_sem.at[1], arecv_sem.at[1], peer_a)
    pending += copies

    def turn_pre(i, carry):
        x, h = i // H, lax.rem(i, H)
        block = pre[h, pl.ds(pl.multiple_of((x + 1) * Zp[0] + PAD, 8), Z), :]
        dir_out[x, pl.ds(pl.multiple_of(h * L, L), L), :] = block.T
        return carry

    lax.fori_loop(0, X * H // 2, turn_pre, 0)
    b_send[1] = reduce_end(copies, a_send.at[1], a_recv.at[1])
    copies = reduce_start(n_chip, b_send.at[1], b_recv.at[1], bsend_sem.at[1], brecv_sem.at[1], peer_b)
    pending += copies
    lax.fori_loop(X * H // 2, X * H, turn_pre, 0)
    total = reduce_end(copies, b_send.at[1], b_recv.at[1])
    total = jnp.sum(jnp.sum(total, axis=0, keepdims=True), axis=1, keepdims=True)
    beta = jnp.broadcast_to(total, (1, L)) / sc[3:4]
    beta = beta[:, :Z] if Z < L else beta

    def finish(i, carry):
        at = (i // 4, pl.ds(pl.multiple_of(lax.rem(i, 4) * 64, 8), 64), slice(None))
        dir_out[at] = dir_out[at] - beta * dir_in[at]
        return carry
    lax.fori_loop(0, X * 4, finish, 0)

    for copy in pending:
        copy.wait_send()
    for e in range(N_EX):
        if e != E_D0:
            sent(e)


def on_device(residual, direction, diagonal, first_weight, conv_weights, last_weight, biases):
    X, Y, Z = residual.shape
    n_slab, n_col = lax.axis_size("slab"), lax.axis_size("col")
    H = Y // L
    flat = jnp.concatenate([first_weight.reshape(-1), conv_weights.reshape(-1),
                            last_weight.reshape(-1), biases.reshape(-1)])
    Zl = [Z // 2**l for l in range(4)]
    Xl = [X // 2**l for l in range(4)]
    rows = [(Xl[l] + 2) * (Zl[l] + 2 * PAD) for l in range(4)]
    one = pltpu.VMEM((H, rows[0], L), F32)
    four = pltpu.VMEM((CH, H, rows[0], L), F32)

    def level(l):
        return pltpu.VMEM((CH, rows[l], L), F32)

    def edge(*lead):
        return pltpu.VMEM((*lead, L), F32)

    def edge_rows(l):
        return max(8, CH * Xl[l])

    n_a, n_b = 2 * n_col, n_slab // 2
    scratch = [
        one, one, one, one, one, four, four, one, one,
        level(1), level(1), level(1), level(2), level(2), level(2), level(3), level(3),
        edge(3, 2, H * X), edge(3, 2, H * X), edge(2, CH * H * X), edge(2, CH * H * X),
        edge(3, 2, edge_rows(1)), edge(3, 2, edge_rows(1)),
        edge(2, 2, edge_rows(2)), edge(2, 2, edge_rows(2)),
        edge(1, 2, edge_rows(3)), edge(1, 2, edge_rows(3)),
        edge(2, H, Z), edge(2, H, Z), edge(2, H * X), edge(2, H * X),
        pltpu.VMEM((2 * L, L), BF16), pltpu.VMEM((L, 2 * L), BF16), edge(8),
        edge(2, 8), edge(2, n_a - 1, 8), edge(2, 8), edge(2, n_b - 1, 8),
        pltpu.SemaphoreType.DMA((N_EX, 4)), pltpu.SemaphoreType.DMA((N_EX, 4)),
        pltpu.SemaphoreType.DMA((2, n_a - 1)), pltpu.SemaphoreType.DMA((2, n_a - 1)),
        pltpu.SemaphoreType.DMA((2, n_b - 1)), pltpu.SemaphoreType.DMA((2, n_b - 1)),
    ]
    vmem = pl.BlockSpec(memory_space=pltpu.VMEM)
    return pl.pallas_call(
        functools.partial(kernel, n_slab, n_col, X, Z),
        out_shape=(jax.ShapeDtypeStruct((X, Y, Z), F32),) * 2,
        in_specs=[pl.BlockSpec(memory_space=pltpu.SMEM), vmem, vmem, vmem],
        out_specs=(vmem, vmem),
        scratch_shapes=scratch,
        compiler_params=pltpu.CompilerParams(
            collective_id=0, has_side_effects=True, vmem_limit_bytes=56 * 2**20),
    )(flat, residual, direction, diagonal)


def solution(mesh):
    in_specs = (P("slab", None, "col"),) * 3 + (P(),) * 4
    return jax.shard_map(
        on_device, mesh=mesh, in_specs=in_specs,
        out_specs=(P("slab", None, "col"),) * 2, check_vma=False,
    )
```

```python
import functools

import jax
import jax.numpy as jnp
from jax import lax
from jax.experimental import pallas as pl
from jax.experimental.pallas import tpu as pltpu
from jax.sharding import PartitionSpec as P

MESH = pl.DeviceIdType.MESH
L = 128
PAD = 8
CH = 4
F32 = jnp.float32
BF16 = jnp.bfloat16

(E_DIR, E_RES, E_IMG, E_P1, E_D0, E_P2, E_D1, E_P3, E_D2, E_R3, E_R2, E_R1, E_NET) = range(13)
N_EX = 13


def split2(value):
    high = value.astype(BF16)
    low = (value - high.astype(F32)).astype(BF16)
    return high, low


def kernel(n_slab, n_col, X, Z, *refs):
    (w_first, w_conv, w_last, w_bias, res_in, dir_in, diag_in, res_out, dir_out,
     dT, rT, iT, nT, gT, d0, z0, net, pre,
     p1, d1, r1, p2, d2, r2, p3, d3,
     zs0, zr0, zsd, zrd, zs1, zr1, zs2, zr2, zs3, zr3, xs_m, xr_m, zs_m, zr_m,
     pool_m, up_m, beside_m, sc, a_send, a_recv, b_send, b_recv,
     send_sem, recv_sem, asend_sem, arecv_sem, bsend_sem, brecv_sem) = refs
    H = 2
    U_FIRST, U_LAST, R_RISE, U_RISE = 4, 4, 32, 1
    slab = lax.axis_index("slab")
    col = lax.axis_index("col")
    core = lax.rem(slab, 2)
    chip = slab // 2
    n_chip = n_slab // 2
    n_a = 2 * n_col
    Zp = [Z // 2**l + 2 * PAD for l in range(4)]
    Zl = [Z // 2**l for l in range(4)]
    Xl = [X // 2**l for l in range(4)]
    has = (slab > 0, slab < n_slab - 1, col > 0, col < n_col - 1)
    targets = (
        (jnp.maximum(slab - 1, 0), col),
        (jnp.minimum(slab + 1, n_slab - 1), col),
        (slab, jnp.maximum(col - 1, 0)),
        (slab, jnp.minimum(col + 1, n_col - 1)),
    )
    opposite = (1, 0, 3, 2)

    def x_views(ref, level):
        rows, pitch, count = Zl[level], Zp[level], Xl[level]
        if len(ref.shape) == 3:
            def view(plane):
                return ref.at[:, pl.ds(plane * pitch + PAD, rows), :]
        else:
            def view(plane):
                return ref.at[:, :, pl.ds(plane * pitch + PAD, rows), :]
        return (view(1), view(count)), (view(0), view(count + 1))

    def x_views4(ref, level):
        return x_views(ref, level)

    exchanges = {}

    def define(e, x_src, x_dst, z_src, z_dst):
        msgs = []
        for side in range(4):
            if side < 2:
                src, dst = x_src[side], x_dst[opposite[side]]
            else:
                src, dst = z_src.at[side - 2], z_dst.at[opposite[side] - 2]
            msgs.append(pltpu.make_async_remote_copy(
                src_ref=src, dst_ref=dst,
                send_sem=send_sem.at[e, side],
                recv_sem=recv_sem.at[e, opposite[side]],
                device_id=targets[side], device_id_type=MESH))
        exchanges[e] = msgs

    def send(e, sides=(0, 1, 2, 3)):
        for side in sides:
            @pl.when(has[side])
            def _(side=side):
                exchanges[e][side].start()

    def receive(e, sides=(0, 1, 2, 3)):
        for side in sides:
            @pl.when(has[side])
            def _(side=side):
                exchanges[e][opposite[side]].wait_recv()

    def sent(e):
        for side in range(4):
            @pl.when(has[side])
            def _(side=side):
                exchanges[e][side].wait_send()

    for e, ref, level, zs, zr in (
        (E_DIR, dT, 0, zs0.at[0], zr0.at[0]),
        (E_RES, rT, 0, zs0.at[1], zr0.at[1]),
        (E_IMG, iT, 0, zs0.at[2], zr0.at[2]),
        (E_P1, p1, 1, zs1.at[0], zr1.at[0]),
        (E_D0, d0, 0, zsd, zrd),
        (E_P2, p2, 2, zs2.at[0], zr2.at[0]),
        (E_P3, p3, 3, zs3.at[0], zr3.at[0]),
        (E_D1, d1, 1, zs1.at[1], zr1.at[1]),
        (E_D2, d2, 2, zs2.at[1], zr2.at[1]),
        (E_R3, d3, 3, zs3.at[1], zr3.at[1]),
        (E_R2, r2, 2, zs2.at[2], zr2.at[2]),
        (E_R1, r1, 1, zs1.at[2], zr1.at[2]),
    ):
        src, dst = x_views(ref, level)
        define(e, src, dst, zs, zr)
    define(E_NET, (xs_m.at[0], xs_m.at[1]), (xr_m.at[0], xr_m.at[1]), zs_m, zr_m)

    def groups(ref):
        if len(ref.shape) == 3:
            return [(i,) for i in range(ref.shape[0])]
        return [(c, h) for c in range(ref.shape[0]) for h in range(ref.shape[1])]

    def rows_at(start, count, stride):
        return pl.ds(start, count, stride=stride) if count > 1 else pl.ds(start, 1)

    def pack(ref, level, zs):
        pitch, count = Zp[level], Xl[level]
        for side, row in ((0, 0), (1, Zl[level] - 1)):
            for g, index in enumerate(groups(ref)):
                zs[side, pl.ds(g * count, count), :] = ref[
                    (*index, rows_at(pitch + PAD + row, count, pitch), slice(None))]

    def unpack(ref, level, zr):
        pitch, count = Zp[level], Xl[level]
        for side, row in ((0, -1), (1, Zl[level])):
            for g, index in enumerate(groups(ref)):
                ref[(*index, rows_at(pitch + PAD + row, count, pitch), slice(None))] = zr[
                    side, pl.ds(g * count, count), :]

    for side in (0, 1):
        @pl.when(jnp.logical_not(has[side]))
        def _(side=side):
            for ref, level in ((dT, 0), (rT, 0), (iT, 0), (p1, 1), (p2, 2), (p3, 3),
                               (d1, 1), (d2, 2), (d3, 3), (r2, 2), (r1, 1)):
                plane = 0 if side == 0 else Xl[level] + 1
                for index in groups(ref):
                    ref[(*index, pl.ds(plane * Zp[level] + PAD, Zl[level]), slice(None))] = (
                        jnp.zeros((Zl[level], L), F32))
            plane = 0 if side == 0 else X + 1
            for c in range(CH):
                for h in range(H):
                    d0[c, h, pl.ds(plane * Zp[0] + PAD, Z), :] = jnp.zeros((Z, L), F32)
            for h in range(H):
                xr_m[side, h] = jnp.zeros((Z, L), F32)
    for side in (2, 3):
        @pl.when(jnp.logical_not(has[side]))
        def _(side=side):
            s = side - 2
            for ref in (zr0, zr1, zr2, zr3):
                for i in range(ref.shape[0]):
                    ref[i, s] = jnp.zeros(ref.shape[2:], F32)
            zrd[s] = jnp.zeros(zrd.shape[1:], F32)
            zr_m[s] = jnp.zeros(zr_m.shape[1:], F32)

    rank_a = col * 2 + core

    def peer_a(j):
        rank = lax.rem(rank_a + j, n_a)
        return (chip * 2 + lax.rem(rank, 2), rank // 2)

    def peer_b(j):
        return (lax.rem(chip + j, n_chip) * 2 + core, col)

    barrier = pltpu.get_barrier_semaphore()
    for j in range(1, n_a):
        pl.semaphore_signal(barrier, inc=1, device_id=peer_a(j), device_id_type=MESH)
    for j in range(1, n_chip):
        pl.semaphore_signal(barrier, inc=1, device_id=peer_b(j), device_id_type=MESH)
    for side in (0, 1):
        @pl.when(has[side])
        def _(side=side):
            pl.semaphore_signal(barrier, inc=1, device_id=targets[side], device_id_type=MESH)

    def turn_in(source, target):
        def body(i, carry):
            x, h = i // H, lax.rem(i, H)
            block = source[x, pl.ds(pl.multiple_of(h * L, L), L), :]
            target[h, pl.ds(pl.multiple_of((x + 1) * Zp[0] + PAD, 8), Z), :] = block.T
            return carry
        lax.fori_loop(0, X * H, body, 0, unroll=4)

    turn_in(dir_in, dT)
    pack(dT, 0, zs0.at[0])
    n_wait = (n_a - 1) + (n_chip - 1) + jnp.where(slab > 0, 1, 0) + jnp.where(slab < n_slab - 1, 1, 0)
    pl.semaphore_wait(barrier, n_wait)
    send(E_DIR)
    turn_in(res_in, rT)
    pack(rT, 0, zs0.at[1])
    send(E_RES)
    turn_in(diag_in, gT)

    def beside_y(center, ny):
        rows = center[0].shape[0]
        lane = lax.broadcasted_iota(jnp.int32, (rows, L), 1)
        count = len(center)
        last = L - 1 if count > 1 else ny - 1
        up = [pltpu.roll(v, 1, 1) for v in center]
        down = [pltpu.roll(v, L - 1, 1) for v in center]
        zero = jnp.zeros((rows, L), F32)
        minus = [jnp.where(lane == 0, up[h - 1] if h > 0 else zero, up[h]) for h in range(count)]
        plus = [jnp.where(lane == last, down[h + 1] if h < count - 1 else zero, down[h])
                for h in range(count)]
        return minus, plus

    def fold(value):
        return jnp.sum(value.reshape(value.shape[0] // 8, 8, L), axis=0)

    receive(E_DIR)
    unpack(dT, 0, zr0.at[0])
    RI = 32

    def image_body(i, carry):
        per = Z // RI
        base = pl.multiple_of((i // per + 1) * Zp[0] + PAD + lax.rem(i, per) * RI, 8)
        center = [dT[h, pl.ds(base, RI), :] for h in range(H)]
        minus, plus = beside_y(center, 2 * L)
        sums = list(carry)
        for h in range(H):
            beside = dT[h, pl.ds(base + Zp[0], RI), :] + dT[h, pl.ds(base - Zp[0], RI), :]
            beside = beside + plus[h] + minus[h]
            beside = beside + dT[h, pl.ds(base + 1, RI), :] + dT[h, pl.ds(base - 1, RI), :]
            image = (6.0 + gT[h, pl.ds(base, RI), :]) * center[h] - beside
            iT[h, pl.ds(base, RI), :] = image
            r = rT[h, pl.ds(base, RI), :]
            for q, term in enumerate((center[h] * image, r * center[h], r * r, r * image,
                                      image * image)):
                sums[q] = sums[q] + fold(term)
        return tuple(sums)

    sums = lax.fori_loop(0, X * (Z // RI), image_body,
                         tuple(jnp.zeros((8, L), F32) for _ in range(5)), unroll=2)

    def reduce_start(n, send_ref, recv_ref, ssem, rsem, peer):
        copies = []
        for j in range(1, n):
            copy = pltpu.make_async_remote_copy(
                src_ref=send_ref, dst_ref=recv_ref.at[j - 1], send_sem=ssem.at[j - 1],
                recv_sem=rsem.at[j - 1], device_id=peer(j), device_id_type=MESH)
            copy.start()
            copies.append(copy)
        return copies

    def reduce_end(copies, send_ref, recv_ref):
        total = send_ref[...]
        for j, copy in enumerate(copies):
            copy.wait_recv()
        for j in range(len(copies)):
            total = total + recv_ref[j]
        return total

    pending = []
    a_send[0] = jnp.zeros((8, L), F32)
    for q in range(5):
        a_send[0, q:q + 1, :] = jnp.sum(sums[q], axis=0, keepdims=True)
    copies = reduce_start(n_a, a_send.at[0], a_recv.at[0], asend_sem.at[0], arecv_sem.at[0], peer_a)
    pending += copies
    pack(iT, 0, zs0.at[2])
    send(E_IMG)
    b_send[0] = reduce_end(copies, a_send.at[0], a_recv.at[0])
    copies = reduce_start(n_chip, b_send.at[0], b_recv.at[0], bsend_sem.at[0], brecv_sem.at[0], peer_b)
    pending += copies

    row = lax.broadcasted_iota(jnp.int32, (2 * L, L), 0)
    lane = lax.broadcasted_iota(jnp.int32, (2 * L, L), 1)
    pool_m[...] = jnp.where(row // 2 == lane, 0.125, 0.0).astype(BF16)
    row = lax.broadcasted_iota(jnp.int32, (2 * L, 2 * L), 0)
    lane = lax.broadcasted_iota(jnp.int32, (2 * L, 2 * L), 1)
    source = lax.rem(row, L)
    up_m[...] = jnp.where(lane // 2 == source, 1.0, 0.0).astype(BF16)
    for l in range(3):
        match = jnp.where(row < L, (lane + 1) // 2 - 1, (lane + 1) // 2)
        match = jnp.where(source < L // 2**l, match, -1)
        beside_m[l] = jnp.where(match == source, 1.0, 0.0).astype(BF16)
    for c in range(CH):
        for h in range(H):
            for plane in (0, X + 1):
                z0[c, h, pl.ds(plane * Zp[0] + PAD, Z), :] = jnp.zeros((Z, L), F32)
            for at in (PAD - 1, PAD + Z):
                z0[c, h, pl.ds(Zp[0] + at, X, stride=Zp[0]), :] = jnp.zeros((X, L), F32)

    total = reduce_end(copies, b_send.at[0], b_recv.at[0])
    full = jnp.broadcast_to(jnp.sum(total, axis=1, keepdims=True), (8, L))
    curvature = full[0:1]
    alpha = full[1:2] / curvature
    mixed = total[2:3] - 2.0 * alpha * total[3:4] + alpha * alpha * total[4:5]
    squares = jnp.maximum(jnp.broadcast_to(jnp.sum(mixed, axis=1, keepdims=True), (1, L)), 0.0)
    cells = float(X * n_slab) * float(2 * L) * float(Z * n_col)
    scale = jnp.sqrt(squares / cells + 1e-06)
    sc[0:1] = alpha
    sc[1:2] = 1.0 / scale
    sc[2:3] = scale
    sc[3:4] = curvature

    receive(E_RES)
    unpack(rT, 0, zr0.at[1])
    receive(E_IMG)
    unpack(iT, 0, zr0.at[2])
    RN = 2 * PAD

    def feed_body(i, carry):
        base = pl.multiple_of(i * RN, 8)
        a, s = sc[0:1], sc[1:2]
        for h in range(H):
            at = (h, pl.ds(base, RN), slice(None))
            nT[at] = (rT[at] - a * iT[at]) * s
        return carry
    lax.fori_loop(0, (X + 2) * Zp[0] // RN, feed_body, 0)

    def conv(load, store, weight, bias, n_in, n_out, count_h, level, ny, rows, x_from, x_to, unroll=1, relu=True):
        per = Zl[level] // rows
        pitch = Zp[level]

        def body(i, carry):
            base = pl.multiple_of((i // per + x_from + 1) * pitch + PAD + lax.rem(i, per) * rows, 8)
            acc = [[None] * count_h for _ in range(n_out)]
            for k in range(n_in):
                center = [load(k, h, base, rows) for h in range(count_h)]
                minus, plus = beside_y(center, ny)
                for o in range(7):
                    for h in range(count_h):
                        tap = (center[h] if o == 0 else
                               load(k, h, base - pitch, rows) if o == 1 else
                               load(k, h, base + pitch, rows) if o == 2 else
                               minus[h] if o == 3 else plus[h] if o == 4 else
                               load(k, h, base - 1, rows) if o == 5 else
                               load(k, h, base + 1, rows))
                        for c in range(n_out):
                            term = weight(o, c, k) * tap
                            acc[c][h] = term if acc[c][h] is None else acc[c][h] + term
            for c in range(n_out):
                for h in range(count_h):
                    value = acc[c][h]
                    if bias is not None:
                        value = value + bias(c)
                    if relu:
                        value = jnp.maximum(value, 0.0)
                    store(c, h, base, rows, value)
            return carry
        lax.fori_loop(0, (x_to - x_from) * per, body, 0, unroll=unroll)

    def loader(ref):
        if len(ref.shape) == 3:
            return lambda k, h, base, rows: ref[k, pl.ds(base, rows), :]
        return lambda k, h, base, rows: ref[k, h, pl.ds(base, rows), :]

    def storer(ref):
        def put(c, h, base, rows, value):
            if len(ref.shape) == 3:
                ref[c, pl.ds(base, rows), :] = value
            else:
                ref[c, h, pl.ds(base, rows), :] = value
        return put

    def inner_conv(which, source, target, count_h, level, ny, rows, x_from=0, x_to=None, unroll=1, relu=True):
        conv(loader(source), storer(target),
             lambda o, c, k: w_conv[which, c, k, o],
             lambda c: w_bias[c, which + 1],
             CH, CH, count_h, level, ny, rows, x_from, Xl[level] if x_to is None else x_to, unroll, relu)

    def pool(source, target, level, count_h):
        Z1, X1 = Zl[level + 1], Xl[level + 1]

        def body(i, carry):
            c, x1 = i // X1, lax.rem(i, X1)
            parts = []
            for h in range(count_h):
                total = None
                for dx in range(2):
                    for dz in range(2):
                        at = pl.ds((2 * x1 + dx + 1) * Zp[level] + PAD + dz, Z1, stride=2)
                        v = source[c, h, at, :] if count_h > 1 else source[c, at, :]
                        total = v if total is None else total + v
                parts.append(total)
            value = jnp.concatenate(parts, axis=1) if count_h > 1 else parts[0]
            high, low = split2(value)
            m = pool_m[0:count_h * L, :]
            out = jnp.dot(high, m, preferred_element_type=F32) + jnp.dot(low, m, preferred_element_type=F32)
            target[c, pl.ds(pl.multiple_of((x1 + 1) * Zp[level + 1] + PAD, 8), Z1), :] = out
            return carry
        lax.fori_loop(0, CH * X1, body, 0, unroll=4)

    def up_conv(which, source, target, level, count_h, unroll=1):
        Z1, X1 = Zl[level + 1], Xl[level + 1]
        pitch, fine = Zp[level + 1], Zp[level]
        rows = min(16, Z1)
        per = Z1 // rows

        def body(i, carry):
            x1, r1 = i // per, lax.rem(i, per) * rows
            base = pl.multiple_of((x1 + 1) * pitch + PAD + r1, 8)
            flat, sides = [], []
            for c in range(CH):
                total = [None] * 7

                def add(place, term):
                    total[place] = term if total[place] is None else total[place] + term

                for k in range(CH):
                    wt = [w_conv[which, c, k, o] for o in range(7)]
                    here = source[k, pl.ds(base, rows), :]
                    x_low, x_high = wt[1] * here, wt[2] * here
                    z_low, z_high = wt[5] * here, wt[6] * here
                    add(0, wt[0] * here)
                    add(1, x_high)
                    add(1, wt[1] * source[k, pl.ds(base - pitch, rows), :])
                    add(2, x_low)
                    add(2, wt[2] * source[k, pl.ds(base + pitch, rows), :])
                    add(3, z_high)
                    add(3, wt[5] * source[k, pl.ds(base - 1, rows), :])
                    add(4, z_low)
                    add(4, wt[6] * source[k, pl.ds(base + 1, rows), :])
                    add(5, wt[3] * here)
                    add(6, wt[4] * here)
                for dx in range(2):
                    part = total[0] + total[1 + dx]
                    for dz in range(2):
                        flat.append(jnp.concatenate(split2(part + total[3 + dz]), axis=1))
                low, high = split2(total[5]), split2(total[6])
                sides.append([jnp.concatenate([low[n], high[n]], axis=1) for n in range(2)])
            flat = jnp.concatenate(flat, axis=0)
            flat = jnp.dot(flat, up_m[:, 0:count_h * L], preferred_element_type=F32)
            sides = jnp.concatenate([v[0] for v in sides] + [v[1] for v in sides], axis=0)
            sides = jnp.dot(sides, beside_m[level, :, 0:count_h * L], preferred_element_type=F32)
            for c in range(CH):
                side = sides[c * rows:(c + 1) * rows] + sides[(CH + c) * rows:(CH + c + 1) * rows]
                for dx in range(2):
                    for dz in range(2):
                        n = (c * 2 + dx) * 2 + dz
                        value = flat[n * rows:(n + 1) * rows] + side
                        at_rows = pl.ds((2 * x1 + dx + 1) * fine + PAD + 2 * r1 + dz, rows, stride=2)
                        for h in range(count_h):
                            at = (c, h, at_rows, slice(None)) if count_h > 1 else (c, at_rows, slice(None))
                            target[at] = jnp.maximum(target[at] + value[:, h * L:(h + 1) * L], 0.0)
            return carry
        lax.fori_loop(0, X1 * per, body, 0, unroll=unroll)

    conv(lambda k, h, base, rows: nT[h, pl.ds(base, rows), :], storer(d0),
         lambda o, c, k: w_first[c, o], lambda c: w_bias[c, 0],
         1, CH, H, 0, 2 * L, 16, 0, X, unroll=U_FIRST)
    def lin0(x_from, x_to):
        inner_conv(5, d0, z0, H, 0, 2 * L, R_RISE, x_from, x_to, unroll=U_RISE, relu=False)

    def residual_out(i, carry):
        x, h = i // H, lax.rem(i, H)
        at = (h, pl.ds(pl.multiple_of((x + 1) * Zp[0] + PAD, 8), Z), slice(None))
        block = rT[at] - sc[0:1] * iT[at]
        res_out[x, pl.ds(pl.multiple_of(h * L, L), L), :] = block.T
        return carry

    def pre_body(i, carry):
        per = Z // RI
        base = pl.multiple_of((i // per + 1) * Zp[0] + PAD + lax.rem(i, per) * RI, 8)
        for h in range(H):
            at = (h, pl.ds(base, RI), slice(None))
            pre[at] = (rT[at] - sc[0:1] * iT[at]) / (6.0 + gT[at])
        return carry

    pack(d0, 0, zsd)
    send(E_D0, (2, 3))
    pool(d0, p1, 0, H)
    pack(p1, 1, zs1.at[0])
    send(E_P1)
    send(E_D0, (0, 1))
    receive(E_D0, (2, 3))
    unpack(d0, 0, zrd)
    lin0(1, 3)
    receive(E_P1)
    unpack(p1, 1, zr1.at[0])
    inner_conv(0, p1, d1, 1, 1, L, min(32, Zl[1]))
    pool(d1, p2, 1, 1)
    pack(p2, 2, zs2.at[0])
    send(E_P2)
    pack(d1, 1, zs1.at[1])
    send(E_D1)
    lin0(3, 5)
    receive(E_P2)
    unpack(p2, 2, zr2.at[0])
    inner_conv(1, p2, d2, 1, 2, L // 2, min(32, Zl[2]))
    pool(d2, p3, 2, 1)
    pack(p3, 3, zs3.at[0])
    send(E_P3)
    pack(d2, 2, zs2.at[1])
    send(E_D2)
    lin0(5, 7)
    receive(E_P3)
    unpack(p3, 3, zr3.at[0])
    inner_conv(2, p3, d3, 1, 3, L // 4, min(16, Zl[3]))
    pack(d3, 3, zs3.at[1])
    send(E_R3)
    receive(E_D2)
    unpack(d2, 2, zr2.at[1])
    inner_conv(3, d2, r2, 1, 2, L // 2, min(32, Zl[2]), relu=False)
    receive(E_D1)
    unpack(d1, 1, zr1.at[1])
    inner_conv(4, d1, r1, 1, 1, L, min(32, Zl[1]), relu=False)
    lax.fori_loop(0, X * H // 2, residual_out, 0, unroll=4)
    receive(E_R3)
    unpack(d3, 3, zr3.at[1])
    up_conv(3, d3, r2, 2, 1)
    pack(r2, 2, zs2.at[2])
    send(E_R2)
    lax.fori_loop(X * H // 2, X * H, residual_out, 0, unroll=4)
    receive(E_D0, (0, 1))
    lin0(0, 1)
    receive(E_R2)
    unpack(r2, 2, zr2.at[2])
    up_conv(4, r2, r1, 1, 1)
    pack(r1, 1, zs1.at[2])
    send(E_R1)
    lin0(X - 1, X)
    lax.fori_loop(0, X * (Z // RI), pre_body, 0, unroll=2)
    receive(E_R1)
    unpack(r1, 1, zr1.at[2])
    up_conv(5, r1, z0, 0, H)
    def last_w(o, k):
        return w_last[k, o]

    for side, plane, o in ((0, 1, 2), (1, X, 1)):
        def part_body(i, carry, side=side, plane=plane, o=o):
            base = pl.multiple_of(i * 32, 8)
            for h in range(H):
                total = None
                for k in range(CH):
                    term = last_w(o, k) * z0[k, h, pl.ds(plane * Zp[0] + PAD + base, 32), :]
                    total = term if total is None else total + term
                xs_m[side, h, pl.ds(base, 32), :] = total
            return carry
        lax.fori_loop(0, Z // 32, part_body, 0)
    for side, at, o in ((0, 0, 6), (1, Z - 1, 5)):
        for h in range(H):
            total = None
            for k in range(CH):
                term = last_w(o, k) * z0[k, h, pl.ds(Zp[0] + PAD + at, X, stride=Zp[0]), :]
                total = term if total is None else total + term
            zs_m[side, pl.ds(h * X, X), :] = total
    send(E_NET)

    def put_net(c, h, base, rows, value):
        net[h, pl.ds(base, rows), :] = value

    conv(loader(z0), put_net, lambda o, c, k: last_w(o, k), None,
          CH, 1, H, 0, 2 * L, 32, 0, X, unroll=U_LAST, relu=False)
    receive(E_NET)
    for side, plane in ((0, 1), (1, X)):
        for h in range(H):
            at = (h, pl.ds(plane * Zp[0] + PAD, Z), slice(None))
            net[at] = net[at] + xr_m[side, h]
    for side, row in ((0, 0), (1, Z - 1)):
        for h in range(H):
            at = (h, pl.ds(Zp[0] + PAD + row, X, stride=Zp[0]), slice(None))
            net[at] = net[at] + zr_m[side, pl.ds(h * X, X), :]

    def pre_sum(i, carry):
        per = Z // RI
        base = pl.multiple_of((i // per + 1) * Zp[0] + PAD + lax.rem(i, per) * RI, 8)
        for h in range(H):
            at = (h, pl.ds(base, RI), slice(None))
            value = pre[at] + sc[2:3] * net[at]
            pre[at] = value
            carry = carry + fold(value * iT[at])
        return carry
    over = lax.fori_loop(0, X * (Z // RI), pre_sum, jnp.zeros((8, L), F32))
    a_send[1] = over
    copies = reduce_start(n_a, a_send.at[1], a_recv.at[1], asend_sem.at[1], arecv_sem.at[1], peer_a)
    pending += copies

    def turn_pre(i, carry):
        x, h = i // H, lax.rem(i, H)
        block = pre[h, pl.ds(pl.multiple_of((x + 1) * Zp[0] + PAD, 8), Z), :]
        dir_out[x, pl.ds(pl.multiple_of(h * L, L), L), :] = block.T
        return carry

    lax.fori_loop(0, X * H // 2, turn_pre, 0, unroll=4)
    b_send[1] = reduce_end(copies, a_send.at[1], a_recv.at[1])
    copies = reduce_start(n_chip, b_send.at[1], b_recv.at[1], bsend_sem.at[1], brecv_sem.at[1], peer_b)
    pending += copies
    lax.fori_loop(X * H // 2, X * H, turn_pre, 0, unroll=4)
    total = reduce_end(copies, b_send.at[1], b_recv.at[1])
    total = jnp.sum(jnp.sum(total, axis=0, keepdims=True), axis=1, keepdims=True)
    beta = jnp.broadcast_to(total, (1, L)) / sc[3:4]
    beta = beta[:, :Z] if Z < L else beta

    def finish(i, carry):
        at = (i // 4, pl.ds(pl.multiple_of(lax.rem(i, 4) * 64, 8), 64), slice(None))
        dir_out[at] = dir_out[at] - beta * dir_in[at]
        return carry
    lax.fori_loop(0, X * 4, finish, 0)

    for copy in pending:
        copy.wait_send()
    for e in range(N_EX):
        sent(e)


def on_device(residual, direction, diagonal, first_weight, conv_weights, last_weight, biases):
    X, Y, Z = residual.shape
    n_slab, n_col = lax.axis_size("slab"), lax.axis_size("col")
    H = Y // L
    Zl = [Z // 2**l for l in range(4)]
    Xl = [X // 2**l for l in range(4)]
    rows = [(Xl[l] + 2) * (Zl[l] + 2 * PAD) for l in range(4)]
    one = pltpu.VMEM((H, rows[0], L), F32)
    four = pltpu.VMEM((CH, H, rows[0], L), F32)

    def level(l):
        return pltpu.VMEM((CH, rows[l], L), F32)

    def edge(*lead):
        return pltpu.VMEM((*lead, L), F32)

    def edge_rows(l):
        return max(8, CH * Xl[l])

    n_a, n_b = 2 * n_col, n_slab // 2
    scratch = [
        one, one, one, one, one, four, four, one, one,
        level(1), level(1), level(1), level(2), level(2), level(2), level(3), level(3),
        edge(3, 2, H * X), edge(3, 2, H * X), edge(2, CH * H * X), edge(2, CH * H * X),
        edge(3, 2, edge_rows(1)), edge(3, 2, edge_rows(1)),
        edge(3, 2, edge_rows(2)), edge(3, 2, edge_rows(2)),
        edge(2, 2, edge_rows(3)), edge(2, 2, edge_rows(3)),
        edge(2, H, Z), edge(2, H, Z), edge(2, H * X), edge(2, H * X),
        pltpu.VMEM((2 * L, L), BF16), pltpu.VMEM((2 * L, 2 * L), BF16),
        pltpu.VMEM((3, 2 * L, 2 * L), BF16), edge(8),
        edge(2, 8), edge(2, n_a - 1, 8), edge(2, 8), edge(2, n_b - 1, 8),
        pltpu.SemaphoreType.DMA((N_EX, 4)), pltpu.SemaphoreType.DMA((N_EX, 4)),
        pltpu.SemaphoreType.DMA((2, n_a - 1)), pltpu.SemaphoreType.DMA((2, n_a - 1)),
        pltpu.SemaphoreType.DMA((2, n_b - 1)), pltpu.SemaphoreType.DMA((2, n_b - 1)),
    ]
    vmem = pl.BlockSpec(memory_space=pltpu.VMEM)
    return pl.pallas_call(
        functools.partial(kernel, n_slab, n_col, X, Z),
        out_shape=(jax.ShapeDtypeStruct((X, Y, Z), F32),) * 2,
        in_specs=[pl.BlockSpec(memory_space=pltpu.SMEM)] * 4 + [vmem] * 3,
        out_specs=(vmem, vmem),
        scratch_shapes=scratch,
        compiler_params=pltpu.CompilerParams(
            collective_id=0, has_side_effects=True, vmem_limit_bytes=56 * 2**20),
    )(first_weight.T, conv_weights.transpose(0, 2, 3, 1), last_weight.T, biases.T,
      residual, direction, diagonal)


def solution(mesh):
    in_specs = (P("slab", None, "col"),) * 3 + (P(),) * 4
    return jax.shard_map(
        on_device, mesh=mesh, in_specs=in_specs,
        out_specs=(P("slab", None, "col"),) * 2, check_vma=False,
    )
```

```python
import functools

import jax
import jax.numpy as jnp
from jax import lax
from jax.experimental import pallas as pl
from jax.experimental.pallas import tpu as pltpu
from jax.sharding import PartitionSpec as P

MESH = pl.DeviceIdType.MESH
L = 128
PAD = 8
CH = 4
F32 = jnp.float32
BF16 = jnp.bfloat16

(E_DIR, E_RES, E_IMG, E_P1, E_D0, E_P2, E_D1, E_P3, E_D2, E_R3, E_R2, E_R1, E_NET) = range(13)
N_EX = 13


def split2(value):
    high = value.astype(BF16)
    low = (value - high.astype(F32)).astype(BF16)
    return high, low


def kernel(n_slab, n_col, X, Z, *refs):
    (w_first, w_conv, w_last, w_bias, res_hbm, dir_hbm, diag_hbm, image_hbm, pre_hbm, coef_out,
     res_in, dir_in, diag_in, image_out, pre_out, gl, dT, rT, iT, gT, d0, z0, net, pre,
     p1, d1, r1, p2, d2, r2, p3, d3,
     zs0, zr0, zsd, zrd, zs1, zr1, zs2, zr2, zs3, zr3, xs_m, xr_m, zs_m, zr_m,
     pool_m, up_m, beside_m, sc, a_send, a_recv, b_send, b_recv,
     io_sem, send_sem, recv_sem, asend_sem, arecv_sem, bsend_sem, brecv_sem) = refs
    H = 2
    U_FIRST, R_FIRST, U_LAST, R_RISE, U_RISE, U_UP = 4, 16, 4, 32, 1, 2
    slab = lax.axis_index("slab")
    col = lax.axis_index("col")
    core = lax.rem(slab, 2)
    chip = slab // 2
    n_chip = n_slab // 2
    n_a = 2 * n_col
    Zp = [Z // 2**l + 2 * PAD for l in range(4)]
    Zl = [Z // 2**l for l in range(4)]
    Xl = [X // 2**l for l in range(4)]
    has = (slab > 0, slab < n_slab - 1, col > 0, col < n_col - 1)
    targets = (
        (jnp.maximum(slab - 1, 0), col),
        (jnp.minimum(slab + 1, n_slab - 1), col),
        (slab, jnp.maximum(col - 1, 0)),
        (slab, jnp.minimum(col + 1, n_col - 1)),
    )
    opposite = (1, 0, 3, 2)

    def x_views(ref, level):
        rows, pitch, count = Zl[level], Zp[level], Xl[level]
        if len(ref.shape) == 3:
            def view(plane):
                return ref.at[:, pl.ds(plane * pitch + PAD, rows), :]
        else:
            def view(plane):
                return ref.at[:, :, pl.ds(plane * pitch + PAD, rows), :]
        return (view(1), view(count)), (view(0), view(count + 1))

    def x_views4(ref, level):
        return x_views(ref, level)

    exchanges = {}

    def define(e, x_src, x_dst, z_src, z_dst):
        msgs = []
        for side in range(4):
            if side < 2:
                src, dst = x_src[side], x_dst[opposite[side]]
            else:
                src, dst = z_src.at[side - 2], z_dst.at[opposite[side] - 2]
            msgs.append(pltpu.make_async_remote_copy(
                src_ref=src, dst_ref=dst,
                send_sem=send_sem.at[e, side],
                recv_sem=recv_sem.at[e, opposite[side]],
                device_id=targets[side], device_id_type=MESH))
        exchanges[e] = msgs

    def send(e, sides=(0, 1, 2, 3)):
        for side in sides:
            @pl.when(has[side])
            def _(side=side):
                exchanges[e][side].start()

    def receive(e, sides=(0, 1, 2, 3)):
        for side in sides:
            @pl.when(has[side])
            def _(side=side):
                exchanges[e][opposite[side]].wait_recv()

    def sent(e):
        for side in range(4):
            @pl.when(has[side])
            def _(side=side):
                exchanges[e][side].wait_send()

    for e, ref, level, zs, zr in (
        (E_DIR, dT, 0, zs0.at[0], zr0.at[0]),
        (E_RES, rT, 0, zs0.at[1], zr0.at[1]),
        (E_IMG, iT, 0, zs0.at[2], zr0.at[2]),
        (E_P1, p1, 1, zs1.at[0], zr1.at[0]),
        (E_D0, d0, 0, zsd, zrd),
        (E_P2, p2, 2, zs2.at[0], zr2.at[0]),
        (E_P3, p3, 3, zs3.at[0], zr3.at[0]),
        (E_D1, d1, 1, zs1.at[1], zr1.at[1]),
        (E_D2, d2, 2, zs2.at[1], zr2.at[1]),
        (E_R3, d3, 3, zs3.at[1], zr3.at[1]),
        (E_R2, r2, 2, zs2.at[2], zr2.at[2]),
        (E_R1, r1, 1, zs1.at[2], zr1.at[2]),
    ):
        src, dst = x_views(ref, level)
        define(e, src, dst, zs, zr)
    define(E_NET, (xs_m.at[0], xs_m.at[1]), (xr_m.at[0], xr_m.at[1]), zs_m, zr_m)

    def groups(ref):
        if len(ref.shape) == 3:
            return [(i,) for i in range(ref.shape[0])]
        return [(c, h) for c in range(ref.shape[0]) for h in range(ref.shape[1])]

    def rows_at(start, count, stride):
        return pl.ds(start, count, stride=stride) if count > 1 else pl.ds(start, 1)

    def pack(ref, level, zs):
        pitch, count = Zp[level], Xl[level]
        for side, row in ((0, 0), (1, Zl[level] - 1)):
            for g, index in enumerate(groups(ref)):
                zs[side, pl.ds(g * count, count), :] = ref[
                    (*index, rows_at(pitch + PAD + row, count, pitch), slice(None))]

    def unpack(ref, level, zr):
        pitch, count = Zp[level], Xl[level]
        for side, row in ((0, -1), (1, Zl[level])):
            for g, index in enumerate(groups(ref)):
                ref[(*index, rows_at(pitch + PAD + row, count, pitch), slice(None))] = zr[
                    side, pl.ds(g * count, count), :]

    loads = [pltpu.make_async_copy(source, target, io_sem.at[n]) for n, (source, target) in
             enumerate(((dir_hbm, dir_in), (res_hbm, res_in), (diag_hbm, diag_in)))]
    for load in loads:
        load.start()

    for side in (0, 1):
        @pl.when(jnp.logical_not(has[side]))
        def _(side=side):
            for ref, level in ((dT, 0), (rT, 0), (iT, 0), (p1, 1), (p2, 2), (p3, 3),
                               (d1, 1), (d2, 2), (d3, 3), (r2, 2), (r1, 1)):
                plane = 0 if side == 0 else Xl[level] + 1
                for index in groups(ref):
                    ref[(*index, pl.ds(plane * Zp[level] + PAD, Zl[level]), slice(None))] = (
                        jnp.zeros((Zl[level], L), F32))
            plane = 0 if side == 0 else X + 1
            for c in range(CH):
                for h in range(H):
                    d0[c, h, pl.ds(plane * Zp[0] + PAD, Z), :] = jnp.zeros((Z, L), F32)
            for h in range(H):
                xr_m[side, h] = jnp.zeros((Z, L), F32)
    for side in (2, 3):
        @pl.when(jnp.logical_not(has[side]))
        def _(side=side):
            s = side - 2
            for ref in (zr0, zr1, zr2, zr3):
                for i in range(ref.shape[0]):
                    ref[i, s] = jnp.zeros(ref.shape[2:], F32)
            zrd[s] = jnp.zeros(zrd.shape[1:], F32)
            zr_m[s] = jnp.zeros(zr_m.shape[1:], F32)

    rank_a = col * 2 + core

    def peer_a(j):
        rank = lax.rem(rank_a + j, n_a)
        return (chip * 2 + lax.rem(rank, 2), rank // 2)

    def peer_b(j):
        return (lax.rem(chip + j, n_chip) * 2 + core, col)

    barrier = pltpu.get_barrier_semaphore()
    for j in range(1, n_a):
        pl.semaphore_signal(barrier, inc=1, device_id=peer_a(j), device_id_type=MESH)
    for j in range(1, n_chip):
        pl.semaphore_signal(barrier, inc=1, device_id=peer_b(j), device_id_type=MESH)
    for side in (0, 1):
        @pl.when(has[side])
        def _(side=side):
            pl.semaphore_signal(barrier, inc=1, device_id=targets[side], device_id_type=MESH)

    def turn_in(source, target):
        def body(i, carry):
            x, h = i // H, lax.rem(i, H)
            block = source[x, pl.ds(pl.multiple_of(h * L, L), L), :]
            target[h, pl.ds(pl.multiple_of((x + 1) * Zp[0] + PAD, 8), Z), :] = block.T
            return carry
        lax.fori_loop(0, X * H, body, 0, unroll=4)

    loads[0].wait()
    turn_in(dir_in, dT)
    pack(dT, 0, zs0.at[0])
    n_wait = (n_a - 1) + (n_chip - 1) + jnp.where(slab > 0, 1, 0) + jnp.where(slab < n_slab - 1, 1, 0)
    pl.semaphore_wait(barrier, n_wait)
    send(E_DIR)
    loads[1].wait()
    turn_in(res_in, rT)
    pack(rT, 0, zs0.at[1])
    send(E_RES)
    loads[2].wait()
    turn_in(diag_in, gT)

    def beside_y(center, ny):
        rows = center[0].shape[0]
        lane = lax.broadcasted_iota(jnp.int32, (rows, L), 1)
        count = len(center)
        last = L - 1 if count > 1 else ny - 1
        up = [pltpu.roll(v, 1, 1) for v in center]
        down = [pltpu.roll(v, L - 1, 1) for v in center]
        zero = jnp.zeros((rows, L), F32)
        minus = [jnp.where(lane == 0, up[h - 1] if h > 0 else zero, up[h]) for h in range(count)]
        plus = [jnp.where(lane == last, down[h + 1] if h < count - 1 else zero, down[h])
                for h in range(count)]
        return minus, plus

    def fold(value):
        return jnp.sum(value.reshape(value.shape[0] // 8, 8, L), axis=0)

    receive(E_DIR)
    unpack(dT, 0, zr0.at[0])
    RI = 32

    def image_body(i, carry):
        per = Z // RI
        base = pl.multiple_of((i // per + 1) * Zp[0] + PAD + lax.rem(i, per) * RI, 8)
        center = [dT[h, pl.ds(base, RI), :] for h in range(H)]
        minus, plus = beside_y(center, 2 * L)
        sums = list(carry)
        for h in range(H):
            beside = dT[h, pl.ds(base + Zp[0], RI), :] + dT[h, pl.ds(base - Zp[0], RI), :]
            beside = beside + plus[h] + minus[h]
            beside = beside + dT[h, pl.ds(base + 1, RI), :] + dT[h, pl.ds(base - 1, RI), :]
            image = (6.0 + gT[h, pl.ds(base, RI), :]) * center[h] - beside
            iT[h, pl.ds(base, RI), :] = image
            r = rT[h, pl.ds(base, RI), :]
            for q, term in enumerate((center[h] * image, r * center[h], r * r, r * image,
                                      image * image)):
                sums[q] = sums[q] + fold(term)
        return tuple(sums)

    sums = lax.fori_loop(0, X * (Z // RI), image_body,
                         tuple(jnp.zeros((8, L), F32) for _ in range(5)), unroll=2)

    def reduce_start(n, send_ref, recv_ref, ssem, rsem, peer):
        copies = []
        for j in range(1, n):
            copy = pltpu.make_async_remote_copy(
                src_ref=send_ref, dst_ref=recv_ref.at[j - 1], send_sem=ssem.at[j - 1],
                recv_sem=rsem.at[j - 1], device_id=peer(j), device_id_type=MESH)
            copy.start()
            copies.append(copy)
        return copies

    def reduce_end(copies, send_ref, recv_ref):
        total = send_ref[...]
        for j, copy in enumerate(copies):
            copy.wait_recv()
        for j in range(len(copies)):
            total = total + recv_ref[j]
        return total

    pending = []
    a_send[0] = jnp.zeros((8, L), F32)
    for q in range(5):
        a_send[0, q:q + 1, :] = jnp.sum(sums[q], axis=0, keepdims=True)
    copies = reduce_start(n_a, a_send.at[0], a_recv.at[0], asend_sem.at[0], arecv_sem.at[0], peer_a)
    pending += copies
    pack(iT, 0, zs0.at[2])
    send(E_IMG)
    row = lax.broadcasted_iota(jnp.int32, (2 * L, L), 0)
    lane = lax.broadcasted_iota(jnp.int32, (2 * L, L), 1)
    pool_m[...] = jnp.where(row // 2 == lane, 0.125, 0.0).astype(BF16)
    row = lax.broadcasted_iota(jnp.int32, (2 * L, 2 * L), 0)
    lane = lax.broadcasted_iota(jnp.int32, (2 * L, 2 * L), 1)
    source = lax.rem(row, L)
    up_m[...] = jnp.where(lane // 2 == source, 1.0, 0.0).astype(BF16)
    for l in range(3):
        match = jnp.where(row < L, (lane + 1) // 2 - 1, (lane + 1) // 2)
        match = jnp.where(source < L // 2**l, match, -1)
        beside_m[l] = jnp.where(match == source, 1.0, 0.0).astype(BF16)
    for c in range(CH):
        for h in range(H):
            for plane in (0, X + 1):
                z0[c, h, pl.ds(plane * Zp[0] + PAD, Z), :] = jnp.zeros((Z, L), F32)
            for at in (PAD - 1, PAD + Z):
                z0[c, h, pl.ds(Zp[0] + at, X, stride=Zp[0]), :] = jnp.zeros((X, L), F32)

    def conv(load, store, weight, bias, n_in, n_out, count_h, level, ny, rows, x_from, x_to, unroll=1, relu=True):
        per = Zl[level] // rows
        pitch = Zp[level]

        def body(i, carry):
            base = pl.multiple_of((i // per + x_from + 1) * pitch + PAD + lax.rem(i, per) * rows, 8)
            acc = [[None] * count_h for _ in range(n_out)]
            for k in range(n_in):
                center = [load(k, h, base, rows) for h in range(count_h)]
                minus, plus = beside_y(center, ny)
                for o in range(7):
                    for h in range(count_h):
                        tap = (center[h] if o == 0 else
                               load(k, h, base - pitch, rows) if o == 1 else
                               load(k, h, base + pitch, rows) if o == 2 else
                               minus[h] if o == 3 else plus[h] if o == 4 else
                               load(k, h, base - 1, rows) if o == 5 else
                               load(k, h, base + 1, rows))
                        for c in range(n_out):
                            term = weight(o, c, k) * tap
                            acc[c][h] = term if acc[c][h] is None else acc[c][h] + term
            for c in range(n_out):
                for h in range(count_h):
                    value = acc[c][h]
                    if bias is not None:
                        value = value + bias(c)
                    if relu:
                        value = jnp.maximum(value, 0.0)
                    store(c, h, base, rows, value)
            return carry
        lax.fori_loop(0, (x_to - x_from) * per, body, 0, unroll=unroll)

    def loader(ref):
        if len(ref.shape) == 3:
            return lambda k, h, base, rows: ref[k, pl.ds(base, rows), :]
        return lambda k, h, base, rows: ref[k, h, pl.ds(base, rows), :]

    def storer(ref):
        def put(c, h, base, rows, value):
            if len(ref.shape) == 3:
                ref[c, pl.ds(base, rows), :] = value
            else:
                ref[c, h, pl.ds(base, rows), :] = value
        return put

    def inner_conv(which, source, target, count_h, level, ny, rows, x_from=0, x_to=None, unroll=1, relu=True):
        conv(loader(source), storer(target),
             lambda o, c, k: w_conv[which, c, k, o],
             lambda c: w_bias[c, which + 1],
             CH, CH, count_h, level, ny, rows, x_from, Xl[level] if x_to is None else x_to, unroll, relu)

    def pool(source, target, level, count_h, active=None):
        Z1, X1 = Zl[level + 1], Xl[level + 1]

        def body(i, carry):
            c, x1 = i // X1, lax.rem(i, X1)
            parts = []
            for h in range(count_h):
                total = None
                for dx in range(2):
                    for dz in range(2):
                        at = pl.ds((2 * x1 + dx + 1) * Zp[level] + PAD + dz, Z1, stride=2)
                        if active is not None:
                            v = active(c, h, at)
                            source[c, h, at, :] = v
                        else:
                            v = source[c, h, at, :] if count_h > 1 else source[c, at, :]
                        total = v if total is None else total + v
                parts.append(total)
            value = jnp.concatenate(parts, axis=1) if count_h > 1 else parts[0]
            high, low = split2(value)
            m = pool_m[0:count_h * L, :]
            out = jnp.dot(high, m, preferred_element_type=F32) + jnp.dot(low, m, preferred_element_type=F32)
            target[c, pl.ds(pl.multiple_of((x1 + 1) * Zp[level + 1] + PAD, 8), Z1), :] = out
            return carry
        lax.fori_loop(0, CH * X1, body, 0, unroll=4)

    def up_conv(which, source, target, level, count_h, unroll=1, other=None):
        Z1, X1 = Zl[level + 1], Xl[level + 1]
        pitch, fine = Zp[level + 1], Zp[level]
        rows = min(16, Z1)
        per = Z1 // rows

        def body(i, carry):
            x1, r1 = i // per, lax.rem(i, per) * rows
            base = pl.multiple_of((x1 + 1) * pitch + PAD + r1, 8)
            flat, sides = [], []
            for c in range(CH):
                total = [None] * 7

                def add(place, term):
                    total[place] = term if total[place] is None else total[place] + term

                for k in range(CH):
                    wt = [w_conv[which, c, k, o] for o in range(7)]
                    here = source[k, pl.ds(base, rows), :]
                    x_low, x_high = wt[1] * here, wt[2] * here
                    z_low, z_high = wt[5] * here, wt[6] * here
                    add(0, wt[0] * here)
                    add(1, x_high)
                    add(1, wt[1] * source[k, pl.ds(base - pitch, rows), :])
                    add(2, x_low)
                    add(2, wt[2] * source[k, pl.ds(base + pitch, rows), :])
                    add(3, z_high)
                    add(3, wt[5] * source[k, pl.ds(base - 1, rows), :])
                    add(4, z_low)
                    add(4, wt[6] * source[k, pl.ds(base + 1, rows), :])
                    add(5, wt[3] * here)
                    add(6, wt[4] * here)
                for dx in range(2):
                    part = total[0] + total[1 + dx]
                    for dz in range(2):
                        flat.append(jnp.concatenate(split2(part + total[3 + dz]), axis=1))
                low, high = split2(total[5]), split2(total[6])
                sides.append([jnp.concatenate([low[n], high[n]], axis=1) for n in range(2)])
            flat = jnp.concatenate(flat, axis=0)
            flat = jnp.dot(flat, up_m[:, 0:count_h * L], preferred_element_type=F32)
            sides = jnp.concatenate([v[0] for v in sides] + [v[1] for v in sides], axis=0)
            sides = jnp.dot(sides, beside_m[level, :, 0:count_h * L], preferred_element_type=F32)
            for c in range(CH):
                side = sides[c * rows:(c + 1) * rows] + sides[(CH + c) * rows:(CH + c + 1) * rows]
                for dx in range(2):
                    for dz in range(2):
                        n = (c * 2 + dx) * 2 + dz
                        value = flat[n * rows:(n + 1) * rows] + side
                        at_rows = pl.ds((2 * x1 + dx + 1) * fine + PAD + 2 * r1 + dz, rows, stride=2)
                        for h in range(count_h):
                            at = (c, h, at_rows, slice(None)) if count_h > 1 else (c, at_rows, slice(None))
                            out = jnp.maximum(target[at] + value[:, h * L:(h + 1) * L], 0.0)
                            target[at] = out
                            if other is not None:
                                carry = carry + fold(out * other[at])
            return carry
        return lax.fori_loop(0, X1 * per, body, jnp.zeros((8, L), F32), unroll=unroll)

    def first_conv(source, target):
        conv(lambda k, h, base, rows: source[h, pl.ds(base, rows), :], storer(target),
             lambda o, c, k: w_first[c, o], None, 1, CH, H, 0, 2 * L, R_FIRST, 0, X,
             unroll=U_FIRST, relu=False)

    receive(E_RES)
    unpack(rT, 0, zr0.at[1])
    first_conv(rT, d0)
    b_send[0] = reduce_end(copies, a_send.at[0], a_recv.at[0])
    copies = reduce_start(n_chip, b_send.at[0], b_recv.at[0], bsend_sem.at[0], brecv_sem.at[0], peer_b)
    pending += copies
    receive(E_IMG)
    unpack(iT, 0, zr0.at[2])
    first_conv(iT, z0)
    total = reduce_end(copies, b_send.at[0], b_recv.at[0])
    full = jnp.broadcast_to(jnp.sum(total, axis=1, keepdims=True), (8, L))
    curvature = full[0:1]
    alpha = full[1:2] / curvature
    mixed = total[2:3] - 2.0 * alpha * total[3:4] + alpha * alpha * total[4:5]
    squares = jnp.maximum(jnp.broadcast_to(jnp.sum(mixed, axis=1, keepdims=True), (1, L)), 0.0)
    cells = float(X * n_slab) * float(2 * L) * float(Z * n_col)
    scale = jnp.sqrt(squares / cells + 1e-06)
    sc[0:1] = alpha
    sc[1:2] = 1.0 / scale
    sc[4:5] = alpha / scale
    sc[2:3] = scale
    sc[3:4] = curvature
    coef_out[0:1] = alpha

    def lin0(x_from, x_to):
        inner_conv(5, d0, z0, H, 0, 2 * L, R_RISE, x_from, x_to, unroll=U_RISE, relu=False)

    def image_turn(i, carry):
        x, h = i // H, lax.rem(i, H)
        block = iT[h, pl.ds(pl.multiple_of((x + 1) * Zp[0] + PAD, 8), Z), :]
        image_out[x, pl.ds(pl.multiple_of(h * L, L), L), :] = block.T
        return carry

    def pre_body(i, carry):
        per = Z // RI
        base = pl.multiple_of((i // per + 1) * Zp[0] + PAD + lax.rem(i, per) * RI, 8)
        for h in range(H):
            at = (h, pl.ds(base, RI), slice(None))
            image = iT[at]
            value = (rT[at] - sc[0:1] * image) / (6.0 + gT[at])
            pre[at] = value
            carry = carry + fold(value * image)
        return carry

    def transposed_last():
        flip = (0, 2, 1, 4, 3, 6, 5)
        conv(lambda k, h, base, rows: iT[h, pl.ds(base, rows), :], storer(gl),
             lambda o, c, k: w_last[c, flip[o]], None, 1, CH, H, 0, 2 * L, R_FIRST, 0, X,
             unroll=U_FIRST, relu=False)

    def down_zero(c, h, at):
        return jnp.maximum(d0[c, h, at, :] * sc[1:2] - z0[c, h, at, :] * sc[4:5] + w_bias[c, 0], 0.0)

    for side, row in ((0, 0), (1, Z - 1)):
        for c in range(CH):
            for h in range(H):
                zsd[side, pl.ds((c * H + h) * X, X), :] = down_zero(
                    c, h, pl.ds(Zp[0] + PAD + row, X, stride=Zp[0]))
    send(E_D0, (2, 3))
    pool(d0, p1, 0, H, down_zero)
    pack(p1, 1, zs1.at[0])
    send(E_P1)
    send(E_D0, (0, 1))
    transposed_last()
    receive(E_D0, (2, 3))
    unpack(d0, 0, zrd)
    lin0(1, 2)
    receive(E_P1)
    unpack(p1, 1, zr1.at[0])
    inner_conv(0, p1, d1, 1, 1, L, min(32, Zl[1]))
    pool(d1, p2, 1, 1)
    pack(p2, 2, zs2.at[0])
    send(E_P2)
    pack(d1, 1, zs1.at[1])
    send(E_D1)
    lin0(2, 4)
    receive(E_P2)
    unpack(p2, 2, zr2.at[0])
    inner_conv(1, p2, d2, 1, 2, L // 2, min(32, Zl[2]))
    pool(d2, p3, 2, 1)
    pack(p3, 3, zs3.at[0])
    send(E_P3)
    pack(d2, 2, zs2.at[1])
    send(E_D2)
    lin0(4, 5)
    lax.fori_loop(0, X * H // 2, image_turn, 0, unroll=4)
    receive(E_P3)
    unpack(p3, 3, zr3.at[0])
    inner_conv(2, p3, d3, 1, 3, L // 4, min(16, Zl[3]))
    pack(d3, 3, zs3.at[1])
    send(E_R3)
    receive(E_D2)
    unpack(d2, 2, zr2.at[1])
    inner_conv(3, d2, r2, 1, 2, L // 2, min(32, Zl[2]), relu=False)
    receive(E_D1)
    unpack(d1, 1, zr1.at[1])
    inner_conv(4, d1, r1, 1, 1, L, min(32, Zl[1]), relu=False)
    lin0(5, 6)
    receive(E_R3)
    unpack(d3, 3, zr3.at[1])
    up_conv(3, d3, r2, 2, 1)
    pack(r2, 2, zs2.at[2])
    send(E_R2)
    lax.fori_loop(X * H // 2, X * H, image_turn, 0, unroll=4)
    image_copy = pltpu.make_async_copy(image_out, image_hbm, io_sem.at[3])
    image_copy.start()
    lin0(6, 7)
    receive(E_D0, (0, 1))
    lin0(0, 1)
    receive(E_R2)
    unpack(r2, 2, zr2.at[2])
    up_conv(4, r2, r1, 1, 1)
    pack(r1, 1, zs1.at[2])
    send(E_R1)
    lin0(X - 1, X)
    over = lax.fori_loop(0, X * (Z // RI), pre_body, jnp.zeros((8, L), F32), unroll=2)
    receive(E_R1)
    unpack(r1, 1, zr1.at[2])
    over = over + sc[2:3] * up_conv(5, r1, z0, 0, H, U_UP, gl)
    a_send[1] = over
    copies = reduce_start(n_a, a_send.at[1], a_recv.at[1], asend_sem.at[1], arecv_sem.at[1], peer_a)
    pending += copies
    def last_w(o, k):
        return w_last[k, o]

    for side, plane, o in ((0, 1, 2), (1, X, 1)):
        def part_body(i, carry, side=side, plane=plane, o=o):
            base = pl.multiple_of(i * 32, 8)
            for h in range(H):
                total = None
                for k in range(CH):
                    term = last_w(o, k) * z0[k, h, pl.ds(plane * Zp[0] + PAD + base, 32), :]
                    total = term if total is None else total + term
                xs_m[side, h, pl.ds(base, 32), :] = total
            return carry
        lax.fori_loop(0, Z // 32, part_body, 0)
    for side, at, o in ((0, 0, 6), (1, Z - 1, 5)):
        for h in range(H):
            total = None
            for k in range(CH):
                term = last_w(o, k) * z0[k, h, pl.ds(Zp[0] + PAD + at, X, stride=Zp[0]), :]
                total = term if total is None else total + term
            zs_m[side, pl.ds(h * X, X), :] = total
    send(E_NET)

    def put_net(c, h, base, rows, value):
        net[h, pl.ds(base, rows), :] = value

    conv(loader(z0), put_net, lambda o, c, k: last_w(o, k), None,
          CH, 1, H, 0, 2 * L, 32, 0, X, unroll=U_LAST, relu=False)
    b_send[1] = reduce_end(copies, a_send.at[1], a_recv.at[1])
    copies = reduce_start(n_chip, b_send.at[1], b_recv.at[1], bsend_sem.at[1], brecv_sem.at[1], peer_b)
    pending += copies
    receive(E_NET)
    for side, plane in ((0, 1), (1, X)):
        for h in range(H):
            at = (h, pl.ds(plane * Zp[0] + PAD, Z), slice(None))
            net[at] = net[at] + xr_m[side, h]
    for side, row in ((0, 0), (1, Z - 1)):
        for h in range(H):
            at = (h, pl.ds(Zp[0] + PAD + row, X, stride=Zp[0]), slice(None))
            net[at] = net[at] + zr_m[side, pl.ds(h * X, X), :]

    def turn_pre(i, carry):
        x, h = i // H, lax.rem(i, H)
        at = (h, pl.ds(pl.multiple_of((x + 1) * Zp[0] + PAD, 8), Z), slice(None))
        block = pre[at] + sc[2:3] * net[at]
        pre_out[x, pl.ds(pl.multiple_of(h * L, L), L), :] = block.T
        return carry

    lax.fori_loop(0, X * H, turn_pre, 0, unroll=4)
    pre_copy = pltpu.make_async_copy(pre_out, pre_hbm, io_sem.at[4])
    pre_copy.start()
    total = reduce_end(copies, b_send.at[1], b_recv.at[1])
    total = jnp.sum(jnp.sum(total, axis=0, keepdims=True), axis=1, keepdims=True)
    coef_out[1:2] = jnp.broadcast_to(total, (1, L)) / sc[3:4]
    coef_out[2:8] = jnp.zeros((6, L), F32)

    image_copy.wait()
    pre_copy.wait()
    for copy in pending:
        copy.wait_send()
    for e in range(N_EX):
        sent(e)


def on_device(residual, direction, diagonal, first_weight, conv_weights, last_weight, biases):
    X, Y, Z = residual.shape
    n_slab, n_col = lax.axis_size("slab"), lax.axis_size("col")
    H = Y // L
    Zl = [Z // 2**l for l in range(4)]
    Xl = [X // 2**l for l in range(4)]
    rows = [(Xl[l] + 2) * (Zl[l] + 2 * PAD) for l in range(4)]
    field = pltpu.VMEM((X, Y, Z), F32)
    one = pltpu.VMEM((H, rows[0], L), F32)
    four = pltpu.VMEM((CH, H, rows[0], L), F32)

    def level(l):
        return pltpu.VMEM((CH, rows[l], L), F32)

    def edge(*lead):
        return pltpu.VMEM((*lead, L), F32)

    def edge_rows(l):
        return max(8, CH * Xl[l])

    n_a, n_b = 2 * n_col, n_slab // 2
    scratch = [
        field, field, field, field, field, four, one, one, one, one, four, four, one, one,
        level(1), level(1), level(1), level(2), level(2), level(2), level(3), level(3),
        edge(3, 2, H * X), edge(3, 2, H * X), edge(2, CH * H * X), edge(2, CH * H * X),
        edge(3, 2, edge_rows(1)), edge(3, 2, edge_rows(1)),
        edge(3, 2, edge_rows(2)), edge(3, 2, edge_rows(2)),
        edge(2, 2, edge_rows(3)), edge(2, 2, edge_rows(3)),
        edge(2, H, Z), edge(2, H, Z), edge(2, H * X), edge(2, H * X),
        pltpu.VMEM((2 * L, L), BF16), pltpu.VMEM((2 * L, 2 * L), BF16),
        pltpu.VMEM((3, 2 * L, 2 * L), BF16), edge(8),
        edge(2, 8), edge(2, n_a - 1, 8), edge(2, 8), edge(2, n_b - 1, 8),
        pltpu.SemaphoreType.DMA((5,)),
        pltpu.SemaphoreType.DMA((N_EX, 4)), pltpu.SemaphoreType.DMA((N_EX, 4)),
        pltpu.SemaphoreType.DMA((2, n_a - 1)), pltpu.SemaphoreType.DMA((2, n_a - 1)),
        pltpu.SemaphoreType.DMA((2, n_b - 1)), pltpu.SemaphoreType.DMA((2, n_b - 1)),
    ]
    vmem = pl.BlockSpec(memory_space=pltpu.VMEM)
    anywhere = pl.BlockSpec(memory_space=pl.ANY)
    image, pre, coef = pl.pallas_call(
        functools.partial(kernel, n_slab, n_col, X, Z),
        out_shape=(jax.ShapeDtypeStruct((X, Y, Z), F32),) * 2 + (jax.ShapeDtypeStruct((8, L), F32),),
        in_specs=[pl.BlockSpec(memory_space=pltpu.SMEM)] * 4 + [anywhere] * 3,
        out_specs=(anywhere, anywhere, vmem),
        scratch_shapes=scratch,
        compiler_params=pltpu.CompilerParams(
            collective_id=0, has_side_effects=True, vmem_limit_bytes=56 * 2**20),
    )(first_weight.T, conv_weights.transpose(0, 2, 3, 1), last_weight.T, biases.T,
      residual, direction, diagonal)
    return residual - coef[0:1, :Z] * image, pre - coef[1:2, :Z] * direction


def solution(mesh):
    in_specs = (P("slab", None, "col"),) * 3 + (P(),) * 4
    return jax.shard_map(
        on_device, mesh=mesh, in_specs=in_specs,
        out_specs=(P("slab", None, "col"),) * 2, check_vma=False,
    )
```

```python
import functools

import jax
import jax.numpy as jnp
from jax import lax
from jax.experimental import pallas as pl
from jax.experimental.pallas import tpu as pltpu
from jax.sharding import PartitionSpec as P

MESH = pl.DeviceIdType.MESH
L = 128
PAD = 8
CH = 4
F32 = jnp.float32
BF16 = jnp.bfloat16

(E_DIR, E_RES, E_IMG, E_P1, E_D0, E_P2, E_D1, E_P3, E_D2, E_R3, E_R2, E_R1, E_NET) = range(13)
N_EX = 13


def split2(value):
    high = value.astype(BF16)
    low = (value - high.astype(F32)).astype(BF16)
    return high, low


def span(start, stop):
    return stop - start, lambda j: j + start


def ends(count):
    return 2, lambda j: j * (count - 1)


def finish(coef, res, direction, image, pre, res_out, dir_out):
    Z = res.shape[2]
    res_out[...] = res[...] - coef[0:1, :Z] * image[...]
    dir_out[...] = pre[...] - coef[1:2, :Z] * direction[...]


def kernel(n_slab, n_col, X, Z, *refs):
    (w_first, w_conv, w_last, w_bias, res_hbm, dir_hbm, diag_hbm, image_hbm, pre_hbm, coef_out,
     res_in, dir_in, diag_in, image_out, pre_out, gl, dT, rT, iT, gT, d0, z0, net, pre,
     p1, d1, r1, p2, d2, r2, p3, d3,
     zs0, zr0, zsd, zrd, zs1, zr1, zs2, zr2, zs3, zr3, xs_m, xr_m, zs_m, zr_m,
     pool_m, pool_s, up_m, beside_m, sc, a_send, a_recv, b_send, b_recv,
     io_sem, send_sem, recv_sem, asend_sem, arecv_sem, bsend_sem, brecv_sem) = refs
    H = 2
    U_FIRST, R_FIRST, U_LAST, R_RISE, U_RISE, U_UP = 4, 16, 4, 32, 1, 2
    slab = lax.axis_index("slab")
    col = lax.axis_index("col")
    core = lax.rem(slab, 2)
    chip = slab // 2
    n_chip = n_slab // 2
    n_a = 2 * n_col
    Zp = [Z // 2**l + 2 * PAD for l in range(4)]
    Zl = [Z // 2**l for l in range(4)]
    Xl = [X // 2**l for l in range(4)]
    has = (slab > 0, slab < n_slab - 1, col > 0, col < n_col - 1)
    targets = (
        (jnp.maximum(slab - 1, 0), col),
        (jnp.minimum(slab + 1, n_slab - 1), col),
        (slab, jnp.maximum(col - 1, 0)),
        (slab, jnp.minimum(col + 1, n_col - 1)),
    )
    opposite = (1, 0, 3, 2)

    def x_views(ref, level):
        rows, pitch, count = Zl[level], Zp[level], Xl[level]
        if len(ref.shape) == 3:
            def view(plane):
                return ref.at[:, pl.ds(plane * pitch + PAD, rows), :]
        else:
            def view(plane):
                return ref.at[:, :, pl.ds(plane * pitch + PAD, rows), :]
        return (view(1), view(count)), (view(0), view(count + 1))

    def x_views4(ref, level):
        return x_views(ref, level)

    exchanges = {}

    def define(e, x_src, x_dst, z_src, z_dst):
        msgs = []
        for side in range(4):
            if side < 2:
                src, dst = x_src[side], x_dst[opposite[side]]
            else:
                src, dst = z_src.at[side - 2], z_dst.at[opposite[side] - 2]
            msgs.append(pltpu.make_async_remote_copy(
                src_ref=src, dst_ref=dst,
                send_sem=send_sem.at[e, side],
                recv_sem=recv_sem.at[e, opposite[side]],
                device_id=targets[side], device_id_type=MESH))
        exchanges[e] = msgs

    def send(e, sides=(0, 1, 2, 3)):
        for side in sides:
            @pl.when(has[side])
            def _(side=side):
                exchanges[e][side].start()

    def receive(e, sides=(0, 1, 2, 3)):
        for side in sides:
            @pl.when(has[side])
            def _(side=side):
                exchanges[e][opposite[side]].wait_recv()

    def sent(e):
        for side in range(4):
            @pl.when(has[side])
            def _(side=side):
                exchanges[e][side].wait_send()

    for e, ref, level, zs, zr in (
        (E_DIR, dT, 0, zs0.at[0], zr0.at[0]),
        (E_RES, rT, 0, zs0.at[1], zr0.at[1]),
        (E_IMG, iT, 0, zs0.at[2], zr0.at[2]),
        (E_P1, p1, 1, zs1.at[0], zr1.at[0]),
        (E_D0, d0, 0, zsd, zrd),
        (E_P2, p2, 2, zs2.at[0], zr2.at[0]),
        (E_P3, p3, 3, zs3.at[0], zr3.at[0]),
        (E_D1, d1, 1, zs1.at[1], zr1.at[1]),
        (E_D2, d2, 2, zs2.at[1], zr2.at[1]),
        (E_R3, d3, 3, zs3.at[1], zr3.at[1]),
        (E_R2, r2, 2, zs2.at[2], zr2.at[2]),
        (E_R1, r1, 1, zs1.at[2], zr1.at[2]),
    ):
        src, dst = x_views(ref, level)
        define(e, src, dst, zs, zr)
    define(E_NET, (xs_m.at[0], xs_m.at[1]), (xr_m.at[0], xr_m.at[1]), zs_m, zr_m)

    def groups(ref):
        if len(ref.shape) == 3:
            return [(i,) for i in range(ref.shape[0])]
        return [(c, h) for c in range(ref.shape[0]) for h in range(ref.shape[1])]

    def rows_at(start, count, stride):
        return pl.ds(start, count, stride=stride) if count > 1 else pl.ds(start, 1)

    def pack(ref, level, zs):
        pitch, count = Zp[level], Xl[level]
        for side, row in ((0, 0), (1, Zl[level] - 1)):
            for g, index in enumerate(groups(ref)):
                zs[side, pl.ds(g * count, count), :] = ref[
                    (*index, rows_at(pitch + PAD + row, count, pitch), slice(None))]

    def unpack(ref, level, zr):
        pitch, count = Zp[level], Xl[level]
        for side, row in ((0, -1), (1, Zl[level])):
            for g, index in enumerate(groups(ref)):
                ref[(*index, rows_at(pitch + PAD + row, count, pitch), slice(None))] = zr[
                    side, pl.ds(g * count, count), :]

    loads = [pltpu.make_async_copy(source, target, io_sem.at[n]) for n, (source, target) in
             enumerate(((dir_hbm, dir_in), (res_hbm, res_in), (diag_hbm, diag_in)))]
    for load in loads:
        load.start()

    for side in (0, 1):
        @pl.when(jnp.logical_not(has[side]))
        def _(side=side):
            for ref, level in ((dT, 0), (rT, 0), (iT, 0), (p1, 1), (p2, 2), (p3, 3),
                               (d1, 1), (d2, 2), (d3, 3), (r2, 2), (r1, 1)):
                plane = 0 if side == 0 else Xl[level] + 1
                for index in groups(ref):
                    ref[(*index, pl.ds(plane * Zp[level] + PAD, Zl[level]), slice(None))] = (
                        jnp.zeros((Zl[level], L), F32))
            plane = 0 if side == 0 else X + 1
            for c in range(CH):
                for h in range(H):
                    d0[c, h, pl.ds(plane * Zp[0] + PAD, Z), :] = jnp.zeros((Z, L), F32)
            for h in range(H):
                xr_m[side, h] = jnp.zeros((Z, L), F32)
    for side in (2, 3):
        @pl.when(jnp.logical_not(has[side]))
        def _(side=side):
            s = side - 2
            for ref in (zr0, zr1, zr2, zr3):
                for i in range(ref.shape[0]):
                    ref[i, s] = jnp.zeros(ref.shape[2:], F32)
            zrd[s] = jnp.zeros(zrd.shape[1:], F32)
            zr_m[s] = jnp.zeros(zr_m.shape[1:], F32)

    rank_a = col * 2 + core

    def peer_a(j):
        rank = lax.rem(rank_a + j, n_a)
        return (chip * 2 + lax.rem(rank, 2), rank // 2)

    def peer_b(j):
        return (lax.rem(chip + j, n_chip) * 2 + core, col)

    barrier = pltpu.get_barrier_semaphore()
    for j in range(1, n_a):
        pl.semaphore_signal(barrier, inc=1, device_id=peer_a(j), device_id_type=MESH)
    for j in range(1, n_chip):
        pl.semaphore_signal(barrier, inc=1, device_id=peer_b(j), device_id_type=MESH)
    for side in (0, 1):
        @pl.when(has[side])
        def _(side=side):
            pl.semaphore_signal(barrier, inc=1, device_id=targets[side], device_id_type=MESH)

    def turn_in(source, target):
        def body(i, carry):
            x, h = i // H, lax.rem(i, H)
            block = source[x, pl.ds(pl.multiple_of(h * L, L), L), :]
            target[h, pl.ds(pl.multiple_of((x + 1) * Zp[0] + PAD, 8), Z), :] = block.T
            return carry
        lax.fori_loop(0, X * H, body, 0, unroll=4)

    loads[0].wait()
    turn_in(dir_in, dT)
    pack(dT, 0, zs0.at[0])
    n_wait = (n_a - 1) + (n_chip - 1) + jnp.where(slab > 0, 1, 0) + jnp.where(slab < n_slab - 1, 1, 0)
    pl.semaphore_wait(barrier, n_wait)
    send(E_DIR)
    loads[1].wait()
    turn_in(res_in, rT)
    pack(rT, 0, zs0.at[1])
    send(E_RES)
    loads[2].wait()
    turn_in(diag_in, gT)

    def beside_y(center, ny):
        rows = center[0].shape[0]
        lane = lax.broadcasted_iota(jnp.int32, (rows, L), 1)
        count = len(center)
        last = L - 1 if count > 1 else ny - 1
        up = [pltpu.roll(v, 1, 1) for v in center]
        down = [pltpu.roll(v, L - 1, 1) for v in center]
        zero = jnp.zeros((rows, L), F32)
        minus = [jnp.where(lane == 0, up[h - 1] if h > 0 else zero, up[h]) for h in range(count)]
        plus = [jnp.where(lane == last, down[h + 1] if h < count - 1 else zero, down[h])
                for h in range(count)]
        return minus, plus

    def fold(value):
        return jnp.sum(value.reshape(value.shape[0] // 8, 8, L), axis=0)

    RI = 32

    def image_body(i, carry, place):
        per = Z // RI
        base = pl.multiple_of((place(i // per) + 1) * Zp[0] + PAD + lax.rem(i, per) * RI, 8)
        center = [dT[h, pl.ds(base, RI), :] for h in range(H)]
        minus, plus = beside_y(center, 2 * L)
        sums = list(carry)
        for h in range(H):
            beside = dT[h, pl.ds(base + Zp[0], RI), :] + dT[h, pl.ds(base - Zp[0], RI), :]
            beside = beside + plus[h] + minus[h]
            beside = beside + dT[h, pl.ds(base + 1, RI), :] + dT[h, pl.ds(base - 1, RI), :]
            image = (6.0 + gT[h, pl.ds(base, RI), :]) * center[h] - beside
            iT[h, pl.ds(base, RI), :] = image
            r = rT[h, pl.ds(base, RI), :]
            for q, term in enumerate((center[h] * image, r * center[h], r * r, r * image,
                                      image * image)):
                sums[q] = sums[q] + fold(term)
        return tuple(sums)

    sums = tuple(jnp.zeros((8, L), F32) for _ in range(5))
    receive(E_DIR, (2, 3))
    unpack(dT, 0, zr0.at[0])
    for sides, (count, place) in ((None, span(1, X - 1)), ((0, 1), ends(X))):
        if sides is not None:
            receive(E_DIR, sides)
        sums = lax.fori_loop(0, count * (Z // RI), functools.partial(image_body, place=place),
                             sums, unroll=2)

    def reduce_start(n, send_ref, recv_ref, ssem, rsem, peer):
        copies = []
        for j in range(1, n):
            copy = pltpu.make_async_remote_copy(
                src_ref=send_ref, dst_ref=recv_ref.at[j - 1], send_sem=ssem.at[j - 1],
                recv_sem=rsem.at[j - 1], device_id=peer(j), device_id_type=MESH)
            copy.start()
            copies.append(copy)
        return copies

    def reduce_end(copies, send_ref, recv_ref):
        total = send_ref[...]
        for j, copy in enumerate(copies):
            copy.wait_recv()
        for j in range(len(copies)):
            total = total + recv_ref[j]
        return total

    pending = []
    a_send[0] = jnp.zeros((8, L), F32)
    for q in range(5):
        a_send[0, q:q + 1, :] = jnp.sum(sums[q], axis=0, keepdims=True)
    copies = reduce_start(n_a, a_send.at[0], a_recv.at[0], asend_sem.at[0], arecv_sem.at[0], peer_a)
    pending += copies
    pack(iT, 0, zs0.at[2])
    send(E_IMG)
    row = lax.broadcasted_iota(jnp.int32, (2 * L, L), 0)
    lane = lax.broadcasted_iota(jnp.int32, (2 * L, L), 1)
    pool_m[...] = jnp.where(row // 2 == lane, 0.125, 0.0).astype(BF16)
    row = lax.broadcasted_iota(jnp.int32, (2 * L, 2 * L), 0)
    lane = lax.broadcasted_iota(jnp.int32, (2 * L, 2 * L), 1)
    source = lax.rem(row, L)
    up_m[...] = jnp.where(lane // 2 == source, 1.0, 0.0).astype(BF16)
    for l in range(3):
        match = jnp.where(row < L, (lane + 1) // 2 - 1, (lane + 1) // 2)
        match = jnp.where(source < L // 2**l, match, -1)
        beside_m[l] = jnp.where(match == source, 1.0, 0.0).astype(BF16)
    for c in range(CH):
        for h in range(H):
            for plane in (0, X + 1):
                z0[c, h, pl.ds(plane * Zp[0] + PAD, Z), :] = jnp.zeros((Z, L), F32)
            for at in (PAD - 1, PAD + Z):
                z0[c, h, pl.ds(Zp[0] + at, X, stride=Zp[0]), :] = jnp.zeros((X, L), F32)

    def conv(load, store, weight, bias, n_in, n_out, count_h, level, ny, rows, planes, unroll=1, relu=True):
        per = Zl[level] // rows
        pitch = Zp[level]

        def body(i, carry):
            base = pl.multiple_of((planes[1](i // per) + 1) * pitch + PAD + lax.rem(i, per) * rows, 8)
            acc = [[None] * count_h for _ in range(n_out)]
            for k in range(n_in):
                center = [load(k, h, base, rows) for h in range(count_h)]
                minus, plus = beside_y(center, ny)
                for o in range(7):
                    for h in range(count_h):
                        tap = (center[h] if o == 0 else
                               load(k, h, base - pitch, rows) if o == 1 else
                               load(k, h, base + pitch, rows) if o == 2 else
                               minus[h] if o == 3 else plus[h] if o == 4 else
                               load(k, h, base - 1, rows) if o == 5 else
                               load(k, h, base + 1, rows))
                        for c in range(n_out):
                            term = weight(o, c, k) * tap
                            acc[c][h] = term if acc[c][h] is None else acc[c][h] + term
            for c in range(n_out):
                for h in range(count_h):
                    value = acc[c][h]
                    if bias is not None:
                        value = value + bias(c)
                    if relu:
                        value = jnp.maximum(value, 0.0)
                    store(c, h, base, rows, value)
            return carry
        lax.fori_loop(0, planes[0] * per, body, 0, unroll=unroll)

    def loader(ref):
        if len(ref.shape) == 3:
            return lambda k, h, base, rows: ref[k, pl.ds(base, rows), :]
        return lambda k, h, base, rows: ref[k, h, pl.ds(base, rows), :]

    def storer(ref):
        def put(c, h, base, rows, value):
            if len(ref.shape) == 3:
                ref[c, pl.ds(base, rows), :] = value
            else:
                ref[c, h, pl.ds(base, rows), :] = value
        return put

    def inner_conv(which, source, target, count_h, level, ny, rows, planes=None, unroll=1, relu=True):
        conv(loader(source), storer(target),
             lambda o, c, k: w_conv[which, c, k, o],
             lambda c: w_bias[c, which + 1],
             CH, CH, count_h, level, ny, rows, span(0, Xl[level]) if planes is None else planes, unroll, relu)

    def pool(source, target, level, count_h, active=None, planes=None):
        Z0, Z1 = Zl[level], Zl[level + 1]
        count, place = span(0, Xl[level + 1]) if planes is None else planes

        def body(i, carry):
            c, x1 = i // count, place(lax.rem(i, count))
            slot = lax.rem(i, 4)
            parts = []
            for h in range(count_h):
                total = None
                for dx in range(2):
                    at = pl.ds(pl.multiple_of((2 * x1 + dx + 1) * Zp[level] + PAD, 8), Z0)
                    if active is not None:
                        v = active(c, h, at)
                        source[c, h, at, :] = v
                    else:
                        v = source[c, h, at, :] if count_h > 1 else source[c, at, :]
                    total = v if total is None else total + v
                parts.append(total)
            value = jnp.concatenate(parts, axis=1) if count_h > 1 else parts[0]
            high, low = split2(value)
            m = pool_m[0:count_h * L, :]
            out = jnp.dot(high, m, preferred_element_type=F32) + jnp.dot(low, m, preferred_element_type=F32)
            pool_s[slot, 0:Z0, :] = out
            target[c, pl.ds(pl.multiple_of((x1 + 1) * Zp[level + 1] + PAD, 8), Z1), :] = (
                pool_s[slot, pl.ds(0, Z1, stride=2), :] + pool_s[slot, pl.ds(1, Z1, stride=2), :])
            return carry
        lax.fori_loop(0, CH * count, body, 0, unroll=4)

    def up_conv(which, source, target, level, count_h, unroll=1, other=None, planes=None):
        Z1, X1 = Zl[level + 1], Xl[level + 1]
        pitch, fine = Zp[level + 1], Zp[level]
        rows = min(16, Z1)
        per = Z1 // rows
        count, place = span(0, X1) if planes is None else planes

        def body(i, carry):
            x1, r1 = place(i // per), lax.rem(i, per) * rows
            base = pl.multiple_of((x1 + 1) * pitch + PAD + r1, 8)
            flat, sides = [], []
            for c in range(CH):
                total = [None] * 7

                def add(place, term):
                    total[place] = term if total[place] is None else total[place] + term

                for k in range(CH):
                    wt = [w_conv[which, c, k, o] for o in range(7)]
                    here = source[k, pl.ds(base, rows), :]
                    x_low, x_high = wt[1] * here, wt[2] * here
                    z_low, z_high = wt[5] * here, wt[6] * here
                    add(0, wt[0] * here)
                    add(1, x_high)
                    add(1, wt[1] * source[k, pl.ds(base - pitch, rows), :])
                    add(2, x_low)
                    add(2, wt[2] * source[k, pl.ds(base + pitch, rows), :])
                    add(3, z_high)
                    add(3, wt[5] * source[k, pl.ds(base - 1, rows), :])
                    add(4, z_low)
                    add(4, wt[6] * source[k, pl.ds(base + 1, rows), :])
                    add(5, wt[3] * here)
                    add(6, wt[4] * here)
                for dx in range(2):
                    part = total[0] + total[1 + dx]
                    for dz in range(2):
                        flat.append(jnp.concatenate(split2(part + total[3 + dz]), axis=1))
                low, high = split2(total[5]), split2(total[6])
                sides.append([jnp.concatenate([low[n], high[n]], axis=1) for n in range(2)])
            flat = jnp.concatenate(flat, axis=0)
            flat = jnp.dot(flat, up_m[:, 0:count_h * L], preferred_element_type=F32)
            sides = jnp.concatenate([v[0] for v in sides] + [v[1] for v in sides], axis=0)
            sides = jnp.dot(sides, beside_m[level, :, 0:count_h * L], preferred_element_type=F32)
            for c in range(CH):
                side = sides[c * rows:(c + 1) * rows] + sides[(CH + c) * rows:(CH + c + 1) * rows]
                for dx in range(2):
                    for dz in range(2):
                        n = (c * 2 + dx) * 2 + dz
                        value = flat[n * rows:(n + 1) * rows] + side
                        at_rows = pl.ds((2 * x1 + dx + 1) * fine + PAD + 2 * r1 + dz, rows, stride=2)
                        for h in range(count_h):
                            at = (c, h, at_rows, slice(None)) if count_h > 1 else (c, at_rows, slice(None))
                            out = jnp.maximum(target[at] + value[:, h * L:(h + 1) * L], 0.0)
                            target[at] = out
                            if other is not None:
                                carry = carry + fold(out * other[at])
            return carry
        return lax.fori_loop(0, count * per, body, jnp.zeros((8, L), F32), unroll=unroll)

    def first_conv(source, target):
        conv(lambda k, h, base, rows: source[h, pl.ds(base, rows), :], storer(target),
             lambda o, c, k: w_first[c, o], None, 1, CH, H, 0, 2 * L, R_FIRST, span(0, X),
             unroll=U_FIRST, relu=False)

    receive(E_RES)
    unpack(rT, 0, zr0.at[1])
    first_conv(rT, d0)
    b_send[0] = reduce_end(copies, a_send.at[0], a_recv.at[0])
    copies = reduce_start(n_chip, b_send.at[0], b_recv.at[0], bsend_sem.at[0], brecv_sem.at[0], peer_b)
    pending += copies
    receive(E_IMG)
    unpack(iT, 0, zr0.at[2])
    first_conv(iT, z0)
    total = reduce_end(copies, b_send.at[0], b_recv.at[0])
    full = jnp.broadcast_to(jnp.sum(total, axis=1, keepdims=True), (8, L))
    curvature = full[0:1]
    alpha = full[1:2] / curvature
    mixed = total[2:3] - 2.0 * alpha * total[3:4] + alpha * alpha * total[4:5]
    squares = jnp.maximum(jnp.broadcast_to(jnp.sum(mixed, axis=1, keepdims=True), (1, L)), 0.0)
    cells = float(X * n_slab) * float(2 * L) * float(Z * n_col)
    scale = jnp.sqrt(squares / cells + 1e-06)
    sc[0:1] = alpha
    sc[1:2] = 1.0 / scale
    sc[4:5] = alpha / scale
    sc[2:3] = scale
    sc[3:4] = curvature
    coef_out[0:1] = alpha

    def lin0(x_from, x_to):
        inner_conv(5, d0, z0, H, 0, 2 * L, R_RISE, span(x_from, x_to), unroll=U_RISE, relu=False)

    def image_turn(i, carry):
        x, h = i // H, lax.rem(i, H)
        block = iT[h, pl.ds(pl.multiple_of((x + 1) * Zp[0] + PAD, 8), Z), :]
        image_out[x, pl.ds(pl.multiple_of(h * L, L), L), :] = block.T
        return carry

    def pre_body(i, carry):
        per = Z // RI
        base = pl.multiple_of((i // per + 1) * Zp[0] + PAD + lax.rem(i, per) * RI, 8)
        for h in range(H):
            at = (h, pl.ds(base, RI), slice(None))
            image = iT[at]
            value = (rT[at] - sc[0:1] * image) / (6.0 + gT[at])
            pre[at] = value
            carry = carry + fold(value * image)
        return carry

    def transposed_last():
        flip = (0, 2, 1, 4, 3, 6, 5)
        conv(lambda k, h, base, rows: iT[h, pl.ds(base, rows), :], storer(gl),
             lambda o, c, k: w_last[c, flip[o]], None, 1, CH, H, 0, 2 * L, R_FIRST, span(0, X),
             unroll=U_FIRST, relu=False)

    def down_zero(c, h, at):
        return jnp.maximum(d0[c, h, at, :] * sc[1:2] - z0[c, h, at, :] * sc[4:5] + w_bias[c, 0], 0.0)

    for side, row in ((0, 0), (1, Z - 1)):
        for c in range(CH):
            for h in range(H):
                zsd[side, pl.ds((c * H + h) * X, X), :] = down_zero(
                    c, h, pl.ds(Zp[0] + PAD + row, X, stride=Zp[0]))
    send(E_D0, (2, 3))
    pool(d0, p1, 0, H, down_zero, ends(Xl[1]))
    send(E_P1, (0, 1))
    pool(d0, p1, 0, H, down_zero, span(1, Xl[1] - 1))
    pack(p1, 1, zs1.at[0])
    send(E_P1, (2, 3))
    send(E_D0, (0, 1))
    transposed_last()
    receive(E_D0, (2, 3))
    unpack(d0, 0, zrd)
    lin0(1, 2)
    receive(E_P1, (2, 3))
    unpack(p1, 1, zr1.at[0])
    inner_conv(0, p1, d1, 1, 1, L, min(32, Zl[1]), span(1, Xl[1] - 1), unroll=2)
    receive(E_P1, (0, 1))
    inner_conv(0, p1, d1, 1, 1, L, min(32, Zl[1]), ends(Xl[1]), unroll=2)
    pool(d1, p2, 1, 1)
    pack(p2, 2, zs2.at[0])
    send(E_P2)
    pack(d1, 1, zs1.at[1])
    send(E_D1)
    lin0(2, 4)
    receive(E_P2)
    unpack(p2, 2, zr2.at[0])
    inner_conv(1, p2, d2, 1, 2, L // 2, min(32, Zl[2]))
    pool(d2, p3, 2, 1)
    pack(p3, 3, zs3.at[0])
    send(E_P3)
    pack(d2, 2, zs2.at[1])
    send(E_D2)
    lin0(4, 5)
    lax.fori_loop(0, X * H // 2, image_turn, 0, unroll=4)
    receive(E_P3)
    unpack(p3, 3, zr3.at[0])
    inner_conv(2, p3, d3, 1, 3, L // 4, min(16, Zl[3]))
    pack(d3, 3, zs3.at[1])
    send(E_R3)
    receive(E_D2)
    unpack(d2, 2, zr2.at[1])
    inner_conv(3, d2, r2, 1, 2, L // 2, min(32, Zl[2]), relu=False)
    receive(E_D1)
    unpack(d1, 1, zr1.at[1])
    inner_conv(4, d1, r1, 1, 1, L, min(32, Zl[1]), relu=False)
    lin0(5, 6)
    receive(E_R3)
    unpack(d3, 3, zr3.at[1])
    up_conv(3, d3, r2, 2, 1)
    pack(r2, 2, zs2.at[2])
    send(E_R2)
    lax.fori_loop(X * H // 2, X * H, image_turn, 0, unroll=4)
    image_copy = pltpu.make_async_copy(image_out, image_hbm, io_sem.at[3])
    image_copy.start()
    lin0(6, 7)
    receive(E_D0, (0, 1))
    lin0(0, 1)
    receive(E_R2)
    unpack(r2, 2, zr2.at[2])
    up_conv(4, r2, r1, 1, 1)
    pack(r1, 1, zs1.at[2])
    send(E_R1)
    lin0(X - 1, X)
    over = lax.fori_loop(0, X * (Z // RI), pre_body, jnp.zeros((8, L), F32), unroll=2)
    receive(E_R1, (2, 3))
    unpack(r1, 1, zr1.at[2])
    over = over + sc[2:3] * up_conv(5, r1, z0, 0, H, U_UP, gl, span(1, Xl[1] - 1))
    receive(E_R1, (0, 1))
    over = over + sc[2:3] * up_conv(5, r1, z0, 0, H, U_UP, gl, ends(Xl[1]))
    a_send[1] = over
    copies = reduce_start(n_a, a_send.at[1], a_recv.at[1], asend_sem.at[1], arecv_sem.at[1], peer_a)
    pending += copies
    def last_w(o, k):
        return w_last[k, o]

    for side, plane, o in ((0, 1, 2), (1, X, 1)):
        def part_body(i, carry, side=side, plane=plane, o=o):
            base = pl.multiple_of(i * 32, 8)
            for h in range(H):
                total = None
                for k in range(CH):
                    term = last_w(o, k) * z0[k, h, pl.ds(plane * Zp[0] + PAD + base, 32), :]
                    total = term if total is None else total + term
                xs_m[side, h, pl.ds(base, 32), :] = total
            return carry
        lax.fori_loop(0, Z // 32, part_body, 0)
    for side, at, o in ((0, 0, 6), (1, Z - 1, 5)):
        for h in range(H):
            total = None
            for k in range(CH):
                term = last_w(o, k) * z0[k, h, pl.ds(Zp[0] + PAD + at, X, stride=Zp[0]), :]
                total = term if total is None else total + term
            zs_m[side, pl.ds(h * X, X), :] = total
    send(E_NET)

    def put_net(c, h, base, rows, value):
        net[h, pl.ds(base, rows), :] = value

    conv(loader(z0), put_net, lambda o, c, k: last_w(o, k), None,
          CH, 1, H, 0, 2 * L, 32, span(0, X), unroll=U_LAST, relu=False)
    b_send[1] = reduce_end(copies, a_send.at[1], a_recv.at[1])
    copies = reduce_start(n_chip, b_send.at[1], b_recv.at[1], bsend_sem.at[1], brecv_sem.at[1], peer_b)
    pending += copies
    receive(E_NET)
    for side, plane in ((0, 1), (1, X)):
        for h in range(H):
            at = (h, pl.ds(plane * Zp[0] + PAD, Z), slice(None))
            net[at] = net[at] + xr_m[side, h]
    for side, row in ((0, 0), (1, Z - 1)):
        for h in range(H):
            at = (h, pl.ds(Zp[0] + PAD + row, X, stride=Zp[0]), slice(None))
            net[at] = net[at] + zr_m[side, pl.ds(h * X, X), :]

    def turn_pre(i, carry):
        x, h = i // H, lax.rem(i, H)
        at = (h, pl.ds(pl.multiple_of((x + 1) * Zp[0] + PAD, 8), Z), slice(None))
        block = pre[at] + sc[2:3] * net[at]
        pre_out[x, pl.ds(pl.multiple_of(h * L, L), L), :] = block.T
        return carry

    lax.fori_loop(0, X * H, turn_pre, 0, unroll=4)
    pre_copy = pltpu.make_async_copy(pre_out, pre_hbm, io_sem.at[4])
    pre_copy.start()
    total = reduce_end(copies, b_send.at[1], b_recv.at[1])
    total = jnp.sum(jnp.sum(total, axis=0, keepdims=True), axis=1, keepdims=True)
    coef_out[1:2] = jnp.broadcast_to(total, (1, L)) / sc[3:4]
    coef_out[2:8] = jnp.zeros((6, L), F32)

    image_copy.wait()
    pre_copy.wait()
    for copy in pending:
        copy.wait_send()
    for e in range(N_EX):
        sent(e)


def on_device(residual, direction, diagonal, first_weight, conv_weights, last_weight, biases):
    X, Y, Z = residual.shape
    n_slab, n_col = lax.axis_size("slab"), lax.axis_size("col")
    H = Y // L
    Zl = [Z // 2**l for l in range(4)]
    Xl = [X // 2**l for l in range(4)]
    rows = [(Xl[l] + 2) * (Zl[l] + 2 * PAD) for l in range(4)]
    field = pltpu.VMEM((X, Y, Z), F32)
    one = pltpu.VMEM((H, rows[0], L), F32)
    four = pltpu.VMEM((CH, H, rows[0], L), F32)

    def level(l):
        return pltpu.VMEM((CH, rows[l], L), F32)

    def edge(*lead):
        return pltpu.VMEM((*lead, L), F32)

    def edge_rows(l):
        return max(8, CH * Xl[l])

    n_a, n_b = 2 * n_col, n_slab // 2
    scratch = [
        field, field, field, field, field, four, one, one, one, one, four, four, one, one,
        level(1), level(1), level(1), level(2), level(2), level(2), level(3), level(3),
        edge(3, 2, H * X), edge(3, 2, H * X), edge(2, CH * H * X), edge(2, CH * H * X),
        edge(3, 2, edge_rows(1)), edge(3, 2, edge_rows(1)),
        edge(3, 2, edge_rows(2)), edge(3, 2, edge_rows(2)),
        edge(2, 2, edge_rows(3)), edge(2, 2, edge_rows(3)),
        edge(2, H, Z), edge(2, H, Z), edge(2, H * X), edge(2, H * X),
        pltpu.VMEM((2 * L, L), BF16), edge(4, Z), pltpu.VMEM((2 * L, 2 * L), BF16),
        pltpu.VMEM((3, 2 * L, 2 * L), BF16), edge(8),
        edge(2, 8), edge(2, n_a - 1, 8), edge(2, 8), edge(2, n_b - 1, 8),
        pltpu.SemaphoreType.DMA((5,)),
        pltpu.SemaphoreType.DMA((N_EX, 4)), pltpu.SemaphoreType.DMA((N_EX, 4)),
        pltpu.SemaphoreType.DMA((2, n_a - 1)), pltpu.SemaphoreType.DMA((2, n_a - 1)),
        pltpu.SemaphoreType.DMA((2, n_b - 1)), pltpu.SemaphoreType.DMA((2, n_b - 1)),
    ]
    vmem = pl.BlockSpec(memory_space=pltpu.VMEM)
    anywhere = pl.BlockSpec(memory_space=pl.ANY)
    image, pre, coef = pl.pallas_call(
        functools.partial(kernel, n_slab, n_col, X, Z),
        out_shape=(jax.ShapeDtypeStruct((X, Y, Z), F32),) * 2 + (jax.ShapeDtypeStruct((8, L), F32),),
        in_specs=[pl.BlockSpec(memory_space=pltpu.SMEM)] * 4 + [anywhere] * 3,
        out_specs=(anywhere, anywhere, vmem),
        scratch_shapes=scratch,
        compiler_params=pltpu.CompilerParams(
            collective_id=0, has_side_effects=True, vmem_limit_bytes=56 * 2**20),
    )(first_weight.T, conv_weights.transpose(0, 2, 3, 1), last_weight.T, biases.T,
      residual, direction, diagonal)
    steps = 4
    block = pl.BlockSpec((X // steps, Y, Z), lambda i: (i, 0, 0))
    return pl.pallas_call(
        finish,
        grid=(steps,),
        out_shape=(jax.ShapeDtypeStruct((X, Y, Z), F32),) * 2,
        in_specs=[pl.BlockSpec((8, L), lambda i: (0, 0))] + [block] * 4,
        out_specs=(block, block),
        compiler_params=pltpu.CompilerParams(vmem_limit_bytes=16 * 2**20),
    )(coef, residual, direction, image, pre)


def solution(mesh):
    in_specs = (P("slab", None, "col"),) * 3 + (P(),) * 4
    return jax.shard_map(
        on_device, mesh=mesh, in_specs=in_specs,
        out_specs=(P("slab", None, "col"),) * 2, check_vma=False,
    )
```

```python
import functools

import jax
import jax.numpy as jnp
from jax import lax
from jax.experimental import pallas as pl
from jax.experimental.pallas import tpu as pltpu
from jax.sharding import PartitionSpec as P

MESH = pl.DeviceIdType.MESH
L = 128
PAD = 8
CH = 4
F32 = jnp.float32
BF16 = jnp.bfloat16

(E_DIR, E_RES, E_IMG, E_P1, E_D0, E_P2, E_D1, E_P3, E_D2, E_R3, E_R2, E_R1, E_NET) = range(13)
N_EX = 13


def split2(value):
    high = value.astype(BF16)
    low = (value - high.astype(F32)).astype(BF16)
    return high, low


def span(start, stop):
    return stop - start, lambda j: j + start


def ends(count):
    return 2, lambda j: j * (count - 1)


def finish(coef, res, direction, image, pre, res_out, dir_out):
    Z = res.shape[2]
    res_out[...] = res[...] - coef[0:1, :Z] * image[...]
    dir_out[...] = pre[...] - coef[1:2, :Z] * direction[...]


def kernel(n_slab, n_col, X, Z, *refs):
    (w_first, w_conv, w_last, w_bias, res_hbm, dir_hbm, diag_hbm, image_hbm, pre_hbm, coef_out,
     res_in, dir_in, diag_in, image_out, pre_out, gl, dT, rT, iT, gT, d0, z0, net, pre,
     p1, d1, r1, p2, d2, r2, p3, d3,
     zs0, zr0, zsd, zrd, zs1, zr1, zs2, zr2, zs3, zr3, xs_m, xr_m, zs_m, zr_m,
     pool_m, pool_s, up_m, beside_m, sc, a_send, a_recv, b_send, b_recv,
     io_sem, send_sem, recv_sem, asend_sem, arecv_sem, bsend_sem, brecv_sem) = refs
    H = 2
    U_FIRST, R_FIRST, U_LAST, R_RISE, U_RISE, U_UP = 4, 16, 4, 32, 1, 2
    slab = lax.axis_index("slab")
    col = lax.axis_index("col")
    core = lax.rem(slab, 2)
    chip = slab // 2
    n_chip = n_slab // 2
    n_a = 2 * n_col
    Zp = [Z // 2**l + 2 * PAD for l in range(4)]
    Zl = [Z // 2**l for l in range(4)]
    Xl = [X // 2**l for l in range(4)]
    has = (slab > 0, slab < n_slab - 1, col > 0, col < n_col - 1)
    targets = (
        (jnp.maximum(slab - 1, 0), col),
        (jnp.minimum(slab + 1, n_slab - 1), col),
        (slab, jnp.maximum(col - 1, 0)),
        (slab, jnp.minimum(col + 1, n_col - 1)),
    )
    opposite = (1, 0, 3, 2)

    def x_views(ref, level):
        rows, pitch, count = Zl[level], Zp[level], Xl[level]
        if len(ref.shape) == 3:
            def view(plane):
                return ref.at[:, pl.ds(plane * pitch + PAD, rows), :]
        else:
            def view(plane):
                return ref.at[:, :, pl.ds(plane * pitch + PAD, rows), :]
        return (view(1), view(count)), (view(0), view(count + 1))

    def x_views4(ref, level):
        return x_views(ref, level)

    exchanges = {}

    def define(e, x_src, x_dst, z_src, z_dst):
        msgs = []
        for side in range(4):
            if side < 2:
                src, dst = x_src[side], x_dst[opposite[side]]
            else:
                src, dst = z_src.at[side - 2], z_dst.at[opposite[side] - 2]
            msgs.append(pltpu.make_async_remote_copy(
                src_ref=src, dst_ref=dst,
                send_sem=send_sem.at[e, side],
                recv_sem=recv_sem.at[e, opposite[side]],
                device_id=targets[side], device_id_type=MESH))
        exchanges[e] = msgs

    def send(e, sides=(0, 1, 2, 3)):
        for side in sides:
            @pl.when(has[side])
            def _(side=side):
                exchanges[e][side].start()

    def receive(e, sides=(0, 1, 2, 3)):
        for side in sides:
            @pl.when(has[side])
            def _(side=side):
                exchanges[e][opposite[side]].wait_recv()

    def sent(e):
        for side in range(4):
            @pl.when(has[side])
            def _(side=side):
                exchanges[e][side].wait_send()

    for e, ref, level, zs, zr in (
        (E_DIR, dT, 0, zs0.at[0], zr0.at[0]),
        (E_RES, rT, 0, zs0.at[1], zr0.at[1]),
        (E_IMG, iT, 0, zs0.at[2], zr0.at[2]),
        (E_P1, p1, 1, zs1.at[0], zr1.at[0]),
        (E_D0, d0, 0, zsd, zrd),
        (E_P2, p2, 2, zs2.at[0], zr2.at[0]),
        (E_P3, p3, 3, zs3.at[0], zr3.at[0]),
        (E_D1, d1, 1, zs1.at[1], zr1.at[1]),
        (E_D2, d2, 2, zs2.at[1], zr2.at[1]),
        (E_R3, d3, 3, zs3.at[1], zr3.at[1]),
        (E_R2, r2, 2, zs2.at[2], zr2.at[2]),
        (E_R1, r1, 1, zs1.at[2], zr1.at[2]),
    ):
        src, dst = x_views(ref, level)
        define(e, src, dst, zs, zr)
    define(E_NET, (xs_m.at[0], xs_m.at[1]), (xr_m.at[0], xr_m.at[1]), zs_m, zr_m)

    def groups(ref):
        if len(ref.shape) == 3:
            return [(i,) for i in range(ref.shape[0])]
        return [(c, h) for c in range(ref.shape[0]) for h in range(ref.shape[1])]

    def rows_at(start, count, stride):
        return pl.ds(start, count, stride=stride) if count > 1 else pl.ds(start, 1)

    def pack(ref, level, zs):
        pitch, count = Zp[level], Xl[level]
        for side, row in ((0, 0), (1, Zl[level] - 1)):
            for g, index in enumerate(groups(ref)):
                zs[side, pl.ds(g * count, count), :] = ref[
                    (*index, rows_at(pitch + PAD + row, count, pitch), slice(None))]

    def unpack(ref, level, zr):
        pitch, count = Zp[level], Xl[level]
        for side, row in ((0, -1), (1, Zl[level])):
            for g, index in enumerate(groups(ref)):
                ref[(*index, rows_at(pitch + PAD + row, count, pitch), slice(None))] = zr[
                    side, pl.ds(g * count, count), :]

    loads = [pltpu.make_async_copy(source, target, io_sem.at[n]) for n, (source, target) in
             enumerate(((dir_hbm, dir_in), (res_hbm, res_in), (diag_hbm, diag_in)))]
    for load in loads:
        load.start()

    for side in (0, 1):
        @pl.when(jnp.logical_not(has[side]))
        def _(side=side):
            for ref, level in ((dT, 0), (rT, 0), (iT, 0), (p1, 1), (p2, 2), (p3, 3),
                               (d1, 1), (d2, 2), (d3, 3), (r2, 2), (r1, 1)):
                plane = 0 if side == 0 else Xl[level] + 1
                for index in groups(ref):
                    ref[(*index, pl.ds(plane * Zp[level] + PAD, Zl[level]), slice(None))] = (
                        jnp.zeros((Zl[level], L), F32))
            plane = 0 if side == 0 else X + 1
            for c in range(CH):
                for h in range(H):
                    d0[c, h, pl.ds(plane * Zp[0] + PAD, Z), :] = jnp.zeros((Z, L), F32)
            for h in range(H):
                xr_m[side, h] = jnp.zeros((Z, L), F32)
    for side in (2, 3):
        @pl.when(jnp.logical_not(has[side]))
        def _(side=side):
            s = side - 2
            for ref in (zr0, zr1, zr2, zr3):
                for i in range(ref.shape[0]):
                    ref[i, s] = jnp.zeros(ref.shape[2:], F32)
            zrd[s] = jnp.zeros(zrd.shape[1:], F32)
            zr_m[s] = jnp.zeros(zr_m.shape[1:], F32)

    rank_a = col * 2 + core

    def peer_a(j):
        rank = lax.rem(rank_a + j, n_a)
        return (chip * 2 + lax.rem(rank, 2), rank // 2)

    def peer_b(j):
        return (lax.rem(chip + j, n_chip) * 2 + core, col)

    barrier = pltpu.get_barrier_semaphore()
    for j in range(1, n_a):
        pl.semaphore_signal(barrier, inc=1, device_id=peer_a(j), device_id_type=MESH)
    for j in range(1, n_chip):
        pl.semaphore_signal(barrier, inc=1, device_id=peer_b(j), device_id_type=MESH)
    for side in (0, 1):
        @pl.when(has[side])
        def _(side=side):
            pl.semaphore_signal(barrier, inc=1, device_id=targets[side], device_id_type=MESH)

    def turn_in(source, target):
        def body(i, carry):
            x, h = i // H, lax.rem(i, H)
            block = source[x, pl.ds(pl.multiple_of(h * L, L), L), :]
            target[h, pl.ds(pl.multiple_of((x + 1) * Zp[0] + PAD, 8), Z), :] = block.T
            return carry
        lax.fori_loop(0, X * H, body, 0, unroll=4)

    loads[0].wait()
    turn_in(dir_in, dT)
    pack(dT, 0, zs0.at[0])
    n_wait = (n_a - 1) + (n_chip - 1) + jnp.where(slab > 0, 1, 0) + jnp.where(slab < n_slab - 1, 1, 0)
    pl.semaphore_wait(barrier, n_wait)
    send(E_DIR)
    loads[1].wait()
    turn_in(res_in, rT)
    pack(rT, 0, zs0.at[1])
    send(E_RES)
    loads[2].wait()
    turn_in(diag_in, gT)

    def beside_y(center, ny):
        rows = center[0].shape[0]
        lane = lax.broadcasted_iota(jnp.int32, (rows, L), 1)
        count = len(center)
        last = L - 1 if count > 1 else ny - 1
        up = [pltpu.roll(v, 1, 1) for v in center]
        down = [pltpu.roll(v, L - 1, 1) for v in center]
        zero = jnp.zeros((rows, L), F32)
        minus = [jnp.where(lane == 0, up[h - 1] if h > 0 else zero, up[h]) for h in range(count)]
        plus = [jnp.where(lane == last, down[h + 1] if h < count - 1 else zero, down[h])
                for h in range(count)]
        return minus, plus

    def fold(value):
        return jnp.sum(value.reshape(value.shape[0] // 8, 8, L), axis=0)

    RI = 32

    def image_body(i, carry, place):
        per = Z // RI
        base = pl.multiple_of((place(i // per) + 1) * Zp[0] + PAD + lax.rem(i, per) * RI, 8)
        center = [dT[h, pl.ds(base, RI), :] for h in range(H)]
        minus, plus = beside_y(center, 2 * L)
        sums = list(carry)
        for h in range(H):
            beside = dT[h, pl.ds(base + Zp[0], RI), :] + dT[h, pl.ds(base - Zp[0], RI), :]
            beside = beside + plus[h] + minus[h]
            beside = beside + dT[h, pl.ds(base + 1, RI), :] + dT[h, pl.ds(base - 1, RI), :]
            image = (6.0 + gT[h, pl.ds(base, RI), :]) * center[h] - beside
            iT[h, pl.ds(base, RI), :] = image
            r = rT[h, pl.ds(base, RI), :]
            for q, term in enumerate((center[h] * image, r * center[h], r * r, r * image,
                                      image * image)):
                sums[q] = sums[q] + fold(term)
        return tuple(sums)

    sums = tuple(jnp.zeros((8, L), F32) for _ in range(5))
    receive(E_DIR, (2, 3))
    unpack(dT, 0, zr0.at[0])
    for sides, (count, place) in ((None, span(1, X - 1)), ((0, 1), ends(X))):
        if sides is not None:
            receive(E_DIR, sides)
        sums = lax.fori_loop(0, count * (Z // RI), functools.partial(image_body, place=place),
                             sums, unroll=2)

    def reduce_start(n, send_ref, recv_ref, ssem, rsem, peer):
        copies = []
        for j in range(1, n):
            copy = pltpu.make_async_remote_copy(
                src_ref=send_ref, dst_ref=recv_ref.at[j - 1], send_sem=ssem.at[j - 1],
                recv_sem=rsem.at[j - 1], device_id=peer(j), device_id_type=MESH)
            copy.start()
            copies.append(copy)
        return copies

    def reduce_end(copies, send_ref, recv_ref):
        total = send_ref[...]
        for j, copy in enumerate(copies):
            copy.wait_recv()
        for j in range(len(copies)):
            total = total + recv_ref[j]
        return total

    pending = []
    a_send[0] = jnp.zeros((8, L), F32)
    for q in range(5):
        a_send[0, q:q + 1, :] = jnp.sum(sums[q], axis=0, keepdims=True)
    copies = reduce_start(n_a, a_send.at[0], a_recv.at[0], asend_sem.at[0], arecv_sem.at[0], peer_a)
    pending += copies
    send(E_IMG, (0, 1))
    pack(iT, 0, zs0.at[2])
    send(E_IMG, (2, 3))
    row = lax.broadcasted_iota(jnp.int32, (2 * L, L), 0)
    lane = lax.broadcasted_iota(jnp.int32, (2 * L, L), 1)
    pool_m[...] = jnp.where(row // 2 == lane, 0.125, 0.0).astype(BF16)
    row = lax.broadcasted_iota(jnp.int32, (2 * L, 2 * L), 0)
    lane = lax.broadcasted_iota(jnp.int32, (2 * L, 2 * L), 1)
    source = lax.rem(row, L)
    up_m[...] = jnp.where(lane // 2 == source, 1.0, 0.0).astype(BF16)
    for l in range(3):
        match = jnp.where(row < L, (lane + 1) // 2 - 1, (lane + 1) // 2)
        match = jnp.where(source < L // 2**l, match, -1)
        beside_m[l] = jnp.where(match == source, 1.0, 0.0).astype(BF16)
    for c in range(CH):
        for h in range(H):
            for plane in (0, X + 1):
                z0[c, h, pl.ds(plane * Zp[0] + PAD, Z), :] = jnp.zeros((Z, L), F32)
            for at in (PAD - 1, PAD + Z):
                z0[c, h, pl.ds(Zp[0] + at, X, stride=Zp[0]), :] = jnp.zeros((X, L), F32)

    def conv(load, store, weight, bias, n_in, n_out, count_h, level, ny, rows, planes, unroll=1, relu=True):
        per = Zl[level] // rows
        pitch = Zp[level]

        def body(i, carry):
            base = pl.multiple_of((planes[1](i // per) + 1) * pitch + PAD + lax.rem(i, per) * rows, 8)
            acc = [[None] * count_h for _ in range(n_out)]
            for k in range(n_in):
                center = [load(k, h, base, rows) for h in range(count_h)]
                minus, plus = beside_y(center, ny)
                for o in range(7):
                    for h in range(count_h):
                        tap = (center[h] if o == 0 else
                               load(k, h, base - pitch, rows) if o == 1 else
                               load(k, h, base + pitch, rows) if o == 2 else
                               minus[h] if o == 3 else plus[h] if o == 4 else
                               load(k, h, base - 1, rows) if o == 5 else
                               load(k, h, base + 1, rows))
                        for c in range(n_out):
                            term = weight(o, c, k) * tap
                            acc[c][h] = term if acc[c][h] is None else acc[c][h] + term
            for c in range(n_out):
                for h in range(count_h):
                    value = acc[c][h]
                    if bias is not None:
                        value = value + bias(c)
                    if relu:
                        value = jnp.maximum(value, 0.0)
                    store(c, h, base, rows, value)
            return carry
        lax.fori_loop(0, planes[0] * per, body, 0, unroll=unroll)

    def loader(ref):
        if len(ref.shape) == 3:
            return lambda k, h, base, rows: ref[k, pl.ds(base, rows), :]
        return lambda k, h, base, rows: ref[k, h, pl.ds(base, rows), :]

    def storer(ref):
        def put(c, h, base, rows, value):
            if len(ref.shape) == 3:
                ref[c, pl.ds(base, rows), :] = value
            else:
                ref[c, h, pl.ds(base, rows), :] = value
        return put

    def inner_conv(which, source, target, count_h, level, ny, rows, planes=None, unroll=1, relu=True):
        conv(loader(source), storer(target),
             lambda o, c, k: w_conv[which, c, k, o],
             lambda c: w_bias[c, which + 1],
             CH, CH, count_h, level, ny, rows, span(0, Xl[level]) if planes is None else planes, unroll, relu)

    def pool(source, target, level, count_h, active=None, planes=None):
        Z0, Z1 = Zl[level], Zl[level + 1]
        count, place = span(0, Xl[level + 1]) if planes is None else planes

        def body(i, carry):
            c, x1 = i // count, place(lax.rem(i, count))
            slot = lax.rem(i, 8)
            parts = []
            for h in range(count_h):
                total = None
                for dx in range(2):
                    at = pl.ds(pl.multiple_of((2 * x1 + dx + 1) * Zp[level] + PAD, 8), Z0)
                    if active is not None:
                        v = active(c, h, at)
                        source[c, h, at, :] = v
                    else:
                        v = source[c, h, at, :] if count_h > 1 else source[c, at, :]
                    total = v if total is None else total + v
                parts.append(total)
            value = jnp.concatenate(parts, axis=1) if count_h > 1 else parts[0]
            high, low = split2(value)
            m = pool_m[0:count_h * L, :]
            out = jnp.dot(high, m, preferred_element_type=F32) + jnp.dot(low, m, preferred_element_type=F32)
            pool_s[slot, 0:Z0, :] = out
            target[c, pl.ds(pl.multiple_of((x1 + 1) * Zp[level + 1] + PAD, 8), Z1), :] = (
                pool_s[slot, pl.ds(0, Z1, stride=2), :] + pool_s[slot, pl.ds(1, Z1, stride=2), :])
            return carry
        lax.fori_loop(0, CH * count, body, 0, unroll=8 if active is not None else 4)

    def up_conv(which, source, target, level, count_h, unroll=1, other=None, planes=None):
        Z1, X1 = Zl[level + 1], Xl[level + 1]
        pitch, fine = Zp[level + 1], Zp[level]
        rows = min(32, Z1)
        per = Z1 // rows
        count, place = span(0, X1) if planes is None else planes

        def body(i, carry):
            x1, r1 = place(i // per), lax.rem(i, per) * rows
            base = pl.multiple_of((x1 + 1) * pitch + PAD + r1, 8)
            flat, sides = [], []
            for c in range(CH):
                total = [None] * 7

                def add(place, term):
                    total[place] = term if total[place] is None else total[place] + term

                for k in range(CH):
                    wt = [w_conv[which, c, k, o] for o in range(7)]
                    here = source[k, pl.ds(base, rows), :]
                    x_low, x_high = wt[1] * here, wt[2] * here
                    z_low, z_high = wt[5] * here, wt[6] * here
                    add(0, wt[0] * here)
                    add(1, x_high)
                    add(1, wt[1] * source[k, pl.ds(base - pitch, rows), :])
                    add(2, x_low)
                    add(2, wt[2] * source[k, pl.ds(base + pitch, rows), :])
                    add(3, z_high)
                    add(3, wt[5] * source[k, pl.ds(base - 1, rows), :])
                    add(4, z_low)
                    add(4, wt[6] * source[k, pl.ds(base + 1, rows), :])
                    add(5, wt[3] * here)
                    add(6, wt[4] * here)
                for dx in range(2):
                    part = total[0] + total[1 + dx]
                    for dz in range(2):
                        flat.append(jnp.concatenate(split2(part + total[3 + dz]), axis=1))
                low, high = split2(total[5]), split2(total[6])
                sides.append([jnp.concatenate([low[n], high[n]], axis=1) for n in range(2)])
            flat = jnp.concatenate(flat, axis=0)
            flat = jnp.dot(flat, up_m[:, 0:count_h * L], preferred_element_type=F32)
            sides = jnp.concatenate([v[0] for v in sides] + [v[1] for v in sides], axis=0)
            sides = jnp.dot(sides, beside_m[level, :, 0:count_h * L], preferred_element_type=F32)
            for c in range(CH):
                side = sides[c * rows:(c + 1) * rows] + sides[(CH + c) * rows:(CH + c + 1) * rows]
                for dx in range(2):
                    for dz in range(2):
                        n = (c * 2 + dx) * 2 + dz
                        value = flat[n * rows:(n + 1) * rows] + side
                        at_rows = pl.ds((2 * x1 + dx + 1) * fine + PAD + 2 * r1 + dz, rows, stride=2)
                        for h in range(count_h):
                            at = (c, h, at_rows, slice(None)) if count_h > 1 else (c, at_rows, slice(None))
                            out = jnp.maximum(target[at] + value[:, h * L:(h + 1) * L], 0.0)
                            target[at] = out
                            if other is not None:
                                carry = carry + fold(out * other[at])
            return carry
        return lax.fori_loop(0, count * per, body, jnp.zeros((8, L), F32), unroll=unroll)

    def first_conv(source, target):
        conv(lambda k, h, base, rows: source[h, pl.ds(base, rows), :], storer(target),
             lambda o, c, k: w_first[c, o], None, 1, CH, H, 0, 2 * L, R_FIRST, span(0, X),
             unroll=U_FIRST, relu=False)

    receive(E_RES)
    unpack(rT, 0, zr0.at[1])
    first_conv(rT, d0)
    b_send[0] = reduce_end(copies, a_send.at[0], a_recv.at[0])
    copies = reduce_start(n_chip, b_send.at[0], b_recv.at[0], bsend_sem.at[0], brecv_sem.at[0], peer_b)
    pending += copies
    receive(E_IMG)
    unpack(iT, 0, zr0.at[2])
    def transposed_last():
        flip = (0, 2, 1, 4, 3, 6, 5)
        conv(lambda k, h, base, rows: iT[h, pl.ds(base, rows), :], storer(gl),
             lambda o, c, k: w_last[c, flip[o]], None, 1, CH, H, 0, 2 * L, R_FIRST, span(0, X),
             unroll=U_FIRST, relu=False)

    first_conv(iT, z0)
    transposed_last()
    total = reduce_end(copies, b_send.at[0], b_recv.at[0])
    full = jnp.broadcast_to(jnp.sum(total, axis=1, keepdims=True), (8, L))
    curvature = full[0:1]
    alpha = full[1:2] / curvature
    mixed = total[2:3] - 2.0 * alpha * total[3:4] + alpha * alpha * total[4:5]
    squares = jnp.maximum(jnp.broadcast_to(jnp.sum(mixed, axis=1, keepdims=True), (1, L)), 0.0)
    cells = float(X * n_slab) * float(2 * L) * float(Z * n_col)
    scale = jnp.sqrt(squares / cells + 1e-06)
    sc[0:1] = alpha
    sc[1:2] = 1.0 / scale
    sc[4:5] = alpha / scale
    sc[2:3] = scale
    sc[3:4] = curvature
    coef_out[0:1] = alpha

    def lin0(x_from, x_to):
        inner_conv(5, d0, z0, H, 0, 2 * L, R_RISE, span(x_from, x_to), unroll=U_RISE, relu=False)

    def image_turn(i, carry):
        x, h = i // H, lax.rem(i, H)
        block = iT[h, pl.ds(pl.multiple_of((x + 1) * Zp[0] + PAD, 8), Z), :]
        image_out[x, pl.ds(pl.multiple_of(h * L, L), L), :] = block.T
        return carry

    def pre_body(i, carry):
        per = Z // RI
        base = pl.multiple_of((i // per + 1) * Zp[0] + PAD + lax.rem(i, per) * RI, 8)
        for h in range(H):
            at = (h, pl.ds(base, RI), slice(None))
            image = iT[at]
            value = (rT[at] - sc[0:1] * image) / (6.0 + gT[at])
            pre[at] = value
            carry = carry + fold(value * image)
        return carry

    def down_zero(c, h, at):
        return jnp.maximum(d0[c, h, at, :] * sc[1:2] - z0[c, h, at, :] * sc[4:5] + w_bias[c, 0], 0.0)

    for side, row in ((0, 0), (1, Z - 1)):
        for c in range(CH):
            for h in range(H):
                zsd[side, pl.ds((c * H + h) * X, X), :] = down_zero(
                    c, h, pl.ds(Zp[0] + PAD + row, X, stride=Zp[0]))
    send(E_D0, (2, 3))
    pool(d0, p1, 0, H, down_zero, ends(Xl[1]))
    send(E_P1, (0, 1))
    pool(d0, p1, 0, H, down_zero, span(1, Xl[1] - 1))
    pack(p1, 1, zs1.at[0])
    send(E_P1, (2, 3))
    send(E_D0, (0, 1))
    receive(E_D0, (2, 3))
    unpack(d0, 0, zrd)
    lin0(1, 3)
    receive(E_P1, (2, 3))
    unpack(p1, 1, zr1.at[0])
    inner_conv(0, p1, d1, 1, 1, L, min(32, Zl[1]), span(1, Xl[1] - 1), unroll=2)
    receive(E_P1, (0, 1))
    inner_conv(0, p1, d1, 1, 1, L, min(32, Zl[1]), ends(Xl[1]), unroll=2)
    pool(d1, p2, 1, 1)
    send(E_P2, (0, 1))
    pack(p2, 2, zs2.at[0])
    send(E_P2, (2, 3))
    send(E_D1, (0, 1))
    pack(d1, 1, zs1.at[1])
    send(E_D1, (2, 3))
    lin0(3, 5)
    receive(E_P2)
    unpack(p2, 2, zr2.at[0])
    inner_conv(1, p2, d2, 1, 2, L // 2, min(32, Zl[2]))
    pool(d2, p3, 2, 1)
    send(E_P3, (0, 1))
    pack(p3, 3, zs3.at[0])
    send(E_P3, (2, 3))
    send(E_D2, (0, 1))
    pack(d2, 2, zs2.at[1])
    send(E_D2, (2, 3))
    lin0(5, 6)
    lax.fori_loop(0, X * H // 2, image_turn, 0, unroll=4)
    receive(E_P3)
    unpack(p3, 3, zr3.at[0])
    inner_conv(2, p3, d3, 1, 3, L // 4, min(16, Zl[3]))
    send(E_R3, (0, 1))
    pack(d3, 3, zs3.at[1])
    send(E_R3, (2, 3))
    receive(E_D2)
    unpack(d2, 2, zr2.at[1])
    inner_conv(3, d2, r2, 1, 2, L // 2, min(32, Zl[2]), relu=False)
    receive(E_D1)
    unpack(d1, 1, zr1.at[1])
    inner_conv(4, d1, r1, 1, 1, L, min(32, Zl[1]), relu=False)
    lin0(6, 7)
    receive(E_R3)
    unpack(d3, 3, zr3.at[1])
    up_conv(3, d3, r2, 2, 1)
    send(E_R2, (0, 1))
    pack(r2, 2, zs2.at[2])
    send(E_R2, (2, 3))
    lax.fori_loop(X * H // 2, X * H, image_turn, 0, unroll=4)
    image_copy = pltpu.make_async_copy(image_out, image_hbm, io_sem.at[3])
    image_copy.start()
    receive(E_D0, (0, 1))
    lin0(0, 1)
    receive(E_R2)
    unpack(r2, 2, zr2.at[2])
    up_conv(4, r2, r1, 1, 1, 2)
    send(E_R1, (0, 1))
    pack(r1, 1, zs1.at[2])
    send(E_R1, (2, 3))
    lin0(X - 1, X)
    over = lax.fori_loop(0, X * (Z // RI), pre_body, jnp.zeros((8, L), F32), unroll=2)
    receive(E_R1, (2, 3))
    unpack(r1, 1, zr1.at[2])
    over = over + sc[2:3] * up_conv(5, r1, z0, 0, H, U_UP, gl, span(1, Xl[1] - 1))
    receive(E_R1, (0, 1))
    over = over + sc[2:3] * up_conv(5, r1, z0, 0, H, U_UP, gl, ends(Xl[1]))
    a_send[1] = over
    copies = reduce_start(n_a, a_send.at[1], a_recv.at[1], asend_sem.at[1], arecv_sem.at[1], peer_a)
    pending += copies
    def last_w(o, k):
        return w_last[k, o]

    for side, plane, o in ((0, 1, 2), (1, X, 1)):
        def part_body(i, carry, side=side, plane=plane, o=o):
            base = pl.multiple_of(i * 32, 8)
            for h in range(H):
                total = None
                for k in range(CH):
                    term = last_w(o, k) * z0[k, h, pl.ds(plane * Zp[0] + PAD + base, 32), :]
                    total = term if total is None else total + term
                xs_m[side, h, pl.ds(base, 32), :] = total
            return carry
        lax.fori_loop(0, Z // 32, part_body, 0)
    for side, at, o in ((0, 0, 6), (1, Z - 1, 5)):
        for h in range(H):
            total = None
            for k in range(CH):
                term = last_w(o, k) * z0[k, h, pl.ds(Zp[0] + PAD + at, X, stride=Zp[0]), :]
                total = term if total is None else total + term
            zs_m[side, pl.ds(h * X, X), :] = total
    send(E_NET)

    def put_net(c, h, base, rows, value):
        net[h, pl.ds(base, rows), :] = value

    conv(loader(z0), put_net, lambda o, c, k: last_w(o, k), None,
          CH, 1, H, 0, 2 * L, 32, span(0, X), unroll=U_LAST, relu=False)
    b_send[1] = reduce_end(copies, a_send.at[1], a_recv.at[1])
    copies = reduce_start(n_chip, b_send.at[1], b_recv.at[1], bsend_sem.at[1], brecv_sem.at[1], peer_b)
    pending += copies
    receive(E_NET)
    for side, plane in ((0, 1), (1, X)):
        for h in range(H):
            at = (h, pl.ds(plane * Zp[0] + PAD, Z), slice(None))
            net[at] = net[at] + xr_m[side, h]
    for side, row in ((0, 0), (1, Z - 1)):
        for h in range(H):
            at = (h, pl.ds(Zp[0] + PAD + row, X, stride=Zp[0]), slice(None))
            net[at] = net[at] + zr_m[side, pl.ds(h * X, X), :]

    def turn_pre(i, carry):
        x, h = i // H, lax.rem(i, H)
        at = (h, pl.ds(pl.multiple_of((x + 1) * Zp[0] + PAD, 8), Z), slice(None))
        block = pre[at] + sc[2:3] * net[at]
        pre_out[x, pl.ds(pl.multiple_of(h * L, L), L), :] = block.T
        return carry

    lax.fori_loop(0, X * H, turn_pre, 0, unroll=4)
    pre_copy = pltpu.make_async_copy(pre_out, pre_hbm, io_sem.at[4])
    pre_copy.start()
    total = reduce_end(copies, b_send.at[1], b_recv.at[1])
    total = jnp.sum(jnp.sum(total, axis=0, keepdims=True), axis=1, keepdims=True)
    coef_out[1:2] = jnp.broadcast_to(total, (1, L)) / sc[3:4]
    coef_out[2:8] = jnp.zeros((6, L), F32)

    image_copy.wait()
    pre_copy.wait()
    for copy in pending:
        copy.wait_send()
    for e in range(N_EX):
        sent(e)


def on_device(residual, direction, diagonal, first_weight, conv_weights, last_weight, biases):
    X, Y, Z = residual.shape
    n_slab, n_col = lax.axis_size("slab"), lax.axis_size("col")
    H = Y // L
    Zl = [Z // 2**l for l in range(4)]
    Xl = [X // 2**l for l in range(4)]
    rows = [(Xl[l] + 2) * (Zl[l] + 2 * PAD) for l in range(4)]
    field = pltpu.VMEM((X, Y, Z), F32)
    one = pltpu.VMEM((H, rows[0], L), F32)
    four = pltpu.VMEM((CH, H, rows[0], L), F32)

    def level(l):
        return pltpu.VMEM((CH, rows[l], L), F32)

    def edge(*lead):
        return pltpu.VMEM((*lead, L), F32)

    def edge_rows(l):
        return max(8, CH * Xl[l])

    n_a, n_b = 2 * n_col, n_slab // 2
    scratch = [
        field, field, field, field, field, four, one, one, one, one, four, four, one, one,
        level(1), level(1), level(1), level(2), level(2), level(2), level(3), level(3),
        edge(3, 2, H * X), edge(3, 2, H * X), edge(2, CH * H * X), edge(2, CH * H * X),
        edge(3, 2, edge_rows(1)), edge(3, 2, edge_rows(1)),
        edge(3, 2, edge_rows(2)), edge(3, 2, edge_rows(2)),
        edge(2, 2, edge_rows(3)), edge(2, 2, edge_rows(3)),
        edge(2, H, Z), edge(2, H, Z), edge(2, H * X), edge(2, H * X),
        pltpu.VMEM((2 * L, L), BF16), edge(8, Z), pltpu.VMEM((2 * L, 2 * L), BF16),
        pltpu.VMEM((3, 2 * L, 2 * L), BF16), edge(8),
        edge(2, 8), edge(2, n_a - 1, 8), edge(2, 8), edge(2, n_b - 1, 8),
        pltpu.SemaphoreType.DMA((5,)),
        pltpu.SemaphoreType.DMA((N_EX, 4)), pltpu.SemaphoreType.DMA((N_EX, 4)),
        pltpu.SemaphoreType.DMA((2, n_a - 1)), pltpu.SemaphoreType.DMA((2, n_a - 1)),
        pltpu.SemaphoreType.DMA((2, n_b - 1)), pltpu.SemaphoreType.DMA((2, n_b - 1)),
    ]
    vmem = pl.BlockSpec(memory_space=pltpu.VMEM)
    anywhere = pl.BlockSpec(memory_space=pl.ANY)
    image, pre, coef = pl.pallas_call(
        functools.partial(kernel, n_slab, n_col, X, Z),
        out_shape=(jax.ShapeDtypeStruct((X, Y, Z), F32),) * 2 + (jax.ShapeDtypeStruct((8, L), F32),),
        in_specs=[pl.BlockSpec(memory_space=pltpu.SMEM)] * 4 + [anywhere] * 3,
        out_specs=(anywhere, anywhere, vmem),
        scratch_shapes=scratch,
        compiler_params=pltpu.CompilerParams(
            collective_id=0, has_side_effects=True, vmem_limit_bytes=56 * 2**20),
    )(first_weight.T, conv_weights.transpose(0, 2, 3, 1), last_weight.T, biases.T,
      residual, direction, diagonal)
    steps = 4
    block = pl.BlockSpec((X // steps, Y, Z), lambda i: (i, 0, 0))
    return pl.pallas_call(
        finish,
        grid=(steps,),
        out_shape=(jax.ShapeDtypeStruct((X, Y, Z), F32),) * 2,
        in_specs=[pl.BlockSpec((8, L), lambda i: (0, 0))] + [block] * 4,
        out_specs=(block, block),
        compiler_params=pltpu.CompilerParams(vmem_limit_bytes=60 * 2**20),
    )(coef, residual, direction, image, pre)


def solution(mesh):
    in_specs = (P("slab", None, "col"),) * 3 + (P(),) * 4
    return jax.shard_map(
        on_device, mesh=mesh, in_specs=in_specs,
        out_specs=(P("slab", None, "col"),) * 2, check_vma=False,
    )
```

```python
import functools

import jax
import jax.numpy as jnp
from jax import lax
from jax.experimental import pallas as pl
from jax.experimental.pallas import tpu as pltpu
from jax.sharding import PartitionSpec as P

MESH = pl.DeviceIdType.MESH
L = 128
PAD = 8
CH = 4
F32 = jnp.float32
BF16 = jnp.bfloat16

(E_DIR, E_RES, E_IMG, E_P1, E_D0, E_P2, E_D1, E_P3, E_D2, E_R3, E_R2, E_R1, E_NET) = range(13)
N_EX = 13


def split2(value):
    high = value.astype(BF16)
    low = (value - high.astype(F32)).astype(BF16)
    return high, low


def span(start, stop):
    return stop - start, lambda j: j + start


def ends(count):
    return 2, lambda j: j * (count - 1)


def kernel(n_slab, n_col, X, Z, *refs):
    (w_first, w_conv, w_last, w_bias, res_hbm, dir_hbm, diag_hbm, image_hbm, pre_hbm, alpha_out, beta_out,
     res_in, dir_in, diag_in, image_out, pre_out, gl, dT, rT, iT, gT, d0, z0, net, pre,
     p1, d1, r1, p2, d2, r2, p3, d3,
     zs0, zr0, zsd, zrd, zs1, zr1, zs2, zr2, zs3, zr3, xs_m, xr_m, zs_m, zr_m,
     pool_m, pool_s, up_m, beside_m, sc, a_send, a_recv, b_send, b_recv,
     io_sem, send_sem, recv_sem, asend_sem, arecv_sem, bsend_sem, brecv_sem) = refs
    H = 2
    U_FIRST, R_FIRST, U_LAST, R_RISE, U_RISE, U_UP = 4, 16, 4, 32, 1, 2
    slab = lax.axis_index("slab")
    col = lax.axis_index("col")
    core = lax.rem(slab, 2)
    chip = slab // 2
    n_chip = n_slab // 2
    n_a = 2 * n_col
    Zp = [Z // 2**l + 2 * PAD for l in range(4)]
    Zl = [Z // 2**l for l in range(4)]
    Xl = [X // 2**l for l in range(4)]
    has = (slab > 0, slab < n_slab - 1, col > 0, col < n_col - 1)
    targets = (
        (jnp.maximum(slab - 1, 0), col),
        (jnp.minimum(slab + 1, n_slab - 1), col),
        (slab, jnp.maximum(col - 1, 0)),
        (slab, jnp.minimum(col + 1, n_col - 1)),
    )
    opposite = (1, 0, 3, 2)

    def x_views(ref, level):
        rows, pitch, count = Zl[level], Zp[level], Xl[level]
        if len(ref.shape) == 3:
            def view(plane):
                return ref.at[:, pl.ds(plane * pitch + PAD, rows), :]
        else:
            def view(plane):
                return ref.at[:, :, pl.ds(plane * pitch + PAD, rows), :]
        return (view(1), view(count)), (view(0), view(count + 1))

    def x_views4(ref, level):
        return x_views(ref, level)

    exchanges = {}

    def define(e, x_src, x_dst, z_src, z_dst):
        msgs = []
        for side in range(4):
            if side < 2:
                src, dst = x_src[side], x_dst[opposite[side]]
            else:
                src, dst = z_src.at[side - 2], z_dst.at[opposite[side] - 2]
            msgs.append(pltpu.make_async_remote_copy(
                src_ref=src, dst_ref=dst,
                send_sem=send_sem.at[e, side],
                recv_sem=recv_sem.at[e, opposite[side]],
                device_id=targets[side], device_id_type=MESH))
        exchanges[e] = msgs

    def send(e, sides=(0, 1, 2, 3)):
        for side in sides:
            @pl.when(has[side])
            def _(side=side):
                exchanges[e][side].start()

    def receive(e, sides=(0, 1, 2, 3)):
        for side in sides:
            @pl.when(has[side])
            def _(side=side):
                exchanges[e][opposite[side]].wait_recv()

    def sent(e):
        for side in range(4):
            @pl.when(has[side])
            def _(side=side):
                exchanges[e][side].wait_send()

    for e, ref, level, zs, zr in (
        (E_DIR, dT, 0, zs0.at[0], zr0.at[0]),
        (E_RES, rT, 0, zs0.at[1], zr0.at[1]),
        (E_IMG, iT, 0, zs0.at[2], zr0.at[2]),
        (E_P1, p1, 1, zs1.at[0], zr1.at[0]),
        (E_D0, d0, 0, zsd, zrd),
        (E_P2, p2, 2, zs2.at[0], zr2.at[0]),
        (E_P3, p3, 3, zs3.at[0], zr3.at[0]),
        (E_D1, d1, 1, zs1.at[1], zr1.at[1]),
        (E_D2, d2, 2, zs2.at[1], zr2.at[1]),
        (E_R3, d3, 3, zs3.at[1], zr3.at[1]),
        (E_R2, r2, 2, zs2.at[2], zr2.at[2]),
        (E_R1, r1, 1, zs1.at[2], zr1.at[2]),
    ):
        src, dst = x_views(ref, level)
        define(e, src, dst, zs, zr)
    define(E_NET, (xs_m.at[0], xs_m.at[1]), (xr_m.at[0], xr_m.at[1]), zs_m, zr_m)

    def groups(ref):
        if len(ref.shape) == 3:
            return [(i,) for i in range(ref.shape[0])]
        return [(c, h) for c in range(ref.shape[0]) for h in range(ref.shape[1])]

    def rows_at(start, count, stride):
        return pl.ds(start, count, stride=stride) if count > 1 else pl.ds(start, 1)

    def pack(ref, level, zs):
        pitch, count = Zp[level], Xl[level]
        for side, row in ((0, 0), (1, Zl[level] - 1)):
            for g, index in enumerate(groups(ref)):
                zs[side, pl.ds(g * count, count), :] = ref[
                    (*index, rows_at(pitch + PAD + row, count, pitch), slice(None))]

    def unpack(ref, level, zr):
        pitch, count = Zp[level], Xl[level]
        for side, row in ((0, -1), (1, Zl[level])):
            for g, index in enumerate(groups(ref)):
                ref[(*index, rows_at(pitch + PAD + row, count, pitch), slice(None))] = zr[
                    side, pl.ds(g * count, count), :]

    loads = [pltpu.make_async_copy(source, target, io_sem.at[n]) for n, (source, target) in
             enumerate(((dir_hbm, dir_in), (res_hbm, res_in), (diag_hbm, diag_in)))]
    for load in loads:
        load.start()

    for side in (0, 1):
        @pl.when(jnp.logical_not(has[side]))
        def _(side=side):
            for ref, level in ((dT, 0), (rT, 0), (iT, 0), (p1, 1), (p2, 2), (p3, 3),
                               (d1, 1), (d2, 2), (d3, 3), (r2, 2), (r1, 1)):
                plane = 0 if side == 0 else Xl[level] + 1
                for index in groups(ref):
                    ref[(*index, pl.ds(plane * Zp[level] + PAD, Zl[level]), slice(None))] = (
                        jnp.zeros((Zl[level], L), F32))
            plane = 0 if side == 0 else X + 1
            for c in range(CH):
                for h in range(H):
                    d0[c, h, pl.ds(plane * Zp[0] + PAD, Z), :] = jnp.zeros((Z, L), F32)
            for h in range(H):
                xr_m[side, h] = jnp.zeros((Z, L), F32)
    for side in (2, 3):
        @pl.when(jnp.logical_not(has[side]))
        def _(side=side):
            s = side - 2
            for ref in (zr0, zr1, zr2, zr3):
                for i in range(ref.shape[0]):
                    ref[i, s] = jnp.zeros(ref.shape[2:], F32)
            zrd[s] = jnp.zeros(zrd.shape[1:], F32)
            zr_m[s] = jnp.zeros(zr_m.shape[1:], F32)

    rank_a = col * 2 + core

    def peer_a(j):
        rank = lax.rem(rank_a + j, n_a)
        return (chip * 2 + lax.rem(rank, 2), rank // 2)

    def peer_b(j):
        return (lax.rem(chip + j, n_chip) * 2 + core, col)

    barrier = pltpu.get_barrier_semaphore()
    for j in range(1, n_a):
        pl.semaphore_signal(barrier, inc=1, device_id=peer_a(j), device_id_type=MESH)
    for j in range(1, n_chip):
        pl.semaphore_signal(barrier, inc=1, device_id=peer_b(j), device_id_type=MESH)
    for side in (0, 1):
        @pl.when(has[side])
        def _(side=side):
            pl.semaphore_signal(barrier, inc=1, device_id=targets[side], device_id_type=MESH)

    def turn_in(source, target):
        def body(i, carry):
            x, h = i // H, lax.rem(i, H)
            block = source[x, pl.ds(pl.multiple_of(h * L, L), L), :]
            target[h, pl.ds(pl.multiple_of((x + 1) * Zp[0] + PAD, 8), Z), :] = block.T
            return carry
        lax.fori_loop(0, X * H, body, 0, unroll=4)

    loads[0].wait()
    turn_in(dir_in, dT)
    pack(dT, 0, zs0.at[0])
    n_wait = (n_a - 1) + (n_chip - 1) + jnp.where(slab > 0, 1, 0) + jnp.where(slab < n_slab - 1, 1, 0)
    pl.semaphore_wait(barrier, n_wait)
    send(E_DIR)
    loads[1].wait()
    turn_in(res_in, rT)
    pack(rT, 0, zs0.at[1])
    send(E_RES)
    loads[2].wait()
    turn_in(diag_in, gT)

    def beside_y(center, ny):
        rows = center[0].shape[0]
        lane = lax.broadcasted_iota(jnp.int32, (rows, L), 1)
        count = len(center)
        last = L - 1 if count > 1 else ny - 1
        up = [pltpu.roll(v, 1, 1) for v in center]
        down = [pltpu.roll(v, L - 1, 1) for v in center]
        zero = jnp.zeros((rows, L), F32)
        minus = [jnp.where(lane == 0, up[h - 1] if h > 0 else zero, up[h]) for h in range(count)]
        plus = [jnp.where(lane == last, down[h + 1] if h < count - 1 else zero, down[h])
                for h in range(count)]
        return minus, plus

    def fold(value):
        return jnp.sum(value.reshape(value.shape[0] // 8, 8, L), axis=0)

    RI = 32

    def image_body(i, carry, place):
        per = Z // RI
        base = pl.multiple_of((place(i // per) + 1) * Zp[0] + PAD + lax.rem(i, per) * RI, 8)
        center = [dT[h, pl.ds(base, RI), :] for h in range(H)]
        minus, plus = beside_y(center, 2 * L)
        sums = list(carry)
        for h in range(H):
            beside = dT[h, pl.ds(base + Zp[0], RI), :] + dT[h, pl.ds(base - Zp[0], RI), :]
            beside = beside + plus[h] + minus[h]
            beside = beside + dT[h, pl.ds(base + 1, RI), :] + dT[h, pl.ds(base - 1, RI), :]
            image = (6.0 + gT[h, pl.ds(base, RI), :]) * center[h] - beside
            iT[h, pl.ds(base, RI), :] = image
            r = rT[h, pl.ds(base, RI), :]
            for q, term in enumerate((center[h] * image, r * center[h], r * r, r * image,
                                      image * image)):
                sums[q] = sums[q] + fold(term)
        return tuple(sums)

    sums = tuple(jnp.zeros((8, L), F32) for _ in range(5))
    receive(E_DIR, (2, 3))
    unpack(dT, 0, zr0.at[0])
    for sides, (count, place) in ((None, span(1, X - 1)), ((0, 1), ends(X))):
        if sides is not None:
            receive(E_DIR, sides)
        sums = lax.fori_loop(0, count * (Z // RI), functools.partial(image_body, place=place),
                             sums, unroll=2)

    def reduce_start(n, send_ref, recv_ref, ssem, rsem, peer):
        copies = []
        for j in range(1, n):
            copy = pltpu.make_async_remote_copy(
                src_ref=send_ref, dst_ref=recv_ref.at[j - 1], send_sem=ssem.at[j - 1],
                recv_sem=rsem.at[j - 1], device_id=peer(j), device_id_type=MESH)
            copy.start()
            copies.append(copy)
        return copies

    def reduce_end(copies, send_ref, recv_ref):
        total = send_ref[...]
        for j, copy in enumerate(copies):
            copy.wait_recv()
        for j in range(len(copies)):
            total = total + recv_ref[j]
        return total

    pending = []
    a_send[0] = jnp.zeros((8, L), F32)
    for q in range(5):
        a_send[0, q:q + 1, :] = jnp.sum(sums[q], axis=0, keepdims=True)
    copies = reduce_start(n_a, a_send.at[0], a_recv.at[0], asend_sem.at[0], arecv_sem.at[0], peer_a)
    pending += copies
    pack(iT, 0, zs0.at[2])
    send(E_IMG)
    row = lax.broadcasted_iota(jnp.int32, (2 * L, L), 0)
    lane = lax.broadcasted_iota(jnp.int32, (2 * L, L), 1)
    pool_m[...] = jnp.where(row // 2 == lane, 0.125, 0.0).astype(BF16)
    row = lax.broadcasted_iota(jnp.int32, (2 * L, 2 * L), 0)
    lane = lax.broadcasted_iota(jnp.int32, (2 * L, 2 * L), 1)
    source = lax.rem(row, L)
    up_m[...] = jnp.where(lane // 2 == source, 1.0, 0.0).astype(BF16)
    for l in range(3):
        match = jnp.where(row < L, (lane + 1) // 2 - 1, (lane + 1) // 2)
        match = jnp.where(source < L // 2**l, match, -1)
        beside_m[l] = jnp.where(match == source, 1.0, 0.0).astype(BF16)
    for c in range(CH):
        for h in range(H):
            for plane in (0, X + 1):
                z0[c, h, pl.ds(plane * Zp[0] + PAD, Z), :] = jnp.zeros((Z, L), F32)
            for at in (PAD - 1, PAD + Z):
                z0[c, h, pl.ds(Zp[0] + at, X, stride=Zp[0]), :] = jnp.zeros((X, L), F32)

    def conv(load, store, weight, bias, n_in, n_out, count_h, level, ny, rows, planes, unroll=1, relu=True):
        per = Zl[level] // rows
        pitch = Zp[level]

        def body(i, carry):
            base = pl.multiple_of((planes[1](i // per) + 1) * pitch + PAD + lax.rem(i, per) * rows, 8)
            acc = [[None] * count_h for _ in range(n_out)]
            for k in range(n_in):
                center = [load(k, h, base, rows) for h in range(count_h)]
                minus, plus = beside_y(center, ny)
                for o in range(7):
                    for h in range(count_h):
                        tap = (center[h] if o == 0 else
                               load(k, h, base - pitch, rows) if o == 1 else
                               load(k, h, base + pitch, rows) if o == 2 else
                               minus[h] if o == 3 else plus[h] if o == 4 else
                               load(k, h, base - 1, rows) if o == 5 else
                               load(k, h, base + 1, rows))
                        for c in range(n_out):
                            term = weight(o, c, k) * tap
                            acc[c][h] = term if acc[c][h] is None else acc[c][h] + term
            for c in range(n_out):
                for h in range(count_h):
                    value = acc[c][h]
                    if bias is not None:
                        value = value + bias(c)
                    if relu:
                        value = jnp.maximum(value, 0.0)
                    store(c, h, base, rows, value)
            return carry
        lax.fori_loop(0, planes[0] * per, body, 0, unroll=unroll)

    def loader(ref):
        if len(ref.shape) == 3:
            return lambda k, h, base, rows: ref[k, pl.ds(base, rows), :]
        return lambda k, h, base, rows: ref[k, h, pl.ds(base, rows), :]

    def storer(ref):
        def put(c, h, base, rows, value):
            if len(ref.shape) == 3:
                ref[c, pl.ds(base, rows), :] = value
            else:
                ref[c, h, pl.ds(base, rows), :] = value
        return put

    def inner_conv(which, source, target, count_h, level, ny, rows, planes=None, unroll=1, relu=True):
        conv(loader(source), storer(target),
             lambda o, c, k: w_conv[which, c, k, o],
             lambda c: w_bias[c, which + 1],
             CH, CH, count_h, level, ny, rows, span(0, Xl[level]) if planes is None else planes, unroll, relu)

    def pool(source, target, level, count_h, active=None, planes=None):
        Z0, Z1 = Zl[level], Zl[level + 1]
        count, place = span(0, Xl[level + 1]) if planes is None else planes

        def body(i, carry):
            c, x1 = i // count, place(lax.rem(i, count))
            slot = lax.rem(i, 8)
            parts = []
            for h in range(count_h):
                total = None
                for dx in range(2):
                    at = pl.ds(pl.multiple_of((2 * x1 + dx + 1) * Zp[level] + PAD, 8), Z0)
                    if active is not None:
                        v = active(c, h, at)
                        source[c, h, at, :] = v
                    else:
                        v = source[c, h, at, :] if count_h > 1 else source[c, at, :]
                    total = v if total is None else total + v
                parts.append(total)
            value = jnp.concatenate(parts, axis=1) if count_h > 1 else parts[0]
            high, low = split2(value)
            m = pool_m[0:count_h * L, :]
            out = jnp.dot(high, m, preferred_element_type=F32) + jnp.dot(low, m, preferred_element_type=F32)
            pool_s[slot, 0:Z0, :] = out
            target[c, pl.ds(pl.multiple_of((x1 + 1) * Zp[level + 1] + PAD, 8), Z1), :] = (
                pool_s[slot, pl.ds(0, Z1, stride=2), :] + pool_s[slot, pl.ds(1, Z1, stride=2), :])
            return carry
        lax.fori_loop(0, CH * count, body, 0, unroll=8 if active is not None else 4)

    def up_conv(which, source, target, level, count_h, unroll=1, other=None, planes=None):
        Z1, X1 = Zl[level + 1], Xl[level + 1]
        pitch, fine = Zp[level + 1], Zp[level]
        rows = min(32, Z1)
        per = Z1 // rows
        count, place = span(0, X1) if planes is None else planes

        def body(i, carry):
            x1, r1 = place(i // per), lax.rem(i, per) * rows
            base = pl.multiple_of((x1 + 1) * pitch + PAD + r1, 8)
            flat, sides = [], []
            for c in range(CH):
                total = [None] * 7

                def add(place, term):
                    total[place] = term if total[place] is None else total[place] + term

                for k in range(CH):
                    wt = [w_conv[which, c, k, o] for o in range(7)]
                    here = source[k, pl.ds(base, rows), :]
                    x_low, x_high = wt[1] * here, wt[2] * here
                    z_low, z_high = wt[5] * here, wt[6] * here
                    add(0, wt[0] * here)
                    add(1, x_high)
                    add(1, wt[1] * source[k, pl.ds(base - pitch, rows), :])
                    add(2, x_low)
                    add(2, wt[2] * source[k, pl.ds(base + pitch, rows), :])
                    add(3, z_high)
                    add(3, wt[5] * source[k, pl.ds(base - 1, rows), :])
                    add(4, z_low)
                    add(4, wt[6] * source[k, pl.ds(base + 1, rows), :])
                    add(5, wt[3] * here)
                    add(6, wt[4] * here)
                for dx in range(2):
                    part = total[0] + total[1 + dx]
                    for dz in range(2):
                        flat.append(jnp.concatenate(split2(part + total[3 + dz]), axis=1))
                low, high = split2(total[5]), split2(total[6])
                sides.append([jnp.concatenate([low[n], high[n]], axis=1) for n in range(2)])
            flat = jnp.concatenate(flat, axis=0)
            flat = jnp.dot(flat, up_m[:, 0:count_h * L], preferred_element_type=F32)
            sides = jnp.concatenate([v[0] for v in sides] + [v[1] for v in sides], axis=0)
            sides = jnp.dot(sides, beside_m[level, :, 0:count_h * L], preferred_element_type=F32)
            for c in range(CH):
                side = sides[c * rows:(c + 1) * rows] + sides[(CH + c) * rows:(CH + c + 1) * rows]
                for dx in range(2):
                    for dz in range(2):
                        n = (c * 2 + dx) * 2 + dz
                        value = flat[n * rows:(n + 1) * rows] + side
                        at_rows = pl.ds((2 * x1 + dx + 1) * fine + PAD + 2 * r1 + dz, rows, stride=2)
                        for h in range(count_h):
                            at = (c, h, at_rows, slice(None)) if count_h > 1 else (c, at_rows, slice(None))
                            out = jnp.maximum(target[at] + value[:, h * L:(h + 1) * L], 0.0)
                            target[at] = out
                            if other is not None:
                                carry = carry + fold(out * other[at])
            return carry
        return lax.fori_loop(0, count * per, body, jnp.zeros((8, L), F32), unroll=unroll)

    def first_conv(source, target):
        conv(lambda k, h, base, rows: source[h, pl.ds(base, rows), :], storer(target),
             lambda o, c, k: w_first[c, o], None, 1, CH, H, 0, 2 * L, R_FIRST, span(0, X),
             unroll=U_FIRST, relu=False)

    receive(E_RES)
    unpack(rT, 0, zr0.at[1])
    first_conv(rT, d0)
    b_send[0] = reduce_end(copies, a_send.at[0], a_recv.at[0])
    copies = reduce_start(n_chip, b_send.at[0], b_recv.at[0], bsend_sem.at[0], brecv_sem.at[0], peer_b)
    pending += copies
    receive(E_IMG)
    unpack(iT, 0, zr0.at[2])
    first_conv(iT, z0)
    total = reduce_end(copies, b_send.at[0], b_recv.at[0])
    full = jnp.broadcast_to(jnp.sum(total, axis=1, keepdims=True), (8, L))
    curvature = full[0:1]
    alpha = full[1:2] / curvature
    mixed = total[2:3] - 2.0 * alpha * total[3:4] + alpha * alpha * total[4:5]
    squares = jnp.maximum(jnp.broadcast_to(jnp.sum(mixed, axis=1, keepdims=True), (1, L)), 0.0)
    cells = float(X * n_slab) * float(2 * L) * float(Z * n_col)
    scale = jnp.sqrt(squares / cells + 1e-06)
    sc[0:1] = alpha
    sc[1:2] = 1.0 / scale
    sc[4:5] = alpha / scale
    sc[2:3] = scale
    sc[3:4] = curvature
    alpha_out[...] = alpha

    def lin0(x_from, x_to):
        inner_conv(5, d0, z0, H, 0, 2 * L, R_RISE, span(x_from, x_to), unroll=U_RISE, relu=False)

    def image_turn(i, carry):
        x, h = i // H, lax.rem(i, H)
        block = iT[h, pl.ds(pl.multiple_of((x + 1) * Zp[0] + PAD, 8), Z), :]
        image_out[x, pl.ds(pl.multiple_of(h * L, L), L), :] = block.T
        return carry

    def pre_body(i, carry):
        per = Z // RI
        base = pl.multiple_of((i // per + 1) * Zp[0] + PAD + lax.rem(i, per) * RI, 8)
        for h in range(H):
            at = (h, pl.ds(base, RI), slice(None))
            image = iT[at]
            value = (rT[at] - sc[0:1] * image) / (6.0 + gT[at])
            pre[at] = value
            carry = carry + fold(value * image)
        return carry

    def transposed_last():
        flip = (0, 2, 1, 4, 3, 6, 5)
        conv(lambda k, h, base, rows: iT[h, pl.ds(base, rows), :], storer(gl),
             lambda o, c, k: w_last[c, flip[o]], None, 1, CH, H, 0, 2 * L, R_FIRST, span(0, X),
             unroll=U_FIRST, relu=False)

    def down_zero(c, h, at):
        return jnp.maximum(d0[c, h, at, :] * sc[1:2] - z0[c, h, at, :] * sc[4:5] + w_bias[c, 0], 0.0)

    for side, row in ((0, 0), (1, Z - 1)):
        for c in range(CH):
            for h in range(H):
                zsd[side, pl.ds((c * H + h) * X, X), :] = down_zero(
                    c, h, pl.ds(Zp[0] + PAD + row, X, stride=Zp[0]))
    send(E_D0, (2, 3))
    pool(d0, p1, 0, H, down_zero, ends(Xl[1]))
    send(E_P1, (0, 1))
    pool(d0, p1, 0, H, down_zero, span(1, Xl[1] - 1))
    pack(p1, 1, zs1.at[0])
    send(E_P1, (2, 3))
    send(E_D0, (0, 1))
    transposed_last()
    receive(E_D0, (2, 3))
    unpack(d0, 0, zrd)
    lin0(1, 2)
    receive(E_P1, (2, 3))
    unpack(p1, 1, zr1.at[0])
    inner_conv(0, p1, d1, 1, 1, L, min(32, Zl[1]), span(1, Xl[1] - 1), unroll=2)
    receive(E_P1, (0, 1))
    inner_conv(0, p1, d1, 1, 1, L, min(32, Zl[1]), ends(Xl[1]), unroll=2)
    pool(d1, p2, 1, 1)
    pack(p2, 2, zs2.at[0])
    send(E_P2)
    pack(d1, 1, zs1.at[1])
    send(E_D1)
    lin0(2, 4)
    receive(E_P2)
    unpack(p2, 2, zr2.at[0])
    inner_conv(1, p2, d2, 1, 2, L // 2, min(32, Zl[2]))
    pool(d2, p3, 2, 1)
    pack(p3, 3, zs3.at[0])
    send(E_P3)
    pack(d2, 2, zs2.at[1])
    send(E_D2)
    lin0(4, 5)
    lax.fori_loop(0, X * H // 2, image_turn, 0, unroll=4)
    receive(E_P3)
    unpack(p3, 3, zr3.at[0])
    inner_conv(2, p3, d3, 1, 3, L // 4, min(16, Zl[3]))
    pack(d3, 3, zs3.at[1])
    send(E_R3)
    receive(E_D2)
    unpack(d2, 2, zr2.at[1])
    inner_conv(3, d2, r2, 1, 2, L // 2, min(32, Zl[2]), relu=False)
    receive(E_D1)
    unpack(d1, 1, zr1.at[1])
    inner_conv(4, d1, r1, 1, 1, L, min(32, Zl[1]), relu=False)
    lin0(5, 6)
    receive(E_R3)
    unpack(d3, 3, zr3.at[1])
    up_conv(3, d3, r2, 2, 1)
    pack(r2, 2, zs2.at[2])
    send(E_R2)
    lax.fori_loop(X * H // 2, X * H, image_turn, 0, unroll=4)
    image_copy = pltpu.make_async_copy(image_out, image_hbm, io_sem.at[3])
    image_copy.start()
    lin0(6, 7)
    receive(E_D0, (0, 1))
    lin0(0, 1)
    receive(E_R2)
    unpack(r2, 2, zr2.at[2])
    up_conv(4, r2, r1, 1, 1, 2)
    pack(r1, 1, zs1.at[2])
    send(E_R1)
    lin0(X - 1, X)
    over = lax.fori_loop(0, X * (Z // RI), pre_body, jnp.zeros((8, L), F32), unroll=2)
    receive(E_R1, (2, 3))
    unpack(r1, 1, zr1.at[2])
    over = over + sc[2:3] * up_conv(5, r1, z0, 0, H, U_UP, gl, span(1, Xl[1] - 1))
    receive(E_R1, (0, 1))
    over = over + sc[2:3] * up_conv(5, r1, z0, 0, H, U_UP, gl, ends(Xl[1]))
    a_send[1] = over
    copies = reduce_start(n_a, a_send.at[1], a_recv.at[1], asend_sem.at[1], arecv_sem.at[1], peer_a)
    pending += copies
    def last_w(o, k):
        return w_last[k, o]

    for side, plane, o in ((0, 1, 2), (1, X, 1)):
        def part_body(i, carry, side=side, plane=plane, o=o):
            base = pl.multiple_of(i * 32, 8)
            for h in range(H):
                total = None
                for k in range(CH):
                    term = last_w(o, k) * z0[k, h, pl.ds(plane * Zp[0] + PAD + base, 32), :]
                    total = term if total is None else total + term
                xs_m[side, h, pl.ds(base, 32), :] = total
            return carry
        lax.fori_loop(0, Z // 32, part_body, 0)
    for side, at, o in ((0, 0, 6), (1, Z - 1, 5)):
        for h in range(H):
            total = None
            for k in range(CH):
                term = last_w(o, k) * z0[k, h, pl.ds(Zp[0] + PAD + at, X, stride=Zp[0]), :]
                total = term if total is None else total + term
            zs_m[side, pl.ds(h * X, X), :] = total
    send(E_NET)

    def put_net(c, h, base, rows, value):
        net[h, pl.ds(base, rows), :] = value

    conv(loader(z0), put_net, lambda o, c, k: last_w(o, k), None,
          CH, 1, H, 0, 2 * L, 32, span(0, X), unroll=U_LAST, relu=False)
    b_send[1] = reduce_end(copies, a_send.at[1], a_recv.at[1])
    copies = reduce_start(n_chip, b_send.at[1], b_recv.at[1], bsend_sem.at[1], brecv_sem.at[1], peer_b)
    pending += copies
    receive(E_NET)
    for side, plane in ((0, 1), (1, X)):
        for h in range(H):
            at = (h, pl.ds(plane * Zp[0] + PAD, Z), slice(None))
            net[at] = net[at] + xr_m[side, h]
    for side, row in ((0, 0), (1, Z - 1)):
        for h in range(H):
            at = (h, pl.ds(Zp[0] + PAD + row, X, stride=Zp[0]), slice(None))
            net[at] = net[at] + zr_m[side, pl.ds(h * X, X), :]

    def turn_pre(i, carry):
        x, h = i // H, lax.rem(i, H)
        at = (h, pl.ds(pl.multiple_of((x + 1) * Zp[0] + PAD, 8), Z), slice(None))
        block = pre[at] + sc[2:3] * net[at]
        pre_out[x, pl.ds(pl.multiple_of(h * L, L), L), :] = block.T
        return carry

    lax.fori_loop(0, X * H, turn_pre, 0, unroll=4)
    pre_copy = pltpu.make_async_copy(pre_out, pre_hbm, io_sem.at[4])
    pre_copy.start()
    total = reduce_end(copies, b_send.at[1], b_recv.at[1])
    total = jnp.sum(jnp.sum(total, axis=0, keepdims=True), axis=1, keepdims=True)
    beta_out[...] = jnp.broadcast_to(total, (1, L)) / sc[3:4]

    image_copy.wait()
    pre_copy.wait()
    for copy in pending:
        copy.wait_send()
    for e in range(N_EX):
        sent(e)


def on_device(residual, direction, diagonal, first_weight, conv_weights, last_weight, biases):
    X, Y, Z = residual.shape
    n_slab, n_col = lax.axis_size("slab"), lax.axis_size("col")
    H = Y // L
    Zl = [Z // 2**l for l in range(4)]
    Xl = [X // 2**l for l in range(4)]
    rows = [(Xl[l] + 2) * (Zl[l] + 2 * PAD) for l in range(4)]
    field = pltpu.VMEM((X, Y, Z), F32)
    one = pltpu.VMEM((H, rows[0], L), F32)
    four = pltpu.VMEM((CH, H, rows[0], L), F32)

    def level(l):
        return pltpu.VMEM((CH, rows[l], L), F32)

    def edge(*lead):
        return pltpu.VMEM((*lead, L), F32)

    def edge_rows(l):
        return max(8, CH * Xl[l])

    n_a, n_b = 2 * n_col, n_slab // 2
    scratch = [
        field, field, field, field, field, four, one, one, one, one, four, four, one, one,
        level(1), level(1), level(1), level(2), level(2), level(2), level(3), level(3),
        edge(3, 2, H * X), edge(3, 2, H * X), edge(2, CH * H * X), edge(2, CH * H * X),
        edge(3, 2, edge_rows(1)), edge(3, 2, edge_rows(1)),
        edge(3, 2, edge_rows(2)), edge(3, 2, edge_rows(2)),
        edge(2, 2, edge_rows(3)), edge(2, 2, edge_rows(3)),
        edge(2, H, Z), edge(2, H, Z), edge(2, H * X), edge(2, H * X),
        pltpu.VMEM((2 * L, L), BF16), edge(8, Z), pltpu.VMEM((2 * L, 2 * L), BF16),
        pltpu.VMEM((3, 2 * L, 2 * L), BF16), edge(8),
        edge(2, 8), edge(2, n_a - 1, 8), edge(2, 8), edge(2, n_b - 1, 8),
        pltpu.SemaphoreType.DMA((5,)),
        pltpu.SemaphoreType.DMA((N_EX, 4)), pltpu.SemaphoreType.DMA((N_EX, 4)),
        pltpu.SemaphoreType.DMA((2, n_a - 1)), pltpu.SemaphoreType.DMA((2, n_a - 1)),
        pltpu.SemaphoreType.DMA((2, n_b - 1)), pltpu.SemaphoreType.DMA((2, n_b - 1)),
    ]
    vmem = pl.BlockSpec(memory_space=pltpu.VMEM)
    anywhere = pl.BlockSpec(memory_space=pl.ANY)
    image, pre, alpha, beta = pl.pallas_call(
        functools.partial(kernel, n_slab, n_col, X, Z),
        out_shape=(jax.ShapeDtypeStruct((X, Y, Z), F32),) * 2 + (jax.ShapeDtypeStruct((1, L), F32),) * 2,
        in_specs=[pl.BlockSpec(memory_space=pltpu.SMEM)] * 4 + [anywhere] * 3,
        out_specs=(anywhere, anywhere, vmem, vmem),
        scratch_shapes=scratch,
        compiler_params=pltpu.CompilerParams(
            collective_id=0, has_side_effects=True, vmem_limit_bytes=56 * 2**20),
    )(first_weight.T, conv_weights.transpose(0, 2, 3, 1), last_weight.T, biases.T,
      residual, direction, diagonal)
    return residual - alpha[:, :Z] * image, pre - beta[:, :Z] * direction


def solution(mesh):
    in_specs = (P("slab", None, "col"),) * 3 + (P(),) * 4
    return jax.shard_map(
        on_device, mesh=mesh, in_specs=in_specs,
        out_specs=(P("slab", None, "col"),) * 2, check_vma=False,
    )
```

```python
import functools

import jax
import jax.numpy as jnp
from jax import lax
from jax.experimental import pallas as pl
from jax.experimental.pallas import tpu as pltpu
from jax.sharding import PartitionSpec as P

MESH = pl.DeviceIdType.MESH
L = 128
PAD = 8
CH = 4
F32 = jnp.float32
BF16 = jnp.bfloat16

(E_DIR, E_RES, E_IMG, E_P1, E_D0, E_P2, E_D1, E_P3, E_D2, E_R3, E_R2, E_R1, E_NET) = range(13)
N_EX = 13


def split2(value):
    high = value.astype(BF16)
    low = (value - high.astype(F32)).astype(BF16)
    return high, low


def span(start, stop):
    return stop - start, lambda j: j + start


def ends(count):
    return 2, lambda j: j * (count - 1)


def kernel(n_slab, n_col, X, Z, *refs):
    (w_first, w_conv, w_last, w_bias, res_hbm, dir_hbm, diag_hbm, image_hbm, pre_hbm, alpha_out, beta_out,
     res_in, dir_in, diag_in, image_out, pre_out, gl, dT, rT, iT, gT, d0, z0, net, pre,
     p1, d1, r1, p2, d2, r2, p3, d3,
     zs0, zr0, zsd, zrd, zs1, zr1, zs2, zr2, zs3, zr3, xs_m, xr_m, zs_m, zr_m,
     pool_m, pool_s, up_m, beside_m, sc, a_send, a_recv, b_send, b_recv,
     io_sem, send_sem, recv_sem, asend_sem, arecv_sem, bsend_sem, brecv_sem) = refs
    H = 2
    U_FIRST, R_FIRST, U_LAST, R_RISE, U_RISE, U_UP = 4, 16, 4, 32, 1, 2
    slab = lax.axis_index("slab")
    col = lax.axis_index("col")
    core = lax.rem(slab, 2)
    chip = slab // 2
    n_chip = n_slab // 2
    n_a = 2 * n_col
    Zp = [Z // 2**l + 2 * PAD for l in range(4)]
    Zl = [Z // 2**l for l in range(4)]
    Xl = [X // 2**l for l in range(4)]
    has = (slab > 0, slab < n_slab - 1, col > 0, col < n_col - 1)
    targets = (
        (jnp.maximum(slab - 1, 0), col),
        (jnp.minimum(slab + 1, n_slab - 1), col),
        (slab, jnp.maximum(col - 1, 0)),
        (slab, jnp.minimum(col + 1, n_col - 1)),
    )
    opposite = (1, 0, 3, 2)

    def x_views(ref, level):
        rows, pitch, count = Zl[level], Zp[level], Xl[level]
        if len(ref.shape) == 3:
            def view(plane):
                return ref.at[:, pl.ds(plane * pitch + PAD, rows), :]
        else:
            def view(plane):
                return ref.at[:, :, pl.ds(plane * pitch + PAD, rows), :]
        return (view(1), view(count)), (view(0), view(count + 1))

    def x_views4(ref, level):
        return x_views(ref, level)

    exchanges = {}

    def define(e, x_src, x_dst, z_src, z_dst):
        msgs = []
        for side in range(4):
            if side < 2:
                src, dst = x_src[side], x_dst[opposite[side]]
            else:
                src, dst = z_src.at[side - 2], z_dst.at[opposite[side] - 2]
            msgs.append(pltpu.make_async_remote_copy(
                src_ref=src, dst_ref=dst,
                send_sem=send_sem.at[e, side],
                recv_sem=recv_sem.at[e, opposite[side]],
                device_id=targets[side], device_id_type=MESH))
        exchanges[e] = msgs

    def send(e, sides=(0, 1, 2, 3)):
        for side in sides:
            @pl.when(has[side])
            def _(side=side):
                exchanges[e][side].start()

    def receive(e, sides=(0, 1, 2, 3)):
        for side in sides:
            @pl.when(has[side])
            def _(side=side):
                exchanges[e][opposite[side]].wait_recv()

    def sent(e):
        for side in range(4):
            @pl.when(has[side])
            def _(side=side):
                exchanges[e][side].wait_send()

    for e, ref, level, zs, zr in (
        (E_DIR, dT, 0, zs0.at[0], zr0.at[0]),
        (E_RES, rT, 0, zs0.at[1], zr0.at[1]),
        (E_IMG, iT, 0, zs0.at[2], zr0.at[2]),
        (E_P1, p1, 1, zs1.at[0], zr1.at[0]),
        (E_D0, d0, 0, zsd, zrd),
        (E_P2, p2, 2, zs2.at[0], zr2.at[0]),
        (E_P3, p3, 3, zs3.at[0], zr3.at[0]),
        (E_D1, d1, 1, zs1.at[1], zr1.at[1]),
        (E_D2, d2, 2, zs2.at[1], zr2.at[1]),
        (E_R3, d3, 3, zs3.at[1], zr3.at[1]),
        (E_R2, r2, 2, zs2.at[2], zr2.at[2]),
        (E_R1, r1, 1, zs1.at[2], zr1.at[2]),
    ):
        src, dst = x_views(ref, level)
        define(e, src, dst, zs, zr)
    define(E_NET, (xs_m.at[0], xs_m.at[1]), (xr_m.at[0], xr_m.at[1]), zs_m, zr_m)

    def groups(ref):
        if len(ref.shape) == 3:
            return [(i,) for i in range(ref.shape[0])]
        return [(c, h) for c in range(ref.shape[0]) for h in range(ref.shape[1])]

    def rows_at(start, count, stride):
        return pl.ds(start, count, stride=stride) if count > 1 else pl.ds(start, 1)

    def pack(ref, level, zs):
        pitch, count = Zp[level], Xl[level]
        for side, row in ((0, 0), (1, Zl[level] - 1)):
            for g, index in enumerate(groups(ref)):
                zs[side, pl.ds(g * count, count), :] = ref[
                    (*index, rows_at(pitch + PAD + row, count, pitch), slice(None))]

    def unpack(ref, level, zr):
        pitch, count = Zp[level], Xl[level]
        for side, row in ((0, -1), (1, Zl[level])):
            for g, index in enumerate(groups(ref)):
                ref[(*index, rows_at(pitch + PAD + row, count, pitch), slice(None))] = zr[
                    side, pl.ds(g * count, count), :]

    loads = [pltpu.make_async_copy(source, target, io_sem.at[n]) for n, (source, target) in
             enumerate(((dir_hbm, dir_in), (res_hbm, res_in), (diag_hbm, diag_in)))]
    for load in loads:
        load.start()

    for side in (0, 1):
        @pl.when(jnp.logical_not(has[side]))
        def _(side=side):
            for ref, level in ((dT, 0), (rT, 0), (iT, 0), (p1, 1), (p2, 2), (p3, 3),
                               (d1, 1), (d2, 2), (d3, 3), (r2, 2), (r1, 1)):
                plane = 0 if side == 0 else Xl[level] + 1
                for index in groups(ref):
                    ref[(*index, pl.ds(plane * Zp[level] + PAD, Zl[level]), slice(None))] = (
                        jnp.zeros((Zl[level], L), F32))
            plane = 0 if side == 0 else X + 1
            for c in range(CH):
                for h in range(H):
                    d0[c, h, pl.ds(plane * Zp[0] + PAD, Z), :] = jnp.zeros((Z, L), F32)
            for h in range(H):
                xr_m[side, h] = jnp.zeros((Z, L), F32)
    for side in (2, 3):
        @pl.when(jnp.logical_not(has[side]))
        def _(side=side):
            s = side - 2
            for ref in (zr0, zr1, zr2, zr3):
                for i in range(ref.shape[0]):
                    ref[i, s] = jnp.zeros(ref.shape[2:], F32)
            zrd[s] = jnp.zeros(zrd.shape[1:], F32)
            zr_m[s] = jnp.zeros(zr_m.shape[1:], F32)

    rank_a = col * 2 + core

    def peer_a(j):
        rank = lax.rem(rank_a + j, n_a)
        return (chip * 2 + lax.rem(rank, 2), rank // 2)

    def peer_b(j):
        return (lax.rem(chip + j, n_chip) * 2 + core, col)

    barrier = pltpu.get_barrier_semaphore()
    for j in range(1, n_a):
        pl.semaphore_signal(barrier, inc=1, device_id=peer_a(j), device_id_type=MESH)
    for j in range(1, n_chip):
        pl.semaphore_signal(barrier, inc=1, device_id=peer_b(j), device_id_type=MESH)
    for side in (0, 1):
        @pl.when(has[side])
        def _(side=side):
            pl.semaphore_signal(barrier, inc=1, device_id=targets[side], device_id_type=MESH)

    def turn_in(source, target):
        def body(i, carry):
            x, h = i // H, lax.rem(i, H)
            block = source[x, pl.ds(pl.multiple_of(h * L, L), L), :]
            target[h, pl.ds(pl.multiple_of((x + 1) * Zp[0] + PAD, 8), Z), :] = block.T
            return carry
        lax.fori_loop(0, X * H, body, 0, unroll=4)

    loads[0].wait()
    turn_in(dir_in, dT)
    pack(dT, 0, zs0.at[0])
    n_wait = (n_a - 1) + (n_chip - 1) + jnp.where(slab > 0, 1, 0) + jnp.where(slab < n_slab - 1, 1, 0)
    pl.semaphore_wait(barrier, n_wait)
    send(E_DIR)
    loads[1].wait()
    turn_in(res_in, rT)
    pack(rT, 0, zs0.at[1])
    send(E_RES)
    loads[2].wait()
    turn_in(diag_in, gT)

    def beside_y(center, ny):
        rows = center[0].shape[0]
        lane = lax.broadcasted_iota(jnp.int32, (rows, L), 1)
        count = len(center)
        last = L - 1 if count > 1 else ny - 1
        up = [pltpu.roll(v, 1, 1) for v in center]
        down = [pltpu.roll(v, L - 1, 1) for v in center]
        zero = jnp.zeros((rows, L), F32)
        minus = [jnp.where(lane == 0, up[h - 1] if h > 0 else zero, up[h]) for h in range(count)]
        plus = [jnp.where(lane == last, down[h + 1] if h < count - 1 else zero, down[h])
                for h in range(count)]
        return minus, plus

    def fold(value):
        return jnp.sum(value.reshape(value.shape[0] // 8, 8, L), axis=0)

    RI = 32

    def image_body(i, carry, place):
        per = Z // RI
        base = pl.multiple_of((place(i // per) + 1) * Zp[0] + PAD + lax.rem(i, per) * RI, 8)
        center = [dT[h, pl.ds(base, RI), :] for h in range(H)]
        minus, plus = beside_y(center, 2 * L)
        sums = list(carry)
        for h in range(H):
            beside = dT[h, pl.ds(base + Zp[0], RI), :] + dT[h, pl.ds(base - Zp[0], RI), :]
            beside = beside + plus[h] + minus[h]
            beside = beside + dT[h, pl.ds(base + 1, RI), :] + dT[h, pl.ds(base - 1, RI), :]
            image = (6.0 + gT[h, pl.ds(base, RI), :]) * center[h] - beside
            iT[h, pl.ds(base, RI), :] = image
            r = rT[h, pl.ds(base, RI), :]
            for q, term in enumerate((center[h] * image, r * center[h], r * r, r * image,
                                      image * image)):
                sums[q] = sums[q] + fold(term)
        return tuple(sums)

    sums = tuple(jnp.zeros((8, L), F32) for _ in range(5))
    receive(E_DIR, (2, 3))
    unpack(dT, 0, zr0.at[0])
    for sides, (count, place) in ((None, span(1, X - 1)), ((0, 1), ends(X))):
        if sides is not None:
            receive(E_DIR, sides)
        sums = lax.fori_loop(0, count * (Z // RI), functools.partial(image_body, place=place),
                             sums, unroll=2)

    def reduce_start(n, send_ref, recv_ref, ssem, rsem, peer):
        copies = []
        for j in range(1, n):
            copy = pltpu.make_async_remote_copy(
                src_ref=send_ref, dst_ref=recv_ref.at[j - 1], send_sem=ssem.at[j - 1],
                recv_sem=rsem.at[j - 1], device_id=peer(j), device_id_type=MESH)
            copy.start()
            copies.append(copy)
        return copies

    def reduce_end(copies, send_ref, recv_ref):
        total = send_ref[...]
        for j, copy in enumerate(copies):
            copy.wait_recv()
        for j in range(len(copies)):
            total = total + recv_ref[j]
        return total

    pending = []
    a_send[0] = jnp.zeros((8, L), F32)
    for q in range(5):
        a_send[0, q:q + 1, :] = jnp.sum(sums[q], axis=0, keepdims=True)
    copies = reduce_start(n_a, a_send.at[0], a_recv.at[0], asend_sem.at[0], arecv_sem.at[0], peer_a)
    pending += copies
    send(E_IMG, (0, 1))
    pack(iT, 0, zs0.at[2])
    send(E_IMG, (2, 3))
    row = lax.broadcasted_iota(jnp.int32, (2 * L, L), 0)
    lane = lax.broadcasted_iota(jnp.int32, (2 * L, L), 1)
    pool_m[...] = jnp.where(row // 2 == lane, 0.125, 0.0).astype(BF16)
    row = lax.broadcasted_iota(jnp.int32, (2 * L, 2 * L), 0)
    lane = lax.broadcasted_iota(jnp.int32, (2 * L, 2 * L), 1)
    source = lax.rem(row, L)
    up_m[...] = jnp.where(lane // 2 == source, 1.0, 0.0).astype(BF16)
    for l in range(3):
        match = jnp.where(row < L, (lane + 1) // 2 - 1, (lane + 1) // 2)
        match = jnp.where(source < L // 2**l, match, -1)
        beside_m[l] = jnp.where(match == source, 1.0, 0.0).astype(BF16)
    for c in range(CH):
        for h in range(H):
            for plane in (0, X + 1):
                z0[c, h, pl.ds(plane * Zp[0] + PAD, Z), :] = jnp.zeros((Z, L), F32)
            for at in (PAD - 1, PAD + Z):
                z0[c, h, pl.ds(Zp[0] + at, X, stride=Zp[0]), :] = jnp.zeros((X, L), F32)

    def conv(load, store, weight, bias, n_in, n_out, count_h, level, ny, rows, planes, unroll=1, relu=True):
        per = Zl[level] // rows
        pitch = Zp[level]

        def body(i, carry):
            base = pl.multiple_of((planes[1](i // per) + 1) * pitch + PAD + lax.rem(i, per) * rows, 8)
            acc = [[None] * count_h for _ in range(n_out)]
            for k in range(n_in):
                center = [load(k, h, base, rows) for h in range(count_h)]
                minus, plus = beside_y(center, ny)
                for o in range(7):
                    for h in range(count_h):
                        tap = (center[h] if o == 0 else
                               load(k, h, base - pitch, rows) if o == 1 else
                               load(k, h, base + pitch, rows) if o == 2 else
                               minus[h] if o == 3 else plus[h] if o == 4 else
                               load(k, h, base - 1, rows) if o == 5 else
                               load(k, h, base + 1, rows))
                        for c in range(n_out):
                            term = weight(o, c, k) * tap
                            acc[c][h] = term if acc[c][h] is None else acc[c][h] + term
            for c in range(n_out):
                for h in range(count_h):
                    value = acc[c][h]
                    if bias is not None:
                        value = value + bias(c)
                    if relu:
                        value = jnp.maximum(value, 0.0)
                    store(c, h, base, rows, value)
            return carry
        lax.fori_loop(0, planes[0] * per, body, 0, unroll=unroll)

    def loader(ref):
        if len(ref.shape) == 3:
            return lambda k, h, base, rows: ref[k, pl.ds(base, rows), :]
        return lambda k, h, base, rows: ref[k, h, pl.ds(base, rows), :]

    def storer(ref):
        def put(c, h, base, rows, value):
            if len(ref.shape) == 3:
                ref[c, pl.ds(base, rows), :] = value
            else:
                ref[c, h, pl.ds(base, rows), :] = value
        return put

    def inner_conv(which, source, target, count_h, level, ny, rows, planes=None, unroll=1, relu=True):
        conv(loader(source), storer(target),
             lambda o, c, k: w_conv[which, c, k, o],
             lambda c: w_bias[c, which + 1],
             CH, CH, count_h, level, ny, rows, span(0, Xl[level]) if planes is None else planes, unroll, relu)

    def pool(source, target, level, count_h, active=None, planes=None):
        Z0, Z1 = Zl[level], Zl[level + 1]
        count, place = span(0, Xl[level + 1]) if planes is None else planes

        def body(i, carry):
            c, x1 = i // count, place(lax.rem(i, count))
            slot = lax.rem(i, 8)
            parts = []
            for h in range(count_h):
                total = None
                for dx in range(2):
                    at = pl.ds(pl.multiple_of((2 * x1 + dx + 1) * Zp[level] + PAD, 8), Z0)
                    if active is not None:
                        v = active(c, h, at)
                        source[c, h, at, :] = v
                    else:
                        v = source[c, h, at, :] if count_h > 1 else source[c, at, :]
                    total = v if total is None else total + v
                parts.append(total)
            value = jnp.concatenate(parts, axis=1) if count_h > 1 else parts[0]
            high, low = split2(value)
            m = pool_m[0:count_h * L, :]
            out = jnp.dot(high, m, preferred_element_type=F32) + jnp.dot(low, m, preferred_element_type=F32)
            pool_s[slot, 0:Z0, :] = out
            target[c, pl.ds(pl.multiple_of((x1 + 1) * Zp[level + 1] + PAD, 8), Z1), :] = (
                pool_s[slot, pl.ds(0, Z1, stride=2), :] + pool_s[slot, pl.ds(1, Z1, stride=2), :])
            return carry
        lax.fori_loop(0, CH * count, body, 0, unroll=8 if active is not None else 4)

    def up_conv(which, source, target, level, count_h, unroll=1, other=None, planes=None):
        Z1, X1 = Zl[level + 1], Xl[level + 1]
        pitch, fine = Zp[level + 1], Zp[level]
        rows = min(32, Z1)
        per = Z1 // rows
        count, place = span(0, X1) if planes is None else planes

        def body(i, carry):
            x1, r1 = place(i // per), lax.rem(i, per) * rows
            base = pl.multiple_of((x1 + 1) * pitch + PAD + r1, 8)
            flat, sides = [], []
            for c in range(CH):
                total = [None] * 7

                def add(place, term):
                    total[place] = term if total[place] is None else total[place] + term

                for k in range(CH):
                    wt = [w_conv[which, c, k, o] for o in range(7)]
                    here = source[k, pl.ds(base, rows), :]
                    x_low, x_high = wt[1] * here, wt[2] * here
                    z_low, z_high = wt[5] * here, wt[6] * here
                    add(0, wt[0] * here)
                    add(1, x_high)
                    add(1, wt[1] * source[k, pl.ds(base - pitch, rows), :])
                    add(2, x_low)
                    add(2, wt[2] * source[k, pl.ds(base + pitch, rows), :])
                    add(3, z_high)
                    add(3, wt[5] * source[k, pl.ds(base - 1, rows), :])
                    add(4, z_low)
                    add(4, wt[6] * source[k, pl.ds(base + 1, rows), :])
                    add(5, wt[3] * here)
                    add(6, wt[4] * here)
                for dx in range(2):
                    part = total[0] + total[1 + dx]
                    for dz in range(2):
                        flat.append(jnp.concatenate(split2(part + total[3 + dz]), axis=1))
                low, high = split2(total[5]), split2(total[6])
                sides.append([jnp.concatenate([low[n], high[n]], axis=1) for n in range(2)])
            flat = jnp.concatenate(flat, axis=0)
            flat = jnp.dot(flat, up_m[:, 0:count_h * L], preferred_element_type=F32)
            sides = jnp.concatenate([v[0] for v in sides] + [v[1] for v in sides], axis=0)
            sides = jnp.dot(sides, beside_m[level, :, 0:count_h * L], preferred_element_type=F32)
            for c in range(CH):
                side = sides[c * rows:(c + 1) * rows] + sides[(CH + c) * rows:(CH + c + 1) * rows]
                for dx in range(2):
                    for dz in range(2):
                        n = (c * 2 + dx) * 2 + dz
                        value = flat[n * rows:(n + 1) * rows] + side
                        at_rows = pl.ds((2 * x1 + dx + 1) * fine + PAD + 2 * r1 + dz, rows, stride=2)
                        for h in range(count_h):
                            at = (c, h, at_rows, slice(None)) if count_h > 1 else (c, at_rows, slice(None))
                            out = jnp.maximum(target[at] + value[:, h * L:(h + 1) * L], 0.0)
                            target[at] = out
                            if other is not None:
                                carry = carry + fold(out * other[at])
            return carry
        return lax.fori_loop(0, count * per, body, jnp.zeros((8, L), F32), unroll=unroll)

    def first_conv(source, target):
        conv(lambda k, h, base, rows: source[h, pl.ds(base, rows), :], storer(target),
             lambda o, c, k: w_first[c, o], None, 1, CH, H, 0, 2 * L, R_FIRST, span(0, X),
             unroll=U_FIRST, relu=False)

    receive(E_RES)
    unpack(rT, 0, zr0.at[1])
    first_conv(rT, d0)
    b_send[0] = reduce_end(copies, a_send.at[0], a_recv.at[0])
    copies = reduce_start(n_chip, b_send.at[0], b_recv.at[0], bsend_sem.at[0], brecv_sem.at[0], peer_b)
    pending += copies
    receive(E_IMG)
    unpack(iT, 0, zr0.at[2])
    first_conv(iT, z0)
    total = reduce_end(copies, b_send.at[0], b_recv.at[0])
    full = jnp.broadcast_to(jnp.sum(total, axis=1, keepdims=True), (8, L))
    curvature = full[0:1]
    alpha = full[1:2] / curvature
    mixed = total[2:3] - 2.0 * alpha * total[3:4] + alpha * alpha * total[4:5]
    squares = jnp.maximum(jnp.broadcast_to(jnp.sum(mixed, axis=1, keepdims=True), (1, L)), 0.0)
    cells = float(X * n_slab) * float(2 * L) * float(Z * n_col)
    scale = jnp.sqrt(squares / cells + 1e-06)
    sc[0:1] = alpha
    sc[1:2] = 1.0 / scale
    sc[4:5] = alpha / scale
    sc[2:3] = scale
    sc[3:4] = curvature
    alpha_out[...] = alpha

    def lin0(x_from, x_to):
        inner_conv(5, d0, z0, H, 0, 2 * L, R_RISE, span(x_from, x_to), unroll=U_RISE, relu=False)

    def image_turn(i, carry):
        x, h = i // H, lax.rem(i, H)
        block = iT[h, pl.ds(pl.multiple_of((x + 1) * Zp[0] + PAD, 8), Z), :]
        image_out[x, pl.ds(pl.multiple_of(h * L, L), L), :] = block.T
        return carry

    def pre_body(i, carry):
        per = Z // RI
        base = pl.multiple_of((i // per + 1) * Zp[0] + PAD + lax.rem(i, per) * RI, 8)
        for h in range(H):
            at = (h, pl.ds(base, RI), slice(None))
            image = iT[at]
            value = (rT[at] - sc[0:1] * image) / (6.0 + gT[at])
            pre[at] = value
            carry = carry + fold(value * image)
        return carry

    def transposed_last():
        flip = (0, 2, 1, 4, 3, 6, 5)
        conv(lambda k, h, base, rows: iT[h, pl.ds(base, rows), :], storer(gl),
             lambda o, c, k: w_last[c, flip[o]], None, 1, CH, H, 0, 2 * L, R_FIRST, span(0, X),
             unroll=U_FIRST, relu=False)

    def down_zero(c, h, at):
        return jnp.maximum(d0[c, h, at, :] * sc[1:2] - z0[c, h, at, :] * sc[4:5] + w_bias[c, 0], 0.0)

    for side, row in ((0, 0), (1, Z - 1)):
        for c in range(CH):
            for h in range(H):
                zsd[side, pl.ds((c * H + h) * X, X), :] = down_zero(
                    c, h, pl.ds(Zp[0] + PAD + row, X, stride=Zp[0]))
    send(E_D0, (2, 3))
    pool(d0, p1, 0, H, down_zero, ends(Xl[1]))
    send(E_P1, (0, 1))
    pool(d0, p1, 0, H, down_zero, span(1, Xl[1] - 1))
    pack(p1, 1, zs1.at[0])
    send(E_P1, (2, 3))
    send(E_D0, (0, 1))
    transposed_last()
    receive(E_D0, (2, 3))
    unpack(d0, 0, zrd)
    lin0(1, 2)
    receive(E_P1, (2, 3))
    unpack(p1, 1, zr1.at[0])
    inner_conv(0, p1, d1, 1, 1, L, min(32, Zl[1]), span(1, Xl[1] - 1), unroll=2)
    receive(E_P1, (0, 1))
    inner_conv(0, p1, d1, 1, 1, L, min(32, Zl[1]), ends(Xl[1]), unroll=2)
    pool(d1, p2, 1, 1)
    send(E_P2, (0, 1))
    pack(p2, 2, zs2.at[0])
    send(E_P2, (2, 3))
    pack(d1, 1, zs1.at[1])
    send(E_D1)
    lin0(2, 4)
    receive(E_P2)
    unpack(p2, 2, zr2.at[0])
    inner_conv(1, p2, d2, 1, 2, L // 2, min(32, Zl[2]))
    pool(d2, p3, 2, 1)
    send(E_P3, (0, 1))
    pack(p3, 3, zs3.at[0])
    send(E_P3, (2, 3))
    pack(d2, 2, zs2.at[1])
    send(E_D2)
    lin0(4, 5)
    lax.fori_loop(0, X * H // 2, image_turn, 0, unroll=4)
    receive(E_P3)
    unpack(p3, 3, zr3.at[0])
    inner_conv(2, p3, d3, 1, 3, L // 4, min(16, Zl[3]))
    send(E_R3, (0, 1))
    pack(d3, 3, zs3.at[1])
    send(E_R3, (2, 3))
    receive(E_D2)
    unpack(d2, 2, zr2.at[1])
    inner_conv(3, d2, r2, 1, 2, L // 2, min(32, Zl[2]), relu=False)
    receive(E_D1)
    unpack(d1, 1, zr1.at[1])
    inner_conv(4, d1, r1, 1, 1, L, min(32, Zl[1]), relu=False)
    lin0(5, 6)
    receive(E_R3)
    unpack(d3, 3, zr3.at[1])
    up_conv(3, d3, r2, 2, 1)
    send(E_R2, (0, 1))
    pack(r2, 2, zs2.at[2])
    send(E_R2, (2, 3))
    lax.fori_loop(X * H // 2, X * H, image_turn, 0, unroll=4)
    image_copy = pltpu.make_async_copy(image_out, image_hbm, io_sem.at[3])
    image_copy.start()
    lin0(6, 7)
    receive(E_D0, (0, 1))
    lin0(0, 1)
    receive(E_R2)
    unpack(r2, 2, zr2.at[2])
    up_conv(4, r2, r1, 1, 1, 2)
    send(E_R1, (0, 1))
    pack(r1, 1, zs1.at[2])
    send(E_R1, (2, 3))
    lin0(X - 1, X)
    over = lax.fori_loop(0, X * (Z // RI), pre_body, jnp.zeros((8, L), F32), unroll=2)
    receive(E_R1, (2, 3))
    unpack(r1, 1, zr1.at[2])
    over = over + sc[2:3] * up_conv(5, r1, z0, 0, H, U_UP, gl, span(1, Xl[1] - 1))
    receive(E_R1, (0, 1))
    over = over + sc[2:3] * up_conv(5, r1, z0, 0, H, U_UP, gl, ends(Xl[1]))
    a_send[1] = over
    copies = reduce_start(n_a, a_send.at[1], a_recv.at[1], asend_sem.at[1], arecv_sem.at[1], peer_a)
    pending += copies
    def last_w(o, k):
        return w_last[k, o]

    for side, plane, o in ((0, 1, 2), (1, X, 1)):
        def part_body(i, carry, side=side, plane=plane, o=o):
            base = pl.multiple_of(i * 32, 8)
            for h in range(H):
                total = None
                for k in range(CH):
                    term = last_w(o, k) * z0[k, h, pl.ds(plane * Zp[0] + PAD + base, 32), :]
                    total = term if total is None else total + term
                xs_m[side, h, pl.ds(base, 32), :] = total
            return carry
        lax.fori_loop(0, Z // 32, part_body, 0)
    for side, at, o in ((0, 0, 6), (1, Z - 1, 5)):
        for h in range(H):
            total = None
            for k in range(CH):
                term = last_w(o, k) * z0[k, h, pl.ds(Zp[0] + PAD + at, X, stride=Zp[0]), :]
                total = term if total is None else total + term
            zs_m[side, pl.ds(h * X, X), :] = total
    send(E_NET)

    def put_net(c, h, base, rows, value):
        net[h, pl.ds(base, rows), :] = value

    conv(loader(z0), put_net, lambda o, c, k: last_w(o, k), None,
          CH, 1, H, 0, 2 * L, 32, span(0, X), unroll=U_LAST, relu=False)
    b_send[1] = reduce_end(copies, a_send.at[1], a_recv.at[1])
    copies = reduce_start(n_chip, b_send.at[1], b_recv.at[1], bsend_sem.at[1], brecv_sem.at[1], peer_b)
    pending += copies
    receive(E_NET)
    for side, plane in ((0, 1), (1, X)):
        for h in range(H):
            at = (h, pl.ds(plane * Zp[0] + PAD, Z), slice(None))
            net[at] = net[at] + xr_m[side, h]
    for side, row in ((0, 0), (1, Z - 1)):
        for h in range(H):
            at = (h, pl.ds(Zp[0] + PAD + row, X, stride=Zp[0]), slice(None))
            net[at] = net[at] + zr_m[side, pl.ds(h * X, X), :]

    def turn_pre(i, carry):
        x, h = i // H, lax.rem(i, H)
        at = (h, pl.ds(pl.multiple_of((x + 1) * Zp[0] + PAD, 8), Z), slice(None))
        block = pre[at] + sc[2:3] * net[at]
        pre_out[x, pl.ds(pl.multiple_of(h * L, L), L), :] = block.T
        return carry

    lax.fori_loop(0, X * H, turn_pre, 0, unroll=4)
    pre_copy = pltpu.make_async_copy(pre_out, pre_hbm, io_sem.at[4])
    pre_copy.start()
    total = reduce_end(copies, b_send.at[1], b_recv.at[1])
    total = jnp.sum(jnp.sum(total, axis=0, keepdims=True), axis=1, keepdims=True)
    beta_out[...] = jnp.broadcast_to(total, (1, L)) / sc[3:4]

    image_copy.wait()
    pre_copy.wait()
    for copy in pending:
        copy.wait_send()
    for e in range(N_EX):
        sent(e)


def on_device(residual, direction, diagonal, first_weight, conv_weights, last_weight, biases):
    X, Y, Z = residual.shape
    n_slab, n_col = lax.axis_size("slab"), lax.axis_size("col")
    H = Y // L
    Zl = [Z // 2**l for l in range(4)]
    Xl = [X // 2**l for l in range(4)]
    rows = [(Xl[l] + 2) * (Zl[l] + 2 * PAD) for l in range(4)]
    field = pltpu.VMEM((X, Y, Z), F32)
    one = pltpu.VMEM((H, rows[0], L), F32)
    four = pltpu.VMEM((CH, H, rows[0], L), F32)

    def level(l):
        return pltpu.VMEM((CH, rows[l], L), F32)

    def edge(*lead):
        return pltpu.VMEM((*lead, L), F32)

    def edge_rows(l):
        return max(8, CH * Xl[l])

    n_a, n_b = 2 * n_col, n_slab // 2
    scratch = [
        field, field, field, field, field, four, one, one, one, one, four, four, one, one,
        level(1), level(1), level(1), level(2), level(2), level(2), level(3), level(3),
        edge(3, 2, H * X), edge(3, 2, H * X), edge(2, CH * H * X), edge(2, CH * H * X),
        edge(3, 2, edge_rows(1)), edge(3, 2, edge_rows(1)),
        edge(3, 2, edge_rows(2)), edge(3, 2, edge_rows(2)),
        edge(2, 2, edge_rows(3)), edge(2, 2, edge_rows(3)),
        edge(2, H, Z), edge(2, H, Z), edge(2, H * X), edge(2, H * X),
        pltpu.VMEM((2 * L, L), BF16), edge(8, Z), pltpu.VMEM((2 * L, 2 * L), BF16),
        pltpu.VMEM((3, 2 * L, 2 * L), BF16), edge(8),
        edge(2, 8), edge(2, n_a - 1, 8), edge(2, 8), edge(2, n_b - 1, 8),
        pltpu.SemaphoreType.DMA((5,)),
        pltpu.SemaphoreType.DMA((N_EX, 4)), pltpu.SemaphoreType.DMA((N_EX, 4)),
        pltpu.SemaphoreType.DMA((2, n_a - 1)), pltpu.SemaphoreType.DMA((2, n_a - 1)),
        pltpu.SemaphoreType.DMA((2, n_b - 1)), pltpu.SemaphoreType.DMA((2, n_b - 1)),
    ]
    vmem = pl.BlockSpec(memory_space=pltpu.VMEM)
    anywhere = pl.BlockSpec(memory_space=pl.ANY)
    image, pre, alpha, beta = pl.pallas_call(
        functools.partial(kernel, n_slab, n_col, X, Z),
        out_shape=(jax.ShapeDtypeStruct((X, Y, Z), F32),) * 2 + (jax.ShapeDtypeStruct((1, L), F32),) * 2,
        in_specs=[pl.BlockSpec(memory_space=pltpu.SMEM)] * 4 + [anywhere] * 3,
        out_specs=(anywhere, anywhere, vmem, vmem),
        scratch_shapes=scratch,
        compiler_params=pltpu.CompilerParams(
            collective_id=0, has_side_effects=True, vmem_limit_bytes=56 * 2**20),
    )(first_weight.T, conv_weights.transpose(0, 2, 3, 1), last_weight.T, biases.T,
      residual, direction, diagonal)
    return residual - alpha[:, :Z] * image, pre - beta[:, :Z] * direction


def solution(mesh):
    in_specs = (P("slab", None, "col"),) * 3 + (P(),) * 4
    return jax.shard_map(
        on_device, mesh=mesh, in_specs=in_specs,
        out_specs=(P("slab", None, "col"),) * 2, check_vma=False,
    )
```
